32 devices in a mesh: dp: 8 (over z, core), tensor: 4 (over y, x).
Axes of the slice: x: 2, y: 2, z: 4, core: 2. Of those that a mesh axis runs over, the one named last changes fastest.
Arguments:
- tokens: bfloat16 [8192, 2048], P('dp', 'tensor'), may hold values from -6 to 6
- norm_gain_attn: float32 [2048], replicated, may hold values from 0.25 to 1.75
- norm_gain_mlp: float32 [2048], replicated, may hold values from 0.25 to 1.75
- w_query: bfloat16 [2048, 2048], P(None, 'tensor'), may hold values from -0.125 to 0.125
- w_key: bfloat16 [2048, 2048], P(None, 'tensor'), may hold values from -0.125 to 0.125
- w_value: bfloat16 [2048, 2048], P(None, 'tensor'), may hold values from -0.125 to 0.125
- w_out: bfloat16 [2048, 2048], P('tensor'), may hold values from -0.375 to 0.375
- w_gate: bfloat16 [2048, 8192], P(None, 'tensor'), may hold values from -0.125 to 0.125
- w_up: bfloat16 [2048, 8192], P(None, 'tensor'), may hold values from -0.125 to 0.125
- w_down: bfloat16 [8192, 2048], P('tensor'), may hold values from -0.0625 to 0.0625
- cotangent: bfloat16 [8192, 2048], P('dp', 'tensor'), may hold values from -6 to 6
- lengths: int32 [8, 8], P('dp'), may hold values from 0 to 1024, as said below
Outputs:
- out_tokens: bfloat16 [8192, 2048], P('dp', 'tensor')
- grad_tokens: bfloat16 [8192, 2048], P('dp', 'tensor')
- grad_gain_attn: float32 [2048], P('tensor')
- grad_gain_mlp: float32 [2048], P('tensor')
- grad_w_query: float32 [2048, 2048], P(None, 'tensor')
- grad_w_key: float32 [2048, 2048], P(None, 'tensor')
- grad_w_value: float32 [2048, 2048], P(None, 'tensor')
- grad_w_out: float32 [2048, 2048], P('tensor')
- grad_w_gate: float32 [2048, 8192], P(None, 'tensor')
- grad_w_up: float32 [2048, 8192], P(None, 'tensor')
- grad_w_down: float32 [8192, 2048], P('tensor')
The draws below stay inside these ranges and needn't reach their ends.
Inputs may be any that keep to these rules, and one draw needn't show every extreme that they name: `lengths`: row g lists the sequences packed from slot 0 of data group g in order; zeros may stand among them; each row sums to 512 or more and to 1024 at most, and the slots after that sum are not live; in every draw one data group holds a single sequence of 1024 tokens.
All inputs are finite; a program needn't handle non-finite values.
Results may differ from the reference program's by a relative error of at most 0.015.
Values may be sent and summed in bfloat16 or wider, within the bound.
A program may use at most 320 MiB of HBM per device.

```python
import math
import jax
import jax.numpy as jnp
from jax import lax

D = 2048
HEADS = 32
HDIM = 64
FF = 8192
TOK_DEV = 1024
NSEQ = 8
TOKENS = 8192
N_DP = 8


def draw_lengths(key, part):
    key = jax.random.fold_in(key, 7)
    load_key, full_key, slot_key, cut_key = jax.random.split(key, 4)
    loads = jax.random.randint(load_key, (N_DP,), TOK_DEV // 2, TOK_DEV + 1)
    full_group = jax.random.randint(full_key, (), 0, N_DP)
    lone_slot = jax.random.randint(slot_key, (), 0, NSEQ)
    group_index = jnp.arange(N_DP)
    cut_points = jax.random.randint(cut_key, (N_DP, NSEQ - 1), 0, TOK_DEV + 1)
    cut_points = jnp.sort(jnp.minimum(cut_points, loads[:, None]), axis=1)
    edges = jnp.concatenate([jnp.zeros((N_DP, 1), jnp.int32), cut_points.astype(jnp.int32), loads[:, None].astype(jnp.int32)], axis=1)
    pieces = edges[:, 1:] - edges[:, :-1]
    lone_row = jnp.where(jnp.arange(NSEQ) == lone_slot, TOK_DEV, 0)
    return jnp.where((group_index == full_group)[:, None], lone_row[None, :], pieces).astype(jnp.int32)


def block_levels(rng, extent, cuts, smallest, top_value):
    def one(axis_at, shards_of):
        heights = jax.random.uniform(jax.random.fold_in(jax.random.fold_in(rng, 6), axis_at), (shards_of,), jnp.float32, smallest / len(cuts), top_value / len(cuts))
        return jnp.repeat(jnp.exp(heights), extent[axis_at] // shards_of).reshape((-1,) + (1,) * (len(extent) - axis_at - 1))

    loudness = one(*cuts[0])
    for cut in cuts[1:]:
        loudness = loudness * one(*cut)
    return loudness


def noise(rng, extent, width, reach, cuts=(), held_as=jnp.bfloat16):
    values = width * jax.random.normal(rng, extent, jnp.float32)
    if cuts:
        values = values * block_levels(rng, extent, cuts, -0.22, 0.18)
    return jnp.clip(values, -reach, reach).astype(held_as)


def setup_inputs(seed: int = 0) -> dict:
    key_of = jax.random.split(jax.random.key(seed), 13)
    tokens = noise(key_of[0], (TOKENS, D), 1.0, 6.0, ((0, 8), (1, 4)))
    norm_gain_attn = jnp.clip(1.0 + 0.15 * jax.random.normal(key_of[1], (D,), jnp.float32), 0.25, 1.75)
    norm_gain_mlp = jnp.clip(1.0 + 0.15 * jax.random.normal(key_of[2], (D,), jnp.float32), 0.25, 1.75)
    w_query = noise(key_of[3], (D, HEADS * HDIM), D ** -0.5, 0.125, ((1, 4),))
    w_key = noise(key_of[4], (D, HEADS * HDIM), D ** -0.5, 0.125, ((1, 4),))
    w_value = noise(key_of[5], (D, HEADS * HDIM), D ** -0.5, 0.125, ((1, 4),))
    w_out = noise(key_of[6], (HEADS * HDIM, D), (HEADS * HDIM // 8) ** -0.5, 0.375, ((0, 4),))
    w_gate = noise(key_of[7], (D, FF), D ** -0.5, 0.125, ((1, 4),))
    w_up = noise(key_of[8], (D, FF), D ** -0.5, 0.125, ((1, 4),))
    w_down = noise(key_of[9], (FF, D), FF ** -0.5, 0.0625, ((0, 4),))
    cotangent = noise(key_of[10], (TOKENS, D), 1.0, 6.0, ((0, 8), (1, 4)))
    lengths = draw_lengths(jax.random.fold_in(key_of[12], 71), 0)
    return dict(tokens=tokens, norm_gain_attn=norm_gain_attn, norm_gain_mlp=norm_gain_mlp, w_query=w_query, w_key=w_key, w_value=w_value, w_out=w_out, w_gate=w_gate, w_up=w_up, w_down=w_down, cotangent=cotangent, lengths=lengths)


EPSILON = 1e-05
ROPE_BASE = 130000.0
HIGH = lax.Precision.HIGHEST

@jax.custom_vjp
def low(v):
    return lax.optimization_barrier(v.astype(jnp.bfloat16)).astype(jnp.float32)

@jax.custom_vjp
def low_back(v):
    return v

def low_keep(v):
    return (low(v), None)

def low_pass(kept, grad):
    return (grad,)

def back_keep(v):
    return (v, None)

def back_low(kept, grad):
    return (low(grad),)
low.defvjp(low_keep, low_pass)
low_back.defvjp(back_keep, back_low)

def matmul(left, right):
    return jnp.dot(left, right, precision=HIGH, preferred_element_type=jnp.float32)

def positions(length_row, slot_count):
    slot_index = jnp.arange(slot_count, dtype=jnp.int32)
    seq_ends = jnp.cumsum(length_row).astype(jnp.int32)
    passed = seq_ends[None, :] <= slot_index[:, None]
    seq_number = lax.optimization_barrier(jnp.sum(passed.astype(jnp.int32), axis=1)).astype(jnp.int32)
    seq_start = lax.optimization_barrier(jnp.sum(jnp.where(passed, length_row[None, :], 0), axis=1)).astype(jnp.int32)
    is_live = slot_index < seq_ends[-1]
    sequence = jnp.where(is_live, seq_number, slot_count + slot_index).astype(jnp.int32)
    position = jnp.where(is_live, slot_index - seq_start, 0).astype(jnp.int32)
    return (sequence, position)

def rotate_tables(position, head_size):
    half_width = head_size // 2
    freq_index = jnp.arange(half_width).astype(jnp.float32)
    inverse = jnp.exp(freq_index * (-2.0 * math.log(ROPE_BASE) / head_size))
    angles = position.astype(jnp.float32)[:, None] * inverse[None, :]
    return (jnp.cos(angles)[:, None, :], jnp.sin(angles)[:, None, :])

def rotate(values, cosine, sine_part):
    half_width = values.shape[-1] // 2
    first_half = values[..., :half_width]
    second = values[..., half_width:]
    return jnp.concatenate([first_half * cosine - second * sine_part, second * cosine + first_half * sine_part], axis=-1)

def rms_norm(values, gain):
    return values * lax.rsqrt(lax.optimization_barrier(jnp.mean(values * values, axis=-1, keepdims=True)) + EPSILON) * gain

def layer(params, tokens, sequence, position):
    gain_attn, gain_mlp, w_query, w_key, w_value, w_out, w_gate, w_up, w_down = params
    slot_count = tokens.shape[0]
    normed = low(rms_norm(tokens, gain_attn))
    cosine, sine_part = rotate_tables(position, HDIM)
    query_rows = low(rotate(low_back(matmul(normed, w_query)).reshape(slot_count, HEADS, HDIM), cosine, sine_part))
    key_rows = low(rotate(low_back(matmul(normed, w_key)).reshape(slot_count, HEADS, HDIM), cosine, sine_part))
    value_rows = low(low_back(matmul(normed, w_value))).reshape(slot_count, HEADS, HDIM)
    slot_index = jnp.arange(slot_count, dtype=jnp.int32)
    allowed = (sequence[:, None] == sequence[None, :]) & (slot_index[None, :] <= slot_index[:, None])
    scores = jnp.einsum('qhd,khd->hqk', query_rows, key_rows, precision=HIGH) * HDIM ** (-0.5)
    scores = low_back(scores)
    scores = jnp.where(allowed[None], scores, -1e+30)
    weights = low(jax.nn.softmax(scores, axis=-1))
    mixed_heads = jnp.einsum('hqk,khd->qhd', weights, value_rows, precision=HIGH).reshape(slot_count, HEADS * HDIM)
    mixed_heads = low(low_back(mixed_heads))
    residual = tokens + low_back(matmul(mixed_heads, w_out))
    normed_mlp = low(rms_norm(residual, gain_mlp))
    gate_proj = low_back(matmul(normed_mlp, w_gate))
    upward = low_back(matmul(normed_mlp, w_up))
    hidden = low(jax.nn.silu(gate_proj) * upward)
    return residual + low_back(matmul(hidden, w_down))

def reference(tokens, norm_gain_attn, norm_gain_mlp, w_query, w_key, w_value, w_out, w_gate, w_up, w_down, cotangent, lengths):
    params = tuple((weight_array.astype(jnp.float32) for weight_array in (norm_gain_attn, norm_gain_mlp, w_query, w_key, w_value, w_out, w_gate, w_up, w_down)))
    inputs = tokens.astype(jnp.float32).reshape(N_DP, TOK_DEV, D)
    cot_groups = cotangent.astype(jnp.float32).reshape(N_DP, TOK_DEV, D)
    sequence, position = jax.vmap(lambda length_row: positions(length_row, TOK_DEV))(lengths)
    checked = jax.checkpoint(layer)

    def forward(params, inputs):

        def one_group(state_carry, group_item):
            group_tokens, group_seq, group_pos = group_item
            return (state_carry, checked(params, group_tokens, group_seq, group_pos))
        _, result = lax.scan(one_group, jnp.zeros((), jnp.float32), (inputs, sequence, position))
        return result
    outputs, pullback = jax.vjp(forward, params, inputs)
    grad_params, grad_inputs = pullback(cot_groups)
    return (outputs.reshape(TOKENS, D).astype(jnp.bfloat16), grad_inputs.reshape(TOKENS, D).astype(jnp.bfloat16), grad_params[0], grad_params[1], grad_params[2], grad_params[3], grad_params[4], grad_params[5], grad_params[6], grad_params[7], grad_params[8])
```

```python
import functools
import math

import jax
import jax.numpy as jnp
from jax import lax
from jax.experimental import pallas as pl
from jax.experimental.pallas import tpu as pltpu
from jax.sharding import PartitionSpec as P

HDIM = 64


EPSILON = 1e-05
ROPE_BASE = 130000.0


def matmul_first(left, right):
    return lax.dot_general(
        left, right, (((0,), (0,)), ((), ())), preferred_element_type=jnp.float32
    )


def matmul_last(left, right):
    return lax.dot_general(
        left, right, (((1,), (1,)), ((), ())), preferred_element_type=jnp.float32
    )


def positions(length_row, slot_count):
    slot_index = jnp.arange(slot_count, dtype=jnp.int32)
    seq_ends = jnp.cumsum(length_row)
    passed = seq_ends[None, :] <= slot_index[:, None]
    seq_number = jnp.sum(passed.astype(jnp.int32), axis=1)
    seq_start = jnp.sum(jnp.where(passed, length_row[None, :], 0), axis=1)
    is_live = slot_index < seq_ends[-1]
    sequence = jnp.where(is_live, seq_number, slot_count + slot_index)
    position = jnp.where(is_live, slot_index - seq_start, 0)
    return (sequence, position)


def rotate_tables(position, head_size):
    half_width = head_size // 2
    freq_index = jnp.arange(half_width).astype(jnp.float32)
    inverse = jnp.exp(freq_index * (-2.0 * math.log(ROPE_BASE) / head_size))
    angles = position.astype(jnp.float32)[:, None] * inverse[None, :]
    return (jnp.cos(angles)[:, None, :], jnp.sin(angles)[:, None, :])


def rotate(values, cosine, sine_part):
    half_width = values.shape[-1] // 2
    first_half = values[..., :half_width]
    second = values[..., half_width:]
    return jnp.concatenate(
        [first_half * cosine - second * sine_part, second * cosine + first_half * sine_part],
        axis=-1,
    )


def rotate_back(values, cosine, sine_part):
    half_width = values.shape[-1] // 2
    first_half = values[..., :half_width]
    second = values[..., half_width:]
    return jnp.concatenate(
        [first_half * cosine + second * sine_part, second * cosine - first_half * sine_part],
        axis=-1,
    )


def piece_mask(sequence, first_row, last_row):
    query_slots = jnp.arange(first_row, last_row)
    key_slots = jnp.arange(last_row)
    same_seq = sequence[first_row:last_row, None] == sequence[None, :last_row]
    return same_seq & (key_slots[None, :] <= query_slots[:, None])


def piece_scores(query_rows, key_rows, sequence, first_row, last_row, score_scale):
    scores = (
        jnp.einsum(
            "qhd,khd->hqk",
            query_rows[first_row:last_row],
            key_rows[:last_row],
            preferred_element_type=jnp.float32,
        )
        * score_scale
    )
    allowed = piece_mask(sequence, first_row, last_row)
    return jnp.where(allowed[None], scores, -1e30)


def attend_forward(query_rows, key_rows, value_rows, sequence, piece_rows, score_scale):
    slot_count = query_rows.shape[0]
    outputs = []
    log_totals = []
    for piece_index in range(slot_count // piece_rows):
        first_row = piece_index * piece_rows
        last_row = first_row + piece_rows
        scores = piece_scores(query_rows, key_rows, sequence, first_row, last_row, score_scale)
        peak = jnp.max(scores, axis=-1, keepdims=True)
        expon = jnp.exp(scores - peak)
        row_total = jnp.sum(expon, axis=-1, keepdims=True)
        weights = (expon / row_total).astype(jnp.bfloat16)
        outputs.append(
            jnp.einsum(
                "hqk,khd->qhd", weights, value_rows[:last_row], preferred_element_type=jnp.float32
            ).astype(jnp.bfloat16)
        )
        log_totals.append(peak + jnp.log(row_total))
    return (jnp.concatenate(outputs, axis=0), log_totals)


def attend_backward(
    query_rows, key_rows, value_rows, grad_mixed, sequence, log_totals, piece_rows, score_scale
):
    slot_count = query_rows.shape[0]
    grad_query_parts = []
    grad_keys = jnp.zeros(key_rows.shape, jnp.float32)
    grad_values = jnp.zeros(value_rows.shape, jnp.float32)
    for piece_index in range(slot_count // piece_rows):
        first_row = piece_index * piece_rows
        last_row = first_row + piece_rows
        scores = piece_scores(query_rows, key_rows, sequence, first_row, last_row, score_scale)
        probs = jnp.exp(scores - log_totals[piece_index])
        grad_piece = grad_mixed[first_row:last_row]
        grad_probs = jnp.einsum(
            "qhd,khd->hqk", grad_piece, value_rows[:last_row], preferred_element_type=jnp.float32
        )
        delta = jnp.sum(probs * grad_probs, axis=-1, keepdims=True)
        grad_scores = (probs * (grad_probs - delta)).astype(jnp.bfloat16)
        grad_query_parts.append(
            jnp.einsum(
                "hqk,khd->qhd", grad_scores, key_rows[:last_row], preferred_element_type=jnp.float32
            )
            * score_scale
        )
        grad_keys = grad_keys.at[:last_row].add(
            jnp.einsum(
                "hqk,qhd->khd",
                grad_scores,
                query_rows[first_row:last_row],
                preferred_element_type=jnp.float32,
            )
            * score_scale
        )
        grad_values = grad_values.at[:last_row].add(
            jnp.einsum(
                "hqk,qhd->khd",
                probs.astype(jnp.bfloat16),
                grad_piece,
                preferred_element_type=jnp.float32,
            )
        )
    return (jnp.concatenate(grad_query_parts, axis=0), grad_keys, grad_values)


MESH = pl.DeviceIdType.MESH
SLOTS = 8
HOP_LAG = 2


class LineSum:
    def __init__(self, total, outs, tile, scratch):
        self.paired = lax.axis_size("dp") == 16
        assert lax.axis_size("dp") in (8, 16)
        self.lag_p = 1
        self.lag_a = 1 + HOP_LAG * self.paired
        self.lag_b = self.lag_a + HOP_LAG
        self.lag_c = self.lag_b + HOP_LAG
        self.lag_f = self.lag_c + HOP_LAG
        self.lag_o = self.lag_f + 1
        self.lag_d = self.lag_o + 1
        self.total = total
        self.outs = outs
        self.tile_rows, self.tile_cols = tile
        self.half = self.tile_rows // 2
        (
            self.stage, self.r_e, self.s_one, self.r_a, self.s_two, self.r_b, self.tot, self.r_f,
            self.s_zero, self.r_p, self.sems, self.out_sems,
        ) = scratch
        dp = lax.axis_index("dp")
        self.tensor = lax.axis_index("tensor")
        self.core = lax.rem(dp, 2)
        z = lax.rem(dp // 2, 4)
        self.is_end = (z == 0) | (z == 3)
        self.is_mid = jnp.logical_not(self.is_end)
        self.sibling = dp + 1 - 2 * self.core
        step = jnp.where((z == 0) | (z == 2), 2, -2)
        self.near = dp + step
        self.across = dp + 6 - 4 * z
        self.twin = lax.rem(dp + 8, lax.axis_size("dp"))

    @staticmethod
    def scratch_shapes(tile):
        rows, cols = tile
        half = pltpu.VMEM((SLOTS, rows // 2, cols), jnp.bfloat16)
        spare = half if lax.axis_size("dp") == 16 else pltpu.VMEM((8, 128), jnp.bfloat16)
        return [pltpu.VMEM((SLOTS, 2, rows // 2, cols), jnp.bfloat16)] + [half] * 7 + [
            spare,
            spare,
            pltpu.SemaphoreType.DMA((12, SLOTS)),
            pltpu.SemaphoreType.DMA((2, SLOTS)),
        ]

    def neighbours(self):
        return (self.sibling, self.near, self.across) + ((self.twin,) if self.paired else ())

    def copy(self, hop, slot, src, dst, target):
        return pltpu.make_async_remote_copy(
            src_ref=src, dst_ref=dst, send_sem=self.sems.at[2 * hop, slot],
            recv_sem=self.sems.at[2 * hop + 1, slot],
            device_id=(target, self.tensor), device_id_type=MESH,
        )

    def hop_e(self, slot):
        return self.copy(0, slot, self.stage.at[slot, 1 - self.core], self.r_e.at[slot], self.sibling)

    def hop_a(self, slot):
        return self.copy(1, slot, self.s_one.at[slot], self.r_a.at[slot], self.near)

    def hop_b(self, slot):
        return self.copy(2, slot, self.s_two.at[slot], self.r_b.at[slot], self.across)

    def hop_c(self, slot):
        return self.copy(3, slot, self.tot.at[slot], self.tot.at[slot], self.near)

    def hop_f(self, slot):
        return self.copy(4, slot, self.tot.at[slot], self.r_f.at[slot], self.sibling)

    def hop_p(self, slot):
        return self.copy(5, slot, self.s_zero.at[slot], self.r_p.at[slot], self.twin)

    def out_copies(self, slot, ref, tile_row, tile_col):
        cols = pl.ds(pl.multiple_of(tile_col * self.tile_cols, self.tile_cols), self.tile_cols)
        first = tile_row * self.tile_rows
        mine = pl.ds(pl.multiple_of(first + self.core * self.half, self.half), self.half)
        other = pl.ds(pl.multiple_of(first + (1 - self.core) * self.half, self.half), self.half)
        return (
            pltpu.make_async_copy(self.tot.at[slot], ref.at[mine, cols], self.out_sems.at[0, slot]),
            pltpu.make_async_copy(self.r_f.at[slot], ref.at[other, cols], self.out_sems.at[1, slot]),
        )

    def on_out(self, chunk, slot, act):
        for ref, first, count, tiles_across in self.outs:
            local = chunk - first

            @pl.when((local >= 0) & (local < count))
            def _(ref=ref, local=local, tiles_across=tiles_across):
                for one in self.out_copies(
                    slot, ref, local // tiles_across, lax.rem(local, tiles_across)
                ):
                    act(one)

    def at(self, chunk, work):
        @pl.when((chunk >= 0) & (chunk < self.total))
        def _():
            work(lax.rem(chunk, SLOTS))

    def put(self, chunk, value):
        self.stage[lax.rem(chunk, SLOTS)] = value.astype(jnp.bfloat16).reshape(
            2, self.half, self.tile_cols
        )

    def tick(self, k):
        def drop(slot):
            self.on_out(k - self.lag_d, slot, lambda one: one.wait())

        def out(slot):
            self.hop_f(slot).wait()
            self.on_out(k - self.lag_o, slot, lambda one: one.start())

        def final(slot):
            @pl.when(self.is_end)
            def _():
                self.hop_c(slot).wait_recv()

            @pl.when(self.is_mid)
            def _():
                self.hop_c(slot).wait_send()

            self.hop_f(slot).start()

        def back(slot):
            @pl.when(self.is_mid)
            def _():
                self.hop_b(slot).wait()
                self.tot[slot] = (
                    self.s_two[slot].astype(jnp.float32) + self.r_b[slot].astype(jnp.float32)
                ).astype(jnp.bfloat16)
                self.hop_c(slot).start()

        def across(slot):
            @pl.when(self.is_mid)
            def _():
                self.hop_a(slot).wait_recv()
                self.s_two[slot] = (
                    self.s_one[slot].astype(jnp.float32) + self.r_a[slot].astype(jnp.float32)
                ).astype(jnp.bfloat16)
                self.hop_b(slot).start()

            @pl.when(self.is_end)
            def _():
                self.hop_a(slot).wait_send()

        def inward(slot):
            if self.paired:
                self.hop_p(slot).wait()
                self.s_one[slot] = (
                    self.s_zero[slot].astype(jnp.float32) + self.r_p[slot].astype(jnp.float32)
                ).astype(jnp.bfloat16)
            else:
                self.hop_e(slot).wait()
                self.s_one[slot] = (
                    self.stage[slot, self.core].astype(jnp.float32)
                    + self.r_e[slot].astype(jnp.float32)
                ).astype(jnp.bfloat16)

            @pl.when(self.is_end)
            def _():
                self.hop_a(slot).start()

        def pair(slot):
            self.hop_e(slot).wait()
            self.s_zero[slot] = (
                self.stage[slot, self.core].astype(jnp.float32)
                + self.r_e[slot].astype(jnp.float32)
            ).astype(jnp.bfloat16)
            self.hop_p(slot).start()

        self.at(k - self.lag_d, drop)
        self.at(k - self.lag_o, out)
        self.at(k - self.lag_f, final)
        self.at(k - self.lag_c, back)
        self.at(k - self.lag_b, across)
        self.at(k - self.lag_a, inward)
        if self.paired:
            self.at(k - self.lag_p, pair)
        self.at(k, lambda slot: self.hop_e(slot).start())


def dot_tokens(left, right):
    return lax.dot_general(
        left, right, (((0,), (0,)), ((), ())), preferred_element_type=jnp.float32
    )


def weight_grads_kernel(tile, shapes, *refs):
    count = len(shapes)
    lefts, rights = refs[:count], refs[count : 2 * count]
    outs = refs[2 * count : 3 * count]
    left_buf, right_buf, load_sems = refs[3 * count : 3 * count + 3]
    scratch = refs[3 * count + 3 :]
    tile_rows, tile_cols = tile
    plan = []
    first = 0
    for (rows, cols), ref in zip(shapes, outs):
        tiles = (rows // tile_rows) * (cols // tile_cols)
        plan.append((ref, first, tiles, cols // tile_cols))
        first += tiles
    line = LineSum(first, plan, tile, scratch)
    barrier = pltpu.get_barrier_semaphore()
    for other in line.neighbours():
        pl.semaphore_signal(
            barrier, inc=1, device_id=(other, line.tensor), device_id_type=MESH
        )

    def loads(m):
        rows, cols = shapes[m]
        return (
            pltpu.make_async_copy(
                lefts[m], left_buf.at[m % 2, :, pl.ds(0, rows)], load_sems.at[0, m % 2]
            ),
            pltpu.make_async_copy(
                rights[m], right_buf.at[m % 2, :, pl.ds(0, cols)], load_sems.at[1, m % 2]
            ),
        )

    for one in loads(0):
        one.start()
    pl.semaphore_wait(barrier, len(line.neighbours()))
    for m in range(count):
        for one in loads(m):
            one.wait()
        if m + 1 < count:
            for one in loads(m + 1):
                one.start()
        _, base, tiles, tiles_across = plan[m]

        @pl.loop(0, tiles)
        def _(i, m=m, base=base, tiles_across=tiles_across):
            rows = pl.ds(pl.multiple_of((i // tiles_across) * tile_rows, tile_rows), tile_rows)
            cols = pl.ds(
                pl.multiple_of(lax.rem(i, tiles_across) * tile_cols, tile_cols), tile_cols
            )
            line.put(base + i, dot_tokens(left_buf[m % 2, :, rows], right_buf[m % 2, :, cols]))
            line.tick(base + i)

    @pl.loop(first, first + line.lag_d)
    def _(k):
        line.tick(k)


def weight_grads(pairs):
    shapes = [(left.shape[1], right.shape[1]) for left, right in pairs]
    slots = pairs[0][0].shape[0]
    tile = (min(512, min(s[0] for s in shapes)), min(512, min(s[1] for s in shapes)))
    widest = (max(s[0] for s in shapes), max(s[1] for s in shapes))
    flops = sum(2 * slots * r * c for r, c in shapes)
    return pl.pallas_call(
        functools.partial(weight_grads_kernel, tile, shapes),
        out_shape=[jax.ShapeDtypeStruct(s, jnp.bfloat16) for s in shapes],
        in_specs=[pl.BlockSpec(memory_space=pl.ANY)] * (2 * len(pairs)),
        out_specs=[pl.BlockSpec(memory_space=pl.ANY)] * len(pairs),
        scratch_shapes=[
            pltpu.VMEM((2, slots, widest[0]), jnp.bfloat16),
            pltpu.VMEM((2, slots, widest[1]), jnp.bfloat16),
            pltpu.SemaphoreType.DMA((2, 2)),
        ]
        + LineSum.scratch_shapes(tile),
        compiler_params=pltpu.CompilerParams(
            collective_id=0, has_side_effects=True, vmem_limit_bytes=56 * 1024 * 1024
        ),
        cost_estimate=pl.CostEstimate(flops=flops, bytes_accessed=100_000_000, transcendentals=0),
    )(*[left for left, _ in pairs], *[right for _, right in pairs])


def body(
    tokens,
    norm_gain_attn,
    norm_gain_mlp,
    w_query,
    w_key,
    w_value,
    w_out,
    w_gate,
    w_up,
    w_down,
    cotangent,
    lengths,
):
    slot_count = tokens.shape[0]
    share_width = tokens.shape[1]
    model_width = share_width * lax.axis_size("tensor")
    heads_here = w_query.shape[1] // HDIM
    piece_rows = min(512, slot_count)
    score_scale = HDIM ** (-0.5)
    col_start = lax.axis_index("tensor") * share_width
    gain_attn_here = lax.dynamic_slice_in_dim(norm_gain_attn, col_start, share_width)
    gain_mlp_here = lax.dynamic_slice_in_dim(norm_gain_mlp, col_start, share_width)
    sequence, position = positions(lengths[0], slot_count)
    cosine, sine_part = rotate_tables(position, HDIM)
    full_input = lax.all_gather(tokens, "tensor", axis=1, tiled=True).astype(jnp.float32)
    rms_attn = lax.rsqrt(jnp.mean(full_input * full_input, axis=-1, keepdims=True) + EPSILON)
    normed = (full_input * rms_attn * norm_gain_attn).astype(jnp.bfloat16)
    query_lin = jnp.dot(normed, w_query, preferred_element_type=jnp.float32)
    key_lin = jnp.dot(normed, w_key, preferred_element_type=jnp.float32)
    value_lin = jnp.dot(normed, w_value, preferred_element_type=jnp.float32)
    query_rows = rotate(query_lin.reshape(slot_count, heads_here, HDIM), cosine, sine_part).astype(
        jnp.bfloat16
    )
    key_rows = rotate(key_lin.reshape(slot_count, heads_here, HDIM), cosine, sine_part).astype(
        jnp.bfloat16
    )
    value_rows = value_lin.astype(jnp.bfloat16).reshape(slot_count, heads_here, HDIM)
    mixed_heads, log_totals = attend_forward(
        query_rows, key_rows, value_rows, sequence, piece_rows, score_scale
    )
    mixed_flat = mixed_heads.reshape(slot_count, heads_here * HDIM)
    attn_part = jnp.dot(mixed_flat, w_out, preferred_element_type=jnp.float32)
    input_here = tokens.astype(jnp.float32)
    attn_here = lax.psum_scatter(attn_part, "tensor", scatter_dimension=1, tiled=True)
    resid_here = input_here + attn_here
    square_sum = lax.psum(jnp.sum(resid_here * resid_here, axis=1), "tensor")
    rms_mlp = lax.rsqrt(square_sum[:, None] / model_width + EPSILON)
    normed_here = (resid_here * rms_mlp * gain_mlp_here).astype(jnp.bfloat16)
    normed_mlp = lax.all_gather(normed_here, "tensor", axis=1, tiled=True)
    gate_proj = jnp.dot(normed_mlp, w_gate, preferred_element_type=jnp.float32)
    upward = jnp.dot(normed_mlp, w_up, preferred_element_type=jnp.float32)
    sigmoid_gate = jax.nn.sigmoid(gate_proj)
    silu_gate = gate_proj * sigmoid_gate
    hidden = (silu_gate * upward).astype(jnp.bfloat16)
    mlp_part = jnp.dot(hidden, w_down, preferred_element_type=jnp.float32)
    mlp_here = lax.psum_scatter(
        mlp_part.astype(jnp.bfloat16), "tensor", scatter_dimension=1, tiled=True
    ).astype(jnp.float32)
    out_tokens = (resid_here + mlp_here).astype(jnp.bfloat16)
    cot_rows = lax.all_gather(cotangent, "tensor", axis=1, tiled=True)
    cot_here = cotangent.astype(jnp.float32)
    d_hidden = matmul_last(cot_rows, w_down)
    d_up = (d_hidden * silu_gate).astype(jnp.bfloat16)
    d_gate = (d_hidden * upward * sigmoid_gate * (1.0 + gate_proj * (1.0 - sigmoid_gate))).astype(
        jnp.bfloat16
    )
    d_normed_part = matmul_last(d_gate, w_gate) + matmul_last(d_up, w_up)
    d_normed_here = lax.psum_scatter(d_normed_part, "tensor", scatter_dimension=1, tiled=True)
    grad_gain_mlp = jnp.sum(d_normed_here * resid_here * rms_mlp, axis=0)
    gained_mlp = gain_mlp_here * d_normed_here
    mlp_row_sum = lax.psum(jnp.sum(gained_mlp * resid_here, axis=1), "tensor")
    d_resid = (
        cot_here
        + rms_mlp * gained_mlp
        - resid_here * rms_mlp * rms_mlp * rms_mlp * mlp_row_sum[:, None] / model_width
    )
    branch_rows = lax.all_gather(d_resid.astype(jnp.bfloat16), "tensor", axis=1, tiled=True)
    grad_mixed = (
        matmul_last(branch_rows, w_out).astype(jnp.bfloat16).reshape(slot_count, heads_here, HDIM)
    )
    grad_query, grad_keys, grad_values = attend_backward(
        query_rows, key_rows, value_rows, grad_mixed, sequence, log_totals, piece_rows, score_scale
    )
    grad_query_lin = (
        rotate_back(grad_query, cosine, sine_part)
        .astype(jnp.bfloat16)
        .reshape(slot_count, heads_here * HDIM)
    )
    grad_key_lin = (
        rotate_back(grad_keys, cosine, sine_part)
        .astype(jnp.bfloat16)
        .reshape(slot_count, heads_here * HDIM)
    )
    grad_value_lin = grad_values.astype(jnp.bfloat16).reshape(slot_count, heads_here * HDIM)
    d_normed_attn = (
        matmul_last(grad_query_lin, w_query)
        + matmul_last(grad_key_lin, w_key)
        + matmul_last(grad_value_lin, w_value)
    )
    d_attn_here = lax.psum_scatter(d_normed_attn, "tensor", scatter_dimension=1, tiled=True)
    grad_gain_attn = jnp.sum(d_attn_here * input_here * rms_attn, axis=0)
    gained_attn = gain_attn_here * d_attn_here
    attn_row_sum = lax.psum(jnp.sum(gained_attn * input_here, axis=1), "tensor")
    grad_tokens = (
        d_resid
        + rms_attn * gained_attn
        - input_here * rms_attn * rms_attn * rms_attn * attn_row_sum[:, None] / model_width
    ).astype(jnp.bfloat16)
    grad_gain_attn, grad_gain_mlp = lax.psum((grad_gain_attn, grad_gain_mlp), "dp")
    (
        grad_w_down,
        grad_w_gate,
        grad_w_up,
        grad_w_out,
        grad_w_value,
        grad_w_query,
        grad_w_key,
    ) = [
        total.astype(jnp.float32)
        for total in weight_grads(
            [
                (hidden, cot_rows),
                (normed_mlp, d_gate),
                (normed_mlp, d_up),
                (mixed_flat, branch_rows),
                (normed, grad_value_lin),
                (normed, grad_query_lin),
                (normed, grad_key_lin),
            ]
        )
    ]
    return (
        out_tokens,
        grad_tokens,
        grad_gain_attn,
        grad_gain_mlp,
        grad_w_query,
        grad_w_key,
        grad_w_value,
        grad_w_out,
        grad_w_gate,
        grad_w_up,
        grad_w_down,
    )


def solution(mesh):
    placed = (
        P("dp", "tensor"),
        P(),
        P(),
        P(None, "tensor"),
        P(None, "tensor"),
        P(None, "tensor"),
        P("tensor", None),
        P(None, "tensor"),
        P(None, "tensor"),
        P("tensor", None),
        P("dp", "tensor"),
        P("dp", None),
    )
    return jax.shard_map(
        body,
        mesh=mesh,
        in_specs=placed,
        out_specs=(
            P("dp", "tensor"),
            P("dp", "tensor"),
            P("tensor"),
            P("tensor"),
            P(None, "tensor"),
            P(None, "tensor"),
            P(None, "tensor"),
            P("tensor", None),
            P(None, "tensor"),
            P(None, "tensor"),
            P("tensor", None),
        ),
        check_vma=False,
    )
```

```python
import functools
import math

import jax
import jax.numpy as jnp
from jax import lax
from jax.experimental import pallas as pl
from jax.experimental.pallas import tpu as pltpu
from jax.sharding import PartitionSpec as P

HDIM = 64
PAIR = 2 * HDIM


EPSILON = 1e-05
ROPE_BASE = 130000.0
SCALE = HDIM ** (-0.5)
MASKED = -1e30
MESH = pl.DeviceIdType.MESH
HOP_LAG = 2
UNIT = 256
MIB = 1024 * 1024


def matmul_first(left, right):
    return lax.dot_general(
        left, right, (((0,), (0,)), ((), ())), preferred_element_type=jnp.float32
    )


def matmul_last(left, right):
    return lax.dot_general(
        left, right, (((1,), (1,)), ((), ())), preferred_element_type=jnp.float32
    )


def matmul(left, right):
    return jnp.dot(left, right, preferred_element_type=jnp.float32)


def span(first, size):
    return pl.ds(pl.multiple_of(first, size), size)


def positions(length_row, slot_count):
    slot_index = jnp.arange(slot_count, dtype=jnp.int32)
    seq_ends = jnp.cumsum(length_row)
    passed = seq_ends[None, :] <= slot_index[:, None]
    seq_number = jnp.sum(passed.astype(jnp.int32), axis=1)
    seq_start = jnp.sum(jnp.where(passed, length_row[None, :], 0), axis=1)
    is_live = slot_index < seq_ends[-1]
    sequence = jnp.where(is_live, seq_number, slot_count + slot_index)
    position = jnp.where(is_live, slot_index - seq_start, 0)
    return (sequence, position)


def rotate_tables(position):
    half_width = HDIM // 2
    freq_index = jnp.arange(half_width).astype(jnp.float32)
    inverse = jnp.exp(freq_index * (-2.0 * math.log(ROPE_BASE) / HDIM))
    angles = position.astype(jnp.float32)[:, None] * inverse[None, :]
    cosine, sine = jnp.cos(angles), jnp.sin(angles)
    return (
        jnp.concatenate([cosine] * 4, axis=1),
        jnp.concatenate([-sine, sine, -sine, sine], axis=1),
    )


def swap_halves(values):
    lane = lax.broadcasted_iota(jnp.int32, values.shape, 1)
    ahead = pltpu.roll(values, PAIR - HDIM // 2, 1)
    behind = pltpu.roll(values, HDIM // 2, 1)
    return jnp.where(lax.rem(lane, HDIM) < HDIM // 2, ahead, behind)


def rotate_back(values, cosine, sine):
    return values * cosine - swap_halves(values) * sine


class LineSum:
    SLOTS = (4, 4, 4, 6, 4, 6, 8, 4, 4, 8)

    def __init__(self, total, outs, tile, scratch):
        self.paired = lax.axis_size("dp") == 16
        assert lax.axis_size("dp") in (8, 16)
        self.lag_p = 1
        self.lag_a = 1 + HOP_LAG * self.paired
        self.lag_b = self.lag_a + HOP_LAG
        self.lag_c = self.lag_b + HOP_LAG
        self.lag_f = self.lag_c + HOP_LAG
        self.lag_o = self.lag_f + 1
        self.lag_d = self.lag_o + 1
        self.total = total
        self.outs = outs
        self.tile_rows, self.tile_cols = tile
        self.half = self.tile_rows // 2
        (
            self.stage, self.r_e, self.s_one, self.r_a, self.s_two, self.r_b, self.tot, self.r_f,
            self.s_zero, self.r_p, self.sems, self.out_sems,
        ) = scratch
        dp = lax.axis_index("dp")
        self.tensor = lax.axis_index("tensor")
        self.core = lax.rem(dp, 2)
        z = lax.rem(dp // 2, 4)
        self.is_end = (z == 0) | (z == 3)
        self.is_mid = jnp.logical_not(self.is_end)
        self.sibling = dp + 1 - 2 * self.core
        self.near = dp + jnp.where((z == 0) | (z == 2), 2, -2)
        self.across = dp + 6 - 4 * z
        self.twin = lax.rem(dp + 8, lax.axis_size("dp"))

    @classmethod
    def scratch_shapes(cls, tile):
        rows, cols = tile
        buffers = [
            pltpu.VMEM(
                (slots, 2, rows // 2, cols) if i == 0 else (slots, rows // 2, cols), jnp.bfloat16
            )
            for i, slots in enumerate(cls.SLOTS)
        ]
        if lax.axis_size("dp") != 16:
            buffers[8] = buffers[9] = pltpu.VMEM((1, 8, 128), jnp.bfloat16)
        return buffers + [pltpu.SemaphoreType.DMA((12, 8)), pltpu.SemaphoreType.DMA((2, 8))]

    def copy(self, hop, chunk, src, dst, target):
        slot = lax.rem(chunk, 8)
        return pltpu.make_async_remote_copy(
            src_ref=src, dst_ref=dst, send_sem=self.sems.at[2 * hop, slot],
            recv_sem=self.sems.at[2 * hop + 1, slot],
            device_id=(target, self.tensor), device_id_type=MESH,
        )

    @staticmethod
    def slot(ref, chunk):
        return ref.at[lax.rem(chunk, ref.shape[0])]

    def hop_e(self, chunk):
        src = self.stage.at[lax.rem(chunk, self.stage.shape[0]), 1 - self.core]
        return self.copy(0, chunk, src, self.slot(self.r_e, chunk), self.sibling)

    def hop_a(self, chunk):
        return self.copy(
            1, chunk, self.slot(self.s_one, chunk), self.slot(self.r_a, chunk), self.near
        )

    def hop_b(self, chunk):
        return self.copy(
            2, chunk, self.slot(self.s_two, chunk), self.slot(self.r_b, chunk), self.across
        )

    def hop_c(self, chunk):
        return self.copy(
            3, chunk, self.slot(self.tot, chunk), self.slot(self.tot, chunk), self.near
        )

    def hop_f(self, chunk):
        return self.copy(
            4, chunk, self.slot(self.tot, chunk), self.slot(self.r_f, chunk), self.sibling
        )

    def hop_p(self, chunk):
        return self.copy(
            5, chunk, self.slot(self.s_zero, chunk), self.slot(self.r_p, chunk), self.twin
        )

    def out_copies(self, chunk, ref, tile_row, tile_col):
        cols = span(tile_col * self.tile_cols, self.tile_cols)
        first = tile_row * self.tile_rows
        mine = span(first + self.core * self.half, self.half)
        other = span(first + (1 - self.core) * self.half, self.half)
        slot = lax.rem(chunk, 8)
        return (
            pltpu.make_async_copy(
                self.slot(self.tot, chunk), ref.at[mine, cols], self.out_sems.at[0, slot]
            ),
            pltpu.make_async_copy(
                self.slot(self.r_f, chunk), ref.at[other, cols], self.out_sems.at[1, slot]
            ),
        )

    def on_out(self, chunk, act):
        for ref, first, count, tiles_across in self.outs:
            local = chunk - first

            @pl.when((local >= 0) & (local < count))
            def _(ref=ref, local=local, tiles_across=tiles_across):
                for one in self.out_copies(
                    chunk, ref, local // tiles_across, lax.rem(local, tiles_across)
                ):
                    act(one)

    def at(self, chunk, work):
        @pl.when((chunk >= 0) & (chunk < self.total))
        def _():
            work(chunk)

    def put(self, chunk, value):
        self.stage[lax.rem(chunk, self.stage.shape[0])] = value.astype(jnp.bfloat16).reshape(
            2, self.half, self.tile_cols
        )

    def add(self, into, left, right, chunk):
        total = self.slot(left, chunk)[...].astype(jnp.float32)
        total += self.slot(right, chunk)[...].astype(jnp.float32)
        self.slot(into, chunk)[...] = total.astype(jnp.bfloat16)

    def join_cores(self, into, chunk):
        self.hop_e(chunk).wait()
        total = self.stage[lax.rem(chunk, self.stage.shape[0]), self.core].astype(jnp.float32)
        total += self.slot(self.r_e, chunk)[...].astype(jnp.float32)
        self.slot(into, chunk)[...] = total.astype(jnp.bfloat16)

    def tick(self, k):
        def drop(chunk):
            self.on_out(chunk, lambda one: one.wait())

        def out(chunk):
            self.hop_f(chunk).wait()
            self.on_out(chunk, lambda one: one.start())

        def final(chunk):
            @pl.when(self.is_end)
            def _():
                self.hop_c(chunk).wait_recv()

            @pl.when(self.is_mid)
            def _():
                self.hop_c(chunk).wait_send()

            self.hop_f(chunk).start()

        def back(chunk):
            @pl.when(self.is_mid)
            def _():
                self.hop_b(chunk).wait()
                self.add(self.tot, self.s_two, self.r_b, chunk)
                self.hop_c(chunk).start()

        def across(chunk):
            @pl.when(self.is_mid)
            def _():
                self.hop_a(chunk).wait_recv()
                self.add(self.s_two, self.s_one, self.r_a, chunk)
                self.hop_b(chunk).start()

            @pl.when(self.is_end)
            def _():
                self.hop_a(chunk).wait_send()

        def inward(chunk):
            if self.paired:
                self.hop_p(chunk).wait()
                self.add(self.s_one, self.s_zero, self.r_p, chunk)
            else:
                self.join_cores(self.s_one, chunk)

            @pl.when(self.is_end)
            def _():
                self.hop_a(chunk).start()

        def pair(chunk):
            self.join_cores(self.s_zero, chunk)
            self.hop_p(chunk).start()

        self.at(k - self.lag_d, drop)
        self.at(k - self.lag_o, out)
        self.at(k - self.lag_f, final)
        self.at(k - self.lag_c, back)
        self.at(k - self.lag_b, across)
        self.at(k - self.lag_a, inward)
        if self.paired:
            self.at(k - self.lag_p, pair)
        self.at(k, lambda chunk: self.hop_e(chunk).start())


class Sizes:
    def __init__(self, slots, width, share, hidden, attn):
        self.slots, self.width, self.share = slots, width, share
        self.hidden, self.attn = hidden, attn
        self.peers = width // share
        self.pairs = attn // PAIR
        self.tile = (min(512, attn), min(512, attn))
        shapes = [
            (hidden, width), (width, hidden), (width, hidden),
            (attn, width), (width, attn), (width, attn), (width, attn),
        ]
        self.shapes = shapes
        self.plan = []
        first = 0
        for rows, cols in shapes:
            across = cols // self.tile[1]
            count = (rows // self.tile[0]) * across
            self.plan.append((first, count, across))
            first += count
        self.total = first
        self.block_units = share // UNIT


def backward_kernel(sz, *refs):
    (
        hidden_h, silu_h, slope_h, cot_h, normed_mlp_h, mixed_h, normed_h, query_h, key_h, value_h,
        w_down_h, w_gate_h, w_up_h, w_out_h, w_query_h, w_key_h, w_value_h,
        cosine, sine, seq_col, seq_row, log_total, rms_cols, gain_attn, gain_mlp,
        *refs,
    ) = refs
    outs, (grad_tokens_h, gains_h), refs = refs[:7], refs[7:9], refs[9:]
    (
        buf_a, buf_b, buf_c, d_gate, d_up, send, full, recv, d_mixed, d_qkv, w_buf,
        acc_key, acc_value, row_part, row_send, row_recv, gains, gains_out,
        load_sems, w_sems, tensor_sems, gain_sems, *line_scratch,
    ) = refs
    slots, width, share, peers = sz.slots, sz.width, sz.share, sz.peers
    n_dp = lax.axis_size("dp")
    dp, me = lax.axis_index("dp"), lax.axis_index("tensor")
    line = LineSum(
        sz.total, [(ref,) + plan for ref, plan in zip(outs, sz.plan)], sz.tile, line_scratch
    )
    tile_rows, tile_cols = sz.tile

    def load(src, dst, index):
        return pltpu.make_async_copy(src, dst, load_sems.at[index])

    def peer(away):
        return lax.rem(me + away, peers)

    def other_dp(away):
        return lax.rem(dp + away, n_dp)

    barrier = pltpu.get_barrier_semaphore()
    first_loads = [load(hidden_h, buf_a.at[:, pl.ds(0, sz.hidden)], 0), load(cot_h, buf_b, 1),
                   load(normed_mlp_h, buf_c, 2)]
    for one in first_loads:
        one.start()
    for away in range(1, n_dp):
        pl.semaphore_signal(
            barrier, inc=1, device_id=(other_dp(away), me), device_id_type=MESH
        )
    for away in range(1, peers):
        pl.semaphore_signal(barrier, inc=1, device_id=(dp, peer(away)), device_id_type=MESH)
    pl.semaphore_wait(barrier, n_dp - 1 + peers - 1)

    attn_at = [pl.ds(i * sz.attn, sz.attn) for i in range(4)]
    grads = [
        (lambda r: buf_a[:, r], lambda c: buf_b[:, c]),
        (lambda r: buf_c[:, r], lambda c: d_gate[:, c]),
        (lambda r: buf_c[:, r], lambda c: d_up[:, c]),
        (lambda r: d_gate[:, pl.ds(pl.multiple_of(3 * sz.attn + r.start, tile_rows), tile_rows)],
         lambda c: buf_a[:, c]),
        (lambda r: buf_b[:, r], lambda c: d_qkv[2, :, c]),
        (lambda r: buf_b[:, r], lambda c: d_qkv[0, :, c]),
        (lambda r: buf_b[:, r], lambda c: d_qkv[1, :, c]),
    ]

    def tile_tick(m, k):
        first, _, across = sz.plan[m]
        rows = span(((k - first) // across) * tile_rows, tile_rows)
        cols = span(lax.rem(k - first, across) * tile_cols, tile_cols)
        left, right = grads[m]
        line.put(k, matmul_first(left(rows), right(cols)))
        line.tick(k)

    cursor = [0]

    def matrix_of(k):
        return [m for m, (first, count, _) in enumerate(sz.plan) if first <= k < first + count][0]

    def advance_to(stop):
        while cursor[0] < stop:
            m = matrix_of(cursor[0])
            until = min(stop, sz.plan[m][0] + sz.plan[m][1])

            @pl.loop(cursor[0], until)
            def _(k, m=m):
                tile_tick(m, k)

            cursor[0] = until

    def run_units(count, unit, group=1):
        done = 0
        while done < count:
            m = matrix_of(cursor[0])
            room = (sz.plan[m][0] + sz.plan[m][1] - cursor[0]) // group
            if not room:
                for g in range(group):
                    unit(done, g)
                    tile_tick(matrix_of(cursor[0]), cursor[0])
                    cursor[0] += 1
                done += 1
                continue
            step = min(room, count - done)

            @pl.loop(0, step)
            def _(i, m=m, done=done, start=cursor[0]):
                for g in range(group):
                    unit(done + i, g)
                    tile_tick(m, start + i * group + g)

            cursor[0] += step * group
            done += step

    def hidden_loads(u):
        cols = span(u * UNIT, UNIT)
        slot = lax.rem(u, 2)
        return (
            pltpu.make_async_copy(w_down_h.at[cols, :], w_buf.at[slot, 0], w_sems.at[0, slot]),
            pltpu.make_async_copy(
                silu_h.at[:, cols], d_qkv.at[slot, :, pl.ds(0, UNIT)], w_sems.at[1, slot]
            ),
            pltpu.make_async_copy(
                slope_h.at[:, cols], d_qkv.at[slot, :, pl.ds(UNIT, UNIT)], w_sems.at[2, slot]
            ),
        )

    def prefetched(count, loads, u):
        for one in loads(u):
            one.wait()

        @pl.when(u + 1 < count)
        def _():
            for one in loads(u + 1):
                one.start()

    def hidden_unit(u, _):
        prefetched(sz.hidden // UNIT, hidden_loads, u)
        slot = lax.rem(u, 2)
        cols = span(u * UNIT, UNIT)
        d_hidden = matmul_last(buf_b[...], w_buf[slot, 0])
        d_up[:, cols] = (d_hidden * d_qkv[slot, :, pl.ds(0, UNIT)]).astype(jnp.bfloat16)
        d_gate[:, cols] = (d_hidden * d_qkv[slot, :, pl.ds(UNIT, UNIT)]).astype(jnp.bfloat16)

    for one in hidden_loads(0):
        one.start()
    for one in first_loads:
        one.wait()
    run_units(sz.hidden // UNIT, hidden_unit)

    def block_of(u):
        return peer(u // sz.block_units + 1)

    def feature(u):
        return block_of(u) * share + lax.rem(u, sz.block_units) * UNIT

    def scatter(round_, away):
        return pltpu.make_async_remote_copy(
            src_ref=send.at[peer(away)], dst_ref=recv.at[away - 1],
            send_sem=tensor_sems.at[2 * round_, away], recv_sem=tensor_sems.at[2 * round_ + 1, away],
            device_id=(dp, peer(away)), device_id_type=MESH,
        )

    def store_part(round_, u, value):
        send[block_of(u), :, span(lax.rem(u, sz.block_units) * UNIT, UNIT)] = value.astype(
            jnp.bfloat16
        )
        for away in range(1, peers):
            @pl.when(u == away * sz.block_units - 1)
            def _(away=away):
                scatter(round_, away).start()

    def gathered(round_):
        for away in range(1, peers):
            scatter(round_, away).wait()
        total = send[me].astype(jnp.float32)
        for away in range(1, peers):
            total += recv[away - 1].astype(jnp.float32)
        return total

    mlp_units = width // UNIT
    hid = pl.ds(0, sz.hidden)

    def mlp_loads(u):
        slot = lax.rem(u, 2)
        rows = span(feature(u), UNIT)
        return (
            pltpu.make_async_copy(
                w_gate_h.at[rows, :], w_buf.at[slot, 0, :, hid], w_sems.at[0, slot]
            ),
            pltpu.make_async_copy(
                w_up_h.at[rows, :], w_buf.at[slot, 1, :, hid], w_sems.at[1, slot]
            ),
        )

    def mlp_unit(u, _):
        prefetched(mlp_units, mlp_loads, u)
        slot = lax.rem(u, 2)
        part = matmul_last(d_gate[...], w_buf[slot, 0, :, hid])
        part += matmul_last(d_up[...], w_buf[slot, 1, :, hid])
        store_part(0, u, part)

    for one in mlp_loads(0):
        one.start()
    run_units(mlp_units, mlp_unit)
    advance_to(cursor[0] + 4)

    def spread(away):
        return pltpu.make_async_remote_copy(
            src_ref=full.at[me], dst_ref=full.at[me],
            send_sem=tensor_sems.at[4, away], recv_sem=tensor_sems.at[5, away],
            device_id=(dp, peer(away)), device_id_type=MESH,
        )

    w_out_rows = sz.attn // UNIT
    w_out_loads = [
        load(w_out_h.at[pl.ds(i * UNIT, UNIT), :], w_buf.at[0, i], 3 + i) for i in range(w_out_rows)
    ]
    for one in w_out_loads:
        one.start()
    full[me] = gathered(0).astype(jnp.bfloat16)
    for away in range(1, peers):
        spread(away).start()
    advance_to(cursor[0] + 8)
    for away in range(1, peers):
        spread(away).wait()
    for one in w_out_loads:
        one.wait()

    gains[dp] = jnp.zeros_like(gains[dp])

    def norm_unit(u, _):
        rows = span(u * UNIT, UNIT)
        row_sum = jnp.zeros((UNIT, 1), jnp.float32)
        for b in range(peers):
            at = pl.ds(b * share, share)
            row_sum += jnp.sum(
                full[b, rows, :].astype(jnp.float32) * buf_c[rows, at].astype(jnp.float32),
                axis=1, keepdims=True,
            )
        rms = rms_cols[rows, 0:1]
        for b in range(peers):
            at = pl.ds(b * share, share)
            gain = gain_mlp[0:1, at]
            lean = buf_c[rows, at].astype(jnp.float32) / gain * (row_sum / width)
            d_resid = buf_b[rows, at].astype(jnp.float32) + rms * (
                gain * full[b, rows, :].astype(jnp.float32) - lean
            )
            buf_a[rows, at] = d_resid.astype(jnp.bfloat16)
        own = span(me * share, share)
        gains[dp, 0:1, :] += jnp.sum(
            full[me, rows, :].astype(jnp.float32) * buf_c[rows, own].astype(jnp.float32),
            axis=0, keepdims=True,
        ) / gain_mlp[0:1, own]
        for i in range(w_out_rows):
            d_mixed[rows, pl.ds(i * UNIT, UNIT)] = matmul_last(
                buf_a[rows, :], w_buf[0, i]
            ).astype(jnp.bfloat16)

    run_units(slots // UNIT, norm_unit)
    advance_to(sz.plan[2][0])

    attn_loads = [
        load(ref, d_gate.at[:, attn_at[i]], 5 + i)
        for i, ref in enumerate((query_h, key_h, value_h, mixed_h))
    ] + [load(normed_h, buf_b, 9)]
    for one in attn_loads:
        one.start()
    for one in attn_loads:
        one.wait()
    blocks = slots // UNIT

    def attend_unit(p, i):
        rows = pl.ds(i * UNIT, UNIT)
        keys = (i + 1) * UNIT
        lanes = [pl.ds(pl.multiple_of(j * sz.attn + p * PAIR, PAIR), PAIR) for j in range(3)]
        mine = span(p * PAIR, PAIR)
        query = d_gate[rows, lanes[0]]
        key = d_gate[pl.ds(0, keys), lanes[1]]
        value = d_gate[pl.ds(0, keys), lanes[2]]
        grad = d_mixed[rows, mine]
        first_head = lax.broadcasted_iota(jnp.int32, (1, PAIR), 1) < HDIM
        key_slot = lax.broadcasted_iota(jnp.int32, (keys, UNIT), 0)
        query_slot = lax.broadcasted_iota(jnp.int32, (keys, UNIT), 1) + i * UNIT
        allowed = (seq_col[pl.ds(0, keys), 0:1] == seq_row[0:1, rows]) & (key_slot <= query_slot)
        found = []
        for h in range(2):
            chosen = first_head if h == 0 else jnp.logical_not(first_head)
            scores = matmul_last(key, jnp.where(chosen, query, 0.0)) * SCALE
            scores -= log_total[pl.ds(2 * p + h, 1), rows]
            probs = jnp.exp(jnp.where(allowed, scores, MASKED))
            grad_probs = matmul_last(value, jnp.where(chosen, grad, 0.0))
            delta = jnp.sum(probs * grad_probs, axis=0, keepdims=True)
            grad_scores = (probs * (grad_probs - delta)).astype(jnp.bfloat16)
            found.append(
                (
                    matmul_first(grad_scores, key),
                    matmul(grad_scores, query),
                    matmul(probs.astype(jnp.bfloat16), grad),
                )
            )
        grad_query, grad_key, grad_value = [
            jnp.where(first_head, one, two) for one, two in zip(*found)
        ]
        d_qkv[0, rows, mine] = rotate_back(
            grad_query * SCALE, cosine[rows, :], sine[rows, :]
        ).astype(jnp.bfloat16)
        for acc, part in ((acc_key, grad_key), (acc_value, grad_value)):
            if i > 0:
                acc[pl.ds(0, keys - UNIT), :] += part[: keys - UNIT]
            acc[pl.ds(keys - UNIT, UNIT), :] = part[keys - UNIT :]
        if i + 1 == blocks:
            d_qkv[1, :, mine] = rotate_back(acc_key[...] * SCALE, cosine[...], sine[...]).astype(
                jnp.bfloat16
            )
            d_qkv[2, :, mine] = acc_value[...].astype(jnp.bfloat16)

    run_units(sz.pairs, attend_unit, blocks)
    advance_to(sz.plan[3][0])

    row_part[...] = jnp.zeros_like(row_part)

    def attn_loads_of(u):
        slot = lax.rem(u, 2)
        rows = span(feature(u), UNIT)
        return [
            pltpu.make_async_copy(ref.at[rows, :], w_buf.at[slot, 0, :, at], w_sems.at[i, slot])
            for i, (ref, at) in enumerate(zip((w_query_h, w_key_h, w_value_h), attn_at))
        ]

    def attn_unit(u, _):
        prefetched(mlp_units, attn_loads_of, u)
        slot = lax.rem(u, 2)
        part = jnp.zeros((slots, UNIT), jnp.float32)
        for i in range(3):
            part += matmul_last(d_qkv[i, :, pl.ds(0, sz.attn)], w_buf[slot, 0, :, attn_at[i]])
        store_part(1, u, part)
        row_part[...] += jnp.sum(
            part * buf_b[:, span(feature(u), UNIT)].astype(jnp.float32), axis=1, keepdims=True
        )

    def row_scatter(away):
        return pltpu.make_async_remote_copy(
            src_ref=row_send, dst_ref=row_recv.at[away - 1],
            send_sem=tensor_sems.at[6, away], recv_sem=tensor_sems.at[7, away],
            device_id=(dp, peer(away)), device_id_type=MESH,
        )

    for one in attn_loads_of(0):
        one.start()
    run_units(mlp_units, attn_unit)
    row_send[...] = row_part[...].T[0:8, :]
    for away in range(1, peers):
        row_scatter(away).start()
    advance_to(sz.total - 2)
    for away in range(1, peers):
        row_scatter(away).wait()
    row_sums = row_send[...]
    for away in range(1, peers):
        row_sums += row_recv[away - 1]
    row_part[...] = jnp.concatenate([row_sums] * (row_part.shape[1] // 8), axis=0).T
    own = span(me * share, share)
    d_own = gathered(1)
    straight = buf_b[:, own].astype(jnp.float32)
    gain = gain_attn[0:1, own]
    gains[dp, 1:2, :] = jnp.sum(d_own * straight, axis=0, keepdims=True) / gain
    send[me] = (
        buf_a[:, own].astype(jnp.float32)
        + rms_cols[:, 1:2] * (gain * d_own - straight / gain * (row_part[:, 0:1] / width))
    ).astype(jnp.bfloat16)
    grad_out = load(send.at[me], grad_tokens_h, 10)
    grad_out.start()

    def gain_copy(away):
        return pltpu.make_async_remote_copy(
            src_ref=gains.at[dp], dst_ref=gains.at[dp],
            send_sem=gain_sems.at[0, away], recv_sem=gain_sems.at[1, away],
            device_id=(other_dp(away), me), device_id_type=MESH,
        )

    for away in range(1, n_dp):
        gain_copy(away).start()
    advance_to(sz.total)
    grad_out.wait()
    for away in range(1, n_dp):
        gain_copy(away).wait()
    total = gains[0]
    for i in range(1, n_dp):
        total += gains[i]
    gains_out[...] = total
    gain_out = load(gains_out, gains_h, 11)
    gain_out.start()

    @pl.loop(sz.total, sz.total + line.lag_d)
    def _(k):
        line.tick(k)

    gain_out.wait()


def backward(sz, big, small):
    whole_rows = pltpu.VMEM((sz.slots, sz.width), jnp.bfloat16)
    hidden_rows = pltpu.VMEM((sz.slots, sz.hidden), jnp.bfloat16)
    assert sz.hidden == 4 * sz.attn and sz.share % UNIT == 0 and sz.hidden <= sz.width
    n_dp = lax.axis_size("dp")
    attn_rows = max(sz.attn, 2 * UNIT)
    flops = 6 * sz.slots * (3 * sz.width * sz.hidden + 4 * sz.width * sz.attn)
    return pl.pallas_call(
        functools.partial(backward_kernel, sz),
        out_shape=[jax.ShapeDtypeStruct(s, jnp.bfloat16) for s in sz.shapes]
        + [
            jax.ShapeDtypeStruct((sz.slots, sz.share), jnp.bfloat16),
            jax.ShapeDtypeStruct((8, sz.share), jnp.float32),
        ],
        in_specs=[pl.BlockSpec(memory_space=pl.ANY)] * len(big)
        + [pl.BlockSpec(memory_space=pltpu.VMEM)] * len(small),
        out_specs=[pl.BlockSpec(memory_space=pl.ANY)] * 9,
        scratch_shapes=[
            whole_rows, whole_rows, whole_rows, hidden_rows, hidden_rows,
            pltpu.VMEM((sz.peers, sz.slots, sz.share), jnp.bfloat16),
            pltpu.VMEM((sz.peers, sz.slots, sz.share), jnp.bfloat16),
            pltpu.VMEM((sz.peers - 1, sz.slots, sz.share), jnp.bfloat16),
            pltpu.VMEM((sz.slots, sz.attn), jnp.bfloat16),
            pltpu.VMEM((3, sz.slots, attn_rows), jnp.bfloat16),
            pltpu.VMEM((2, 2, UNIT, sz.width), jnp.bfloat16),
            pltpu.VMEM((sz.slots, PAIR), jnp.float32),
            pltpu.VMEM((sz.slots, PAIR), jnp.float32),
            pltpu.VMEM((sz.slots, PAIR), jnp.float32),
            pltpu.VMEM((8, sz.slots), jnp.float32),
            pltpu.VMEM((sz.peers - 1, 8, sz.slots), jnp.float32),
            pltpu.VMEM((n_dp, 8, sz.share), jnp.float32),
            pltpu.VMEM((8, sz.share), jnp.float32),
            pltpu.SemaphoreType.DMA((12,)),
            pltpu.SemaphoreType.DMA((3, 2)),
            pltpu.SemaphoreType.DMA((8, sz.peers)),
            pltpu.SemaphoreType.DMA((2, n_dp)),
        ]
        + LineSum.scratch_shapes(sz.tile),
        compiler_params=pltpu.CompilerParams(
            collective_id=0, has_side_effects=True, vmem_limit_bytes=63 * MIB
        ),
        cost_estimate=pl.CostEstimate(
            flops=flops, bytes_accessed=200 * MIB, transcendentals=sz.slots * sz.slots * 8
        ),
    )(*big, *small)


def rotate(values, cosine, sine_part):
    half_width = values.shape[-1] // 2
    first_half = values[..., :half_width]
    second = values[..., half_width:]
    return jnp.concatenate(
        [first_half * cosine - second * sine_part, second * cosine + first_half * sine_part],
        axis=-1,
    )


def piece_mask(sequence, first_row, last_row):
    query_slots = jnp.arange(first_row, last_row)
    key_slots = jnp.arange(last_row)
    same_seq = sequence[first_row:last_row, None] == sequence[None, :last_row]
    return same_seq & (key_slots[None, :] <= query_slots[:, None])


def piece_scores(query_rows, key_rows, sequence, first_row, last_row, score_scale):
    scores = (
        jnp.einsum(
            "qhd,khd->hqk",
            query_rows[first_row:last_row],
            key_rows[:last_row],
            preferred_element_type=jnp.float32,
        )
        * score_scale
    )
    allowed = piece_mask(sequence, first_row, last_row)
    return jnp.where(allowed[None], scores, MASKED)


def attend_forward(query_rows, key_rows, value_rows, sequence, piece_rows, score_scale):
    slot_count = query_rows.shape[0]
    outputs = []
    log_totals = []
    for piece_index in range(slot_count // piece_rows):
        first_row = piece_index * piece_rows
        last_row = first_row + piece_rows
        scores = piece_scores(query_rows, key_rows, sequence, first_row, last_row, score_scale)
        peak = jnp.max(scores, axis=-1, keepdims=True)
        expon = jnp.exp(scores - peak)
        row_total = jnp.sum(expon, axis=-1, keepdims=True)
        weights = (expon / row_total).astype(jnp.bfloat16)
        outputs.append(
            jnp.einsum(
                "hqk,khd->qhd", weights, value_rows[:last_row], preferred_element_type=jnp.float32
            ).astype(jnp.bfloat16)
        )
        log_totals.append(peak + jnp.log(row_total))
    return (jnp.concatenate(outputs, axis=0), log_totals)


def body(
    tokens,
    norm_gain_attn,
    norm_gain_mlp,
    w_query,
    w_key,
    w_value,
    w_out,
    w_gate,
    w_up,
    w_down,
    cotangent,
    lengths,
):
    slot_count = tokens.shape[0]
    share_width = tokens.shape[1]
    model_width = share_width * lax.axis_size("tensor")
    attn_width = w_query.shape[1]
    heads_here = attn_width // HDIM
    piece_rows = min(512, slot_count)
    sz = Sizes(slot_count, model_width, share_width, w_gate.shape[1], attn_width)
    col_start = lax.axis_index("tensor") * share_width
    gain_mlp_here = lax.dynamic_slice_in_dim(norm_gain_mlp, col_start, share_width)
    sequence, position = positions(lengths[0], slot_count)
    cos_lanes, sin_lanes = rotate_tables(position)
    cosine, sine_part = cos_lanes[:, None, :32], sin_lanes[:, None, 32:64]
    full_input = lax.all_gather(tokens, "tensor", axis=1, tiled=True).astype(jnp.float32)
    rms_attn = lax.rsqrt(jnp.mean(full_input * full_input, axis=-1, keepdims=True) + EPSILON)
    normed = (full_input * rms_attn * norm_gain_attn).astype(jnp.bfloat16)
    query_lin = matmul(normed, w_query)
    key_lin = matmul(normed, w_key)
    value_lin = matmul(normed, w_value)
    query_rows = rotate(query_lin.reshape(slot_count, heads_here, HDIM), cosine, sine_part).astype(
        jnp.bfloat16
    )
    key_rows = rotate(key_lin.reshape(slot_count, heads_here, HDIM), cosine, sine_part).astype(
        jnp.bfloat16
    )
    value_rows = value_lin.astype(jnp.bfloat16).reshape(slot_count, heads_here, HDIM)
    mixed_heads, log_totals = attend_forward(
        query_rows, key_rows, value_rows, sequence, piece_rows, SCALE
    )
    log_total = jnp.concatenate(log_totals, axis=1)[..., 0]
    mixed_flat = mixed_heads.reshape(slot_count, attn_width)
    attn_part = matmul(mixed_flat, w_out)
    input_here = tokens.astype(jnp.float32)
    attn_here = lax.psum_scatter(attn_part, "tensor", scatter_dimension=1, tiled=True)
    resid_here = input_here + attn_here
    square_sum = lax.psum(jnp.sum(resid_here * resid_here, axis=1), "tensor")
    rms_mlp = lax.rsqrt(square_sum[:, None] / model_width + EPSILON)
    normed_here = (resid_here * rms_mlp * gain_mlp_here).astype(jnp.bfloat16)
    normed_mlp = lax.all_gather(normed_here, "tensor", axis=1, tiled=True)
    gate_proj = matmul(normed_mlp, w_gate)
    upward = matmul(normed_mlp, w_up)
    sigmoid_gate = jax.nn.sigmoid(gate_proj)
    silu_gate = gate_proj * sigmoid_gate
    hidden = (silu_gate * upward).astype(jnp.bfloat16)
    slope = (upward * sigmoid_gate * (1.0 + gate_proj * (1.0 - sigmoid_gate))).astype(jnp.bfloat16)
    mlp_part = matmul(hidden, w_down)
    mlp_here = lax.psum_scatter(
        mlp_part.astype(jnp.bfloat16), "tensor", scatter_dimension=1, tiled=True
    ).astype(jnp.float32)
    out_tokens = (resid_here + mlp_here).astype(jnp.bfloat16)
    cot_rows = lax.all_gather(cotangent, "tensor", axis=1, tiled=True)

    def flat(values):
        return values.reshape(slot_count, attn_width)

    big = (
        hidden, silu_gate.astype(jnp.bfloat16), slope, cot_rows, normed_mlp, mixed_flat, normed,
        flat(query_rows), flat(key_rows), flat(value_rows),
        w_down, w_gate, w_up, w_out, w_query, w_key, w_value,
    )
    lanes = jnp.arange(PAIR)[None, :]
    small = (
        cos_lanes, sin_lanes,
        jnp.broadcast_to(sequence[:, None], (slot_count, PAIR)),
        jnp.broadcast_to(sequence[None, :], (8, slot_count)),
        log_total,
        jnp.where(lanes == 0, rms_mlp, rms_attn),
        jnp.broadcast_to(norm_gain_attn[None, :], (8, model_width)),
        jnp.broadcast_to(norm_gain_mlp[None, :], (8, model_width)),
    )
    down, gate, up, out, value, query, key, grad_tokens, gains = backward(sz, big, small)

    def wide(values):
        return values.astype(jnp.float32)

    return (
        out_tokens,
        grad_tokens,
        gains[1],
        gains[0],
        wide(query),
        wide(key),
        wide(value),
        wide(out),
        wide(gate),
        wide(up),
        wide(down),
    )


def solution(mesh):
    placed = (
        P("dp", "tensor"),
        P(),
        P(),
        P(None, "tensor"),
        P(None, "tensor"),
        P(None, "tensor"),
        P("tensor", None),
        P(None, "tensor"),
        P(None, "tensor"),
        P("tensor", None),
        P("dp", "tensor"),
        P("dp", None),
    )
    return jax.shard_map(
        body,
        mesh=mesh,
        in_specs=placed,
        out_specs=(
            P("dp", "tensor"),
            P("dp", "tensor"),
            P("tensor"),
            P("tensor"),
            P(None, "tensor"),
            P(None, "tensor"),
            P(None, "tensor"),
            P("tensor", None),
            P(None, "tensor"),
            P(None, "tensor"),
            P("tensor", None),
        ),
        check_vma=False,
    )
```

```python
import functools
import math

import jax
import jax.numpy as jnp
from jax import lax
from jax.experimental import pallas as pl
from jax.experimental.pallas import tpu as pltpu
from jax.sharding import PartitionSpec as P

HDIM = 64
PAIR = 2 * HDIM


EPSILON = 1e-05
ROPE_BASE = 130000.0
SCALE = HDIM ** (-0.5)
MASKED = -1e30
MESH = pl.DeviceIdType.MESH
HOP_LAG = 2
UNIT = 256
MIB = 1024 * 1024


def matmul_first(left, right):
    return lax.dot_general(
        left, right, (((0,), (0,)), ((), ())), preferred_element_type=jnp.float32
    )


def matmul_last(left, right):
    return lax.dot_general(
        left, right, (((1,), (1,)), ((), ())), preferred_element_type=jnp.float32
    )


def matmul(left, right):
    return jnp.dot(left, right, preferred_element_type=jnp.float32)


def span(first, size):
    return pl.ds(pl.multiple_of(first, size), size)


def positions(length_row, slot_count):
    slot_index = jnp.arange(slot_count, dtype=jnp.int32)
    seq_ends = jnp.cumsum(length_row)
    passed = seq_ends[None, :] <= slot_index[:, None]
    seq_number = jnp.sum(passed.astype(jnp.int32), axis=1)
    seq_start = jnp.sum(jnp.where(passed, length_row[None, :], 0), axis=1)
    is_live = slot_index < seq_ends[-1]
    sequence = jnp.where(is_live, seq_number, slot_count + slot_index)
    position = jnp.where(is_live, slot_index - seq_start, 0)
    return (sequence, position)


def rotate_tables(position):
    half_width = HDIM // 2
    freq_index = jnp.arange(half_width).astype(jnp.float32)
    inverse = jnp.exp(freq_index * (-2.0 * math.log(ROPE_BASE) / HDIM))
    angles = position.astype(jnp.float32)[:, None] * inverse[None, :]
    cosine, sine = jnp.cos(angles), jnp.sin(angles)
    return (
        jnp.concatenate([cosine] * 4, axis=1),
        jnp.concatenate([-sine, sine, -sine, sine], axis=1),
    )


def swap_halves(values):
    lane = lax.broadcasted_iota(jnp.int32, values.shape, 1)
    ahead = pltpu.roll(values, PAIR - HDIM // 2, 1)
    behind = pltpu.roll(values, HDIM // 2, 1)
    return jnp.where(lax.rem(lane, HDIM) < HDIM // 2, ahead, behind)


def rotate_back(values, cosine, sine):
    return values * cosine - swap_halves(values) * sine


class LineSum:
    SLOTS = (2, 2, 2, 6, 2, 4, 8, 3, 2, 4)

    def __init__(self, total, outs, tile, scratch):
        self.paired = lax.axis_size("dp") == 16
        assert lax.axis_size("dp") in (8, 16)
        self.lag_p = 1
        self.lag_a = 1 + HOP_LAG * self.paired
        self.lag_b = self.lag_a + HOP_LAG
        self.lag_c = self.lag_b + HOP_LAG
        self.lag_f = self.lag_c + HOP_LAG
        self.lag_o = self.lag_f + 1
        self.lag_d = self.lag_o + 1
        self.total = total
        self.outs = outs
        self.tile_rows, self.tile_cols = tile
        self.half = self.tile_rows // 2
        (
            self.stage, self.r_e, self.s_one, self.r_a, self.s_two, self.r_b, self.tot, self.r_f,
            self.s_zero, self.r_p, self.sems, self.out_sems,
        ) = scratch
        dp = lax.axis_index("dp")
        self.tensor = lax.axis_index("tensor")
        self.core = lax.rem(dp, 2)
        z = lax.rem(dp // 2, 4)
        self.is_end = (z == 0) | (z == 3)
        self.is_mid = jnp.logical_not(self.is_end)
        self.sibling = dp + 1 - 2 * self.core
        self.near = dp + jnp.where((z == 0) | (z == 2), 2, -2)
        self.across = dp + 6 - 4 * z
        self.twin = lax.rem(dp + 8, lax.axis_size("dp"))

    @classmethod
    def scratch_shapes(cls, tile):
        rows, cols = tile
        buffers = [
            pltpu.VMEM(
                (slots, 2, rows // 2, cols) if i == 0 else (slots, rows // 2, cols), jnp.bfloat16
            )
            for i, slots in enumerate(cls.SLOTS)
        ]
        if lax.axis_size("dp") != 16:
            buffers[8] = buffers[9] = pltpu.VMEM((1, 8, 128), jnp.bfloat16)
        return buffers + [pltpu.SemaphoreType.DMA((12, 8)), pltpu.SemaphoreType.DMA((2, 8))]

    def copy(self, hop, chunk, src, dst, target):
        slot = lax.rem(chunk, 8)
        return pltpu.make_async_remote_copy(
            src_ref=src, dst_ref=dst, send_sem=self.sems.at[2 * hop, slot],
            recv_sem=self.sems.at[2 * hop + 1, slot],
            device_id=(target, self.tensor), device_id_type=MESH,
        )

    @staticmethod
    def slot(ref, chunk):
        return ref.at[lax.rem(chunk, ref.shape[0])]

    def hop_e(self, chunk):
        src = self.stage.at[lax.rem(chunk, self.stage.shape[0]), 1 - self.core]
        return self.copy(0, chunk, src, self.slot(self.r_e, chunk), self.sibling)

    def hop_a(self, chunk):
        return self.copy(
            1, chunk, self.slot(self.s_one, chunk), self.slot(self.r_a, chunk), self.near
        )

    def hop_b(self, chunk):
        return self.copy(
            2, chunk, self.slot(self.s_two, chunk), self.slot(self.r_b, chunk), self.across
        )

    def hop_c(self, chunk):
        return self.copy(
            3, chunk, self.slot(self.tot, chunk), self.slot(self.tot, chunk), self.near
        )

    def hop_f(self, chunk):
        return self.copy(
            4, chunk, self.slot(self.tot, chunk), self.slot(self.r_f, chunk), self.sibling
        )

    def hop_p(self, chunk):
        return self.copy(
            5, chunk, self.slot(self.s_zero, chunk), self.slot(self.r_p, chunk), self.twin
        )

    def out_copies(self, chunk, ref, tile_row, tile_col):
        cols = span(tile_col * self.tile_cols, self.tile_cols)
        first = tile_row * self.tile_rows
        mine = span(first + self.core * self.half, self.half)
        other = span(first + (1 - self.core) * self.half, self.half)
        slot = lax.rem(chunk, 8)
        return (
            pltpu.make_async_copy(
                self.slot(self.tot, chunk), ref.at[mine, cols], self.out_sems.at[0, slot]
            ),
            pltpu.make_async_copy(
                self.slot(self.r_f, chunk), ref.at[other, cols], self.out_sems.at[1, slot]
            ),
        )

    def on_out(self, chunk, act):
        for ref, first, count, place in self.outs:
            local = chunk - first

            @pl.when((local >= 0) & (local < count))
            def _(ref=ref, local=local, place=place):
                for one in self.out_copies(chunk, ref, *place(local)):
                    act(one)

    def at(self, chunk, work):
        @pl.when((chunk >= 0) & (chunk < self.total))
        def _():
            work(chunk)

    def put(self, chunk, value):
        self.stage[lax.rem(chunk, self.stage.shape[0])] = value.astype(jnp.bfloat16).reshape(
            2, self.half, self.tile_cols
        )

    def add(self, into, left, right, chunk):
        total = self.slot(left, chunk)[...].astype(jnp.float32)
        total += self.slot(right, chunk)[...].astype(jnp.float32)
        self.slot(into, chunk)[...] = total.astype(jnp.bfloat16)

    def join_cores(self, into, chunk):
        self.hop_e(chunk).wait()
        total = self.stage[lax.rem(chunk, self.stage.shape[0]), self.core].astype(jnp.float32)
        total += self.slot(self.r_e, chunk)[...].astype(jnp.float32)
        self.slot(into, chunk)[...] = total.astype(jnp.bfloat16)

    def tick(self, k):
        def drop(chunk):
            self.on_out(chunk, lambda one: one.wait())

        def out(chunk):
            self.hop_f(chunk).wait()
            self.on_out(chunk, lambda one: one.start())

        def final(chunk):
            @pl.when(self.is_end)
            def _():
                self.hop_c(chunk).wait_recv()

            @pl.when(self.is_mid)
            def _():
                self.hop_c(chunk).wait_send()

            self.hop_f(chunk).start()

        def back(chunk):
            @pl.when(self.is_mid)
            def _():
                self.hop_b(chunk).wait()
                self.add(self.tot, self.s_two, self.r_b, chunk)
                self.hop_c(chunk).start()

        def across(chunk):
            @pl.when(self.is_mid)
            def _():
                self.hop_a(chunk).wait_recv()
                self.add(self.s_two, self.s_one, self.r_a, chunk)
                self.hop_b(chunk).start()

            @pl.when(self.is_end)
            def _():
                self.hop_a(chunk).wait_send()

        def inward(chunk):
            if self.paired:
                self.hop_p(chunk).wait()
                self.add(self.s_one, self.s_zero, self.r_p, chunk)
            else:
                self.join_cores(self.s_one, chunk)

            @pl.when(self.is_end)
            def _():
                self.hop_a(chunk).start()

        def pair(chunk):
            self.join_cores(self.s_zero, chunk)
            self.hop_p(chunk).start()

        self.at(k - self.lag_d, drop)
        self.at(k - self.lag_o, out)
        self.at(k - self.lag_f, final)
        self.at(k - self.lag_c, back)
        self.at(k - self.lag_b, across)
        self.at(k - self.lag_a, inward)
        if self.paired:
            self.at(k - self.lag_p, pair)
        self.at(k, lambda chunk: self.hop_e(chunk).start())


class Sizes:
    def __init__(self, slots, width, share, hidden, attn):
        self.slots, self.width, self.share = slots, width, share
        self.hidden, self.attn = hidden, attn
        self.peers = width // share
        self.pairs = attn // PAIR
        self.tile = (min(512, attn), min(512, attn))
        shapes = [
            (hidden, width), (width, hidden), (width, hidden),
            (attn, width), (width, attn), (width, attn), (width, attn),
        ]
        self.shapes = shapes
        self.plan = []
        first = 0
        for rows, cols in shapes:
            across = cols // self.tile[1]
            count = (rows // self.tile[0]) * across
            self.plan.append((first, count, across))
            first += count
        self.total = first
        self.block_units = share // UNIT
        self.act_unit = min(512, hidden)


def partner(me, away, peers):
    place, found = 1, 0
    while place < peers:
        found += lax.rem(me // place + away // place, 2) * place
        place *= 2
    return found


def forward_kernel(sz, *refs):
    (
        tokens_h, w_query_h, w_key_h, w_value_h, w_out_h, w_gate_h, w_up_h,
        cosine, sine, seq_col, seq_row, gain_attn, gain_mlp,
        normed_h, qkv_h, mixed_h, log_h, resid_h, normed_mlp_h, hidden_h, silu_h, slope_h, stats_h,
        rows_in, w_qkv, w_out, w_mlp, normed, qkv, mixed, part, recv, resid, acts,
        log_total, row_stats, bias, load_sems, tensor_sems, out_sems, act_sems,
    ) = refs
    slots, width, share, peers, attn = sz.slots, sz.width, sz.share, sz.peers, sz.attn
    dp, me = lax.axis_index("dp"), lax.axis_index("tensor")
    chunks = slots // UNIT
    others = [partner(me, away, peers) for away in range(1, peers)]

    def rows_of(c):
        return pl.ds(c * UNIT, UNIT)

    def remote(kind, c, away, src, dst):
        return pltpu.make_async_remote_copy(
            src_ref=src, dst_ref=dst, send_sem=tensor_sems.at[2 * kind, c, away],
            recv_sem=tensor_sems.at[2 * kind + 1, c, away],
            device_id=(dp, others[away - 1]), device_id_type=MESH,
        )

    def send_tokens(c, away):
        return remote(0, c, away, tokens_h.at[rows_of(c), :], rows_in.at[me, rows_of(c), :])

    def scatter(c, away):
        return remote(
            1, c, away, part.at[others[away - 1], rows_of(c), :], recv.at[away - 1, rows_of(c), :]
        )

    def spread(c, away):
        block = rows_in.at[me, rows_of(c), :]
        return remote(2, c, away, block, block)

    def load(src, dst, index):
        return pltpu.make_async_copy(src, dst, load_sems.at[index])

    def out_copy(src, dst, index, c):
        return pltpu.make_async_copy(src, dst, out_sems.at[index, c])

    away_order = range(peers - 1, 0, -1)
    barrier = pltpu.get_barrier_semaphore()
    own_load = load(tokens_h, rows_in.at[me], 0)
    own_load.start()
    for other in others:
        pl.semaphore_signal(barrier, inc=1, device_id=(dp, other), device_id_type=MESH)
    weight_loads = [
        load(ref, w_qkv.at[i], 1 + i) for i, ref in enumerate((w_query_h, w_key_h, w_value_h))
    ] + [load(w_out_h, w_out, 4), load(w_gate_h, w_mlp.at[0], 5), load(w_up_h, w_mlp.at[1], 6)]
    for one in weight_loads:
        one.start()
    pl.semaphore_wait(barrier, peers - 1)
    for c in range(chunks):
        for away in away_order:
            send_tokens(c, away).start()

    outs = {}

    def write(src, dst, index, c):
        outs[index, c] = out_copy(src, dst, index, c)
        outs[index, c].start()

    def project(c):
        rows = rows_of(c)
        for away in away_order:
            send_tokens(c, away).wait()
        if c == 0:
            own_load.wait()
            for one in weight_loads[:3]:
                one.wait()
        squares = jnp.zeros((UNIT, 1), jnp.float32)
        for b in range(peers):
            squares += jnp.sum(
                jnp.square(rows_in[b, rows, :].astype(jnp.float32)), axis=1, keepdims=True
            )
        rms = lax.rsqrt(squares / width + EPSILON)
        row_stats[rows, 1:2] = rms
        for b in range(peers):
            at = pl.ds(b * share, share)
            normed[rows, at] = (
                rows_in[b, rows, :].astype(jnp.float32) * rms * gain_attn[0:1, at]
            ).astype(jnp.bfloat16)
        write(normed.at[rows, :], normed_h.at[rows, :], 0, c)
        for i in range(3):
            found = matmul(normed[rows, :], w_qkv[i])
            if i < 2:
                for p in range(sz.pairs):
                    lanes = found[:, p * PAIR : (p + 1) * PAIR]
                    qkv[i, rows, pl.ds(p * PAIR, PAIR)] = (
                        lanes * cosine[rows, :] + swap_halves(lanes) * sine[rows, :]
                    ).astype(jnp.bfloat16)
            else:
                qkv[i, rows, :] = found.astype(jnp.bfloat16)
            write(qkv.at[i, rows, :], qkv_h.at[i, rows, :], 1 + i, c)

    def attend(c):
        rows = rows_of(c)
        keys = (c + 1) * UNIT
        key_slot = lax.broadcasted_iota(jnp.int32, (keys, UNIT), 0)
        query_slot = lax.broadcasted_iota(jnp.int32, (keys, UNIT), 1) + c * UNIT
        allowed = (seq_col[pl.ds(0, keys), 0:1] == seq_row[0:1, rows]) & (key_slot <= query_slot)
        bias[pl.ds(0, keys), :] = jnp.where(allowed, 0.0, MASKED)

        @pl.loop(0, sz.pairs)
        def _(p):
            mine = span(p * PAIR, PAIR)
            query = qkv[0, rows, mine]
            key = qkv[1, pl.ds(0, keys), mine]
            value = qkv[2, pl.ds(0, keys), mine]
            first_head = lax.broadcasted_iota(jnp.int32, (1, PAIR), 1) < HDIM
            found = []
            for h in range(2):
                chosen = first_head if h == 0 else jnp.logical_not(first_head)
                scores = matmul_last(key, jnp.where(chosen, query, 0.0)) * SCALE
                scores += bias[pl.ds(0, keys), :]
                peak = jnp.max(scores, axis=0, keepdims=True)
                expon = jnp.exp(scores - peak)
                total = jnp.sum(expon, axis=0, keepdims=True)
                log_total[pl.ds(2 * p + h, 1), rows] = peak + jnp.log(total)
                weights = (expon * (1.0 / total)).astype(jnp.bfloat16)
                found.append(matmul_first(weights, value))
            mixed[rows, mine] = jnp.where(first_head, *found).astype(jnp.bfloat16)

        write(mixed.at[rows, :], mixed_h.at[rows, :], 4, c)

    def project_out(c):
        rows = rows_of(c)
        if c == 0:
            weight_loads[3].wait()

        def block(b):
            part[b, rows, :] = matmul(
                mixed[rows, :], w_out[:, span(b * share, share)]
            ).astype(jnp.bfloat16)

        for away in away_order:
            block(others[away - 1])
            scatter(c, away).start()
        resid[rows, :] = rows_in[me, rows, :].astype(jnp.float32) + matmul(
            mixed[rows, :], w_out[:, span(me * share, share)]
        )

    def residual(c):
        rows = rows_of(c)
        for away in away_order:
            scatter(c, away).wait()
        total = resid[rows, :]
        for away in away_order:
            total += recv[away - 1, rows, :].astype(jnp.float32)
        resid[rows, :] = total
        write(resid.at[rows, :], resid_h.at[rows, :], 5, c)
        rows_in[me, rows, :] = total.astype(jnp.bfloat16)
        for away in away_order:
            spread(c, away).start()

    def act_copies(slot, c, u):
        at = pl.ds(u * sz.act_unit, sz.act_unit)
        return [
            pltpu.make_async_copy(
                acts.at[slot, i], ref.at[rows_of(c), at], act_sems.at[slot, i]
            )
            for i, ref in enumerate((hidden_h, silu_h, slope_h))
        ]

    act_units = sz.hidden // sz.act_unit
    pending = {}

    def feed(c):
        rows = rows_of(c)
        for away in away_order:
            spread(c, away).wait()
        if c == 0:
            for one in weight_loads[4:]:
                one.wait()
        squares = jnp.zeros((UNIT, 1), jnp.float32)
        for b in range(peers):
            squares += jnp.sum(
                jnp.square(rows_in[b, rows, :].astype(jnp.float32)), axis=1, keepdims=True
            )
        rms = lax.rsqrt(squares / width + EPSILON)
        row_stats[rows, 0:1] = rms
        outs.pop((0, c)).wait()
        for b in range(peers):
            at = pl.ds(b * share, share)
            normed[rows, at] = (
                rows_in[b, rows, :].astype(jnp.float32) * rms * gain_mlp[0:1, at]
            ).astype(jnp.bfloat16)
        write(normed.at[rows, :], normed_mlp_h.at[rows, :], 6, c)
        for u in range(act_units):
            slot = (c * act_units + u) % 2
            for one in pending.pop(slot, []):
                one.wait()
            at = pl.ds(u * sz.act_unit, sz.act_unit)
            gate = matmul(normed[rows, :], w_mlp[0, :, at])
            upward = matmul(normed[rows, :], w_mlp[1, :, at])
            sigmoid = 1.0 / (1.0 + jnp.exp(-gate))
            silu = gate * sigmoid
            acts[slot, 0] = (silu * upward).astype(jnp.bfloat16)
            acts[slot, 1] = silu.astype(jnp.bfloat16)
            acts[slot, 2] = (upward * sigmoid * (1.0 + gate * (1.0 - sigmoid))).astype(jnp.bfloat16)
            pending[slot] = act_copies(slot, c, u)
            for one in pending[slot]:
                one.start()

    log_total[...] = jnp.zeros_like(log_total)
    row_stats[...] = seq_col[...]
    for c in range(chunks):
        project(c)
        attend(c)
        project_out(c)
        if c >= 2:
            residual(c - 2)
    for c in range(max(chunks - 2, 0), chunks):
        residual(c)
    for c in range(chunks):
        feed(c)
    write(log_total, log_h, 7, 0)
    write(row_stats, stats_h, 7, 1)
    for slot in list(pending):
        for one in pending.pop(slot):
            one.wait()
    for one in outs.values():
        one.wait()


def forward(sz, big, small):
    slots, width, share, attn, hidden = sz.slots, sz.width, sz.share, sz.attn, sz.hidden
    chunks = slots // UNIT
    bf16, f32 = jnp.bfloat16, jnp.float32
    shapes = [
        ((slots, width), bf16), ((3, slots, attn), bf16), ((slots, attn), bf16), ((8, slots), f32),
        ((slots, share), f32), ((slots, width), bf16), ((slots, hidden), bf16),
        ((slots, hidden), bf16), ((slots, hidden), bf16), ((slots, PAIR), f32),
    ]
    flops = 2 * slots * (4 * width * attn + 2 * width * hidden)
    return pl.pallas_call(
        functools.partial(forward_kernel, sz),
        out_shape=[jax.ShapeDtypeStruct(*s) for s in shapes],
        in_specs=[pl.BlockSpec(memory_space=pl.ANY)] * len(big)
        + [pl.BlockSpec(memory_space=pltpu.VMEM)] * len(small),
        out_specs=[pl.BlockSpec(memory_space=pl.ANY)] * len(shapes),
        scratch_shapes=[
            pltpu.VMEM((sz.peers, slots, share), bf16),
            pltpu.VMEM((3, width, attn), bf16),
            pltpu.VMEM((attn, width), bf16),
            pltpu.VMEM((2, width, hidden), bf16),
            pltpu.VMEM((slots, width), bf16),
            pltpu.VMEM((3, slots, attn), bf16),
            pltpu.VMEM((slots, attn), bf16),
            pltpu.VMEM((sz.peers, slots, share), bf16),
            pltpu.VMEM((sz.peers - 1, slots, share), bf16),
            pltpu.VMEM((slots, share), f32),
            pltpu.VMEM((2, 3, UNIT, sz.act_unit), bf16),
            pltpu.VMEM((8, slots), f32),
            pltpu.VMEM((slots, PAIR), f32),
            pltpu.VMEM((slots, UNIT), f32),
            pltpu.SemaphoreType.DMA((7,)),
            pltpu.SemaphoreType.DMA((6, chunks, sz.peers)),
            pltpu.SemaphoreType.DMA((8, chunks)),
            pltpu.SemaphoreType.DMA((2, 3)),
        ],
        compiler_params=pltpu.CompilerParams(
            collective_id=1, has_side_effects=True, vmem_limit_bytes=63 * MIB
        ),
        cost_estimate=pl.CostEstimate(
            flops=flops, bytes_accessed=60 * MIB, transcendentals=slots * slots * 8
        ),
    )(*big, *small)


def backward_kernel(sz, *refs):
    (
        hidden_h, silu_h, slope_h, cot_h, normed_mlp_h, mixed_h, normed_h, qkv_h,
        w_down_h, w_gate_h, w_up_h, w_out_h, w_query_h, w_key_h, w_value_h,
        resid_h, cosine, sine, seq_row, log_total, row_stats, gain_attn, gain_mlp,
        *refs,
    ) = refs
    outs, (grad_tokens_h, out_tokens_h, gains_h), refs = refs[:7], refs[7:10], refs[10:]
    (
        buf_a, buf_b, buf_c, d_gate, d_up, send, full, recv, d_mixed, d_qkv, w_buf, w_cols,
        acc_key, acc_value, row_part, row_send, row_recv, gains, gains_out,
        load_sems, w_sems, tensor_sems, gain_sems, *line_scratch,
    ) = refs
    slots, width, share, peers = sz.slots, sz.width, sz.share, sz.peers
    n_dp = lax.axis_size("dp")
    dp, me = lax.axis_index("dp"), lax.axis_index("tensor")
    tile_rows, tile_cols = sz.tile
    assert tile_cols == share

    def place_of(m):
        across, down = sz.plan[m][2], sz.shapes[m][0] // tile_rows
        if m == 0:
            return lambda i: (lax.rem(i, down), partner(me, i // down, peers))
        return lambda i: (i // across, lax.rem(i, across))

    places = [place_of(m) for m in range(len(sz.plan))]
    line = LineSum(
        sz.total, [(ref, plan[0], plan[1], at) for ref, plan, at in zip(outs, sz.plan, places)],
        sz.tile, line_scratch,
    )

    def load(src, dst, index):
        return pltpu.make_async_copy(src, dst, load_sems.at[index])

    def peer(away):
        return partner(me, away, peers)

    def other_dp(away):
        return lax.rem(dp + away, n_dp)

    barrier = pltpu.get_barrier_semaphore()
    own = span(me * share, share)
    first_loads = [
        load(hidden_h, buf_a.at[:, pl.ds(0, sz.hidden)], 0), load(cot_h, buf_b.at[:, own], 1),
        load(normed_mlp_h, buf_c, 2),
    ]
    for one in first_loads:
        one.start()

    def remote(kind, away, src, dst):
        return pltpu.make_async_remote_copy(
            src_ref=src, dst_ref=dst, send_sem=tensor_sems.at[2 * kind, away],
            recv_sem=tensor_sems.at[2 * kind + 1, away],
            device_id=(dp, peer(away)), device_id_type=MESH,
        )

    def send_cot(away):
        return remote(4, away, cot_h, buf_b.at[:, own])
    for away in range(1, n_dp):
        pl.semaphore_signal(
            barrier, inc=1, device_id=(other_dp(away), me), device_id_type=MESH
        )
    for away in range(1, peers):
        pl.semaphore_signal(barrier, inc=1, device_id=(dp, peer(away)), device_id_type=MESH)
    pl.semaphore_wait(barrier, n_dp - 1 + peers - 1)
    for away in range(1, peers):
        send_cot(away).start()

    attn_at = [pl.ds(i * sz.attn, sz.attn) for i in range(4)]
    grads = [
        (lambda r: buf_a[:, r], lambda c: buf_b[:, c]),
        (lambda r: buf_c[:, r], lambda c: d_gate[:, c]),
        (lambda r: buf_c[:, r], lambda c: d_up[:, c]),
        (lambda r: d_gate[:, pl.ds(pl.multiple_of(3 * sz.attn + r.start, tile_rows), tile_rows)],
         lambda c: buf_a[:, c]),
        (lambda r: buf_b[:, r], lambda c: d_qkv[2, :, c]),
        (lambda r: buf_b[:, r], lambda c: d_qkv[0, :, c]),
        (lambda r: buf_b[:, r], lambda c: d_qkv[1, :, c]),
    ]

    def cot_at(away):
        last = sz.plan[1][0] - sz.hidden // UNIT // 2 - 1
        return min(away * (sz.shapes[0][0] // tile_rows), last)

    def tile_tick(m, k):
        row, col = places[m](k - sz.plan[m][0])
        rows, cols = span(row * tile_rows, tile_rows), span(col * tile_cols, tile_cols)
        if m == 0:
            for away in range(1, peers):
                @pl.when(k == cot_at(away))
                def _(away=away):
                    send_cot(away).wait()
        left, right = grads[m]
        line.put(k, matmul_first(left(rows), right(cols)))
        line.tick(k)

    cursor = [0]

    def matrix_of(k):
        return [m for m, (first, count, _) in enumerate(sz.plan) if first <= k < first + count][0]

    def advance_to(stop):
        while cursor[0] < stop:
            m = matrix_of(cursor[0])
            until = min(stop, sz.plan[m][0] + sz.plan[m][1])

            @pl.loop(cursor[0], until)
            def _(k, m=m):
                tile_tick(m, k)

            cursor[0] = until

    def run_units(count, unit, group=1):
        done = 0
        while done < count:
            m = matrix_of(cursor[0])
            room = (sz.plan[m][0] + sz.plan[m][1] - cursor[0]) // group
            if not room:
                for g in range(group):
                    unit(done, g)
                    tile_tick(matrix_of(cursor[0]), cursor[0])
                    cursor[0] += 1
                done += 1
                continue
            step = min(room, count - done)

            @pl.loop(0, step)
            def _(i, m=m, done=done, start=cursor[0]):
                for g in range(group):
                    unit(done + i, g)
                    tile_tick(m, start + i * group + g)

            cursor[0] += step * group
            done += step

    order = list(range(peers - 1, 0, -1)) + [0]

    def block_of(u):
        return partner(me, peers - 1 - u // sz.block_units, peers)

    def feature(u):
        return block_of(u) * share + lax.rem(u, sz.block_units) * UNIT

    def scatter(round_, away):
        dst = full.at[me] if round_ == 2 else recv.at[away - 1]
        return remote(round_, away, send.at[peer(away)], dst)

    def store_part(round_, u, value):
        send[block_of(u), :, span(lax.rem(u, sz.block_units) * UNIT, UNIT)] = value.astype(
            jnp.bfloat16
        )
        for i, away in enumerate(order[:-1] if round_ != 1 else ()):
            @pl.when(u == (i + 1) * sz.block_units - 1)
            def _(away=away):
                scatter(round_, away).start()

    mlp_units = width // UNIT
    hid = pl.ds(0, sz.hidden)

    def prefetched(count, loads, u):
        for one in loads(u):
            one.wait()

        @pl.when(u + 1 < count)
        def _():
            for one in loads(u + 1):
                one.start()

    def hidden_loads(u):
        cols = span(u * UNIT, UNIT)
        slot = lax.rem(u, 2)
        return (
            pltpu.make_async_copy(w_down_h.at[cols, :], w_buf.at[slot, 0], w_sems.at[0, slot]),
            pltpu.make_async_copy(
                silu_h.at[:, cols], d_qkv.at[slot, :, pl.ds(0, UNIT)], w_sems.at[1, slot]
            ),
            pltpu.make_async_copy(
                slope_h.at[:, cols], d_qkv.at[slot, :, pl.ds(UNIT, UNIT)], w_sems.at[2, slot]
            ),
        )

    def hidden_unit(u, _):
        prefetched(sz.hidden // UNIT, hidden_loads, u)
        slot = lax.rem(u, 2)
        cols = span(u * UNIT, UNIT)
        d_hidden = matmul_last(buf_b[...], w_buf[slot, 0])
        d_up[:, cols] = (d_hidden * d_qkv[slot, :, pl.ds(0, UNIT)]).astype(jnp.bfloat16)
        d_gate[:, cols] = (d_hidden * d_qkv[slot, :, pl.ds(UNIT, UNIT)]).astype(jnp.bfloat16)

    def twice(unit):
        def both(u, g):
            unit(2 * u, g)
            unit(2 * u + 1, g)

        return both

    for one in hidden_loads(0):
        one.start()
    for one in first_loads:
        one.wait()
    advance_to(sz.plan[1][0] - sz.hidden // UNIT // 2)
    run_units(sz.hidden // UNIT // 2, twice(hidden_unit))

    def gather(round_):
        for away in range(1, peers):
            scatter(round_, away).wait()

    def gathered(round_, rows):
        total = send[me, rows, :].astype(jnp.float32)
        for away in range(1, peers):
            block = full[peer(away), rows, :] if round_ == 2 else recv[away - 1, rows, :]
            total += block.astype(jnp.float32)
        return total

    def mlp_loads(u):
        slot = lax.rem(u, 2)
        rows = span(feature(u), UNIT)
        return (
            pltpu.make_async_copy(
                w_gate_h.at[rows, :], w_buf.at[slot, 0, :, hid], w_sems.at[0, slot]
            ),
            pltpu.make_async_copy(
                w_up_h.at[rows, :], w_buf.at[slot, 1, :, hid], w_sems.at[1, slot]
            ),
        )

    def mlp_unit(u, _):
        prefetched(mlp_units, mlp_loads, u)
        slot = lax.rem(u, 2)
        part = matmul_last(d_gate[...], w_buf[slot, 0, :, hid])
        part += matmul_last(d_up[...], w_buf[slot, 1, :, hid])
        store_part(0, u, part)

    for one in mlp_loads(0):
        one.start()
    run_units(mlp_units, mlp_unit)
    advance_to(cursor[0] + 4)

    def spread(away):
        return remote(3, away, full.at[me], full.at[me])

    w_out_rows = sz.attn // UNIT
    w_out_loads = [
        load(w_out_h.at[pl.ds(i * UNIT, UNIT), :], w_buf.at[0, i], 3 + i) for i in range(w_out_rows)
    ]
    for one in w_out_loads:
        one.start()
    gather(0)

    @pl.loop(0, slots // UNIT)
    def _(i):
        full[me, span(i * UNIT, UNIT), :] = gathered(0, span(i * UNIT, UNIT)).astype(jnp.bfloat16)

    for away in range(1, peers):
        spread(away).start()
    advance_to(sz.plan[2][0])

    hidden_load = load(hidden_h, d_gate, 0)
    hidden_load.start()

    def out_loads(u):
        slot = lax.rem(u, 2)
        return [
            pltpu.make_async_copy(
                w_down_h.at[:, span(feature(u), UNIT)], w_cols.at[slot], w_sems.at[0, slot]
            )
        ]

    def out_unit(u, _):
        prefetched(mlp_units, out_loads, u)
        store_part(1, u, matmul(d_gate[...], w_cols[lax.rem(u, 2)]))

    for one in out_loads(0):
        one.start()
    hidden_load.wait()
    run_units(mlp_units // 2, twice(out_unit))

    for away in range(1, peers):
        spread(away).wait()
    for one in w_out_loads:
        one.wait()

    gains[dp] = jnp.zeros_like(gains[dp])

    def norm_unit(u, _):
        rows = span(u * UNIT, UNIT)
        row_sum = jnp.zeros((UNIT, 1), jnp.float32)
        for b in range(peers):
            at = pl.ds(b * share, share)
            row_sum += jnp.sum(
                full[b, rows, :].astype(jnp.float32) * buf_c[rows, at].astype(jnp.float32),
                axis=1, keepdims=True,
            )
        rms = row_stats[rows, 0:1]
        for b in range(peers):
            at = pl.ds(b * share, share)
            gain = gain_mlp[0:1, at]
            lean = buf_c[rows, at].astype(jnp.float32) / gain * (row_sum / width)
            d_resid = buf_b[rows, at].astype(jnp.float32) + rms * (
                gain * full[b, rows, :].astype(jnp.float32) - lean
            )
            buf_a[rows, at] = d_resid.astype(jnp.bfloat16)
        gains[dp, 0:1, :] += jnp.sum(
            full[me, rows, :].astype(jnp.float32) * buf_c[rows, own].astype(jnp.float32),
            axis=0, keepdims=True,
        ) / gain_mlp[0:1, own]
        for i in range(w_out_rows):
            d_mixed[rows, pl.ds(i * UNIT, UNIT)] = matmul_last(
                buf_a[rows, :], w_buf[0, i]
            ).astype(jnp.bfloat16)

    run_units(slots // UNIT, norm_unit)
    for away in range(1, peers):
        scatter(1, away).start()

    attn_loads = [
        load(ref, d_gate.at[:, attn_at[i]], 5 + i)
        for i, ref in enumerate((qkv_h.at[0], qkv_h.at[1], qkv_h.at[2], mixed_h))
    ] + [load(normed_h, buf_b, 9)]
    for one in attn_loads:
        one.start()
    for one in attn_loads:
        one.wait()
    blocks = slots // UNIT

    def attend_unit(p, i):
        rows = pl.ds(i * UNIT, UNIT)
        keys = (i + 1) * UNIT
        lanes = [pl.ds(pl.multiple_of(j * sz.attn + p * PAIR, PAIR), PAIR) for j in range(3)]
        mine = span(p * PAIR, PAIR)
        query = d_gate[rows, lanes[0]]
        key = d_gate[pl.ds(0, keys), lanes[1]]
        value = d_gate[pl.ds(0, keys), lanes[2]]
        grad = d_mixed[rows, mine]
        first_head = lax.broadcasted_iota(jnp.int32, (1, PAIR), 1) < HDIM
        key_slot = lax.broadcasted_iota(jnp.int32, (keys, UNIT), 0)
        query_slot = lax.broadcasted_iota(jnp.int32, (keys, UNIT), 1) + i * UNIT
        allowed = (row_stats[pl.ds(0, keys), 2:3] == seq_row[0:1, rows]) & (key_slot <= query_slot)
        found = []
        for h in range(2):
            chosen = first_head if h == 0 else jnp.logical_not(first_head)
            scores = matmul_last(key, jnp.where(chosen, query, 0.0)) * SCALE
            scores -= log_total[pl.ds(2 * p + h, 1), rows]
            probs = jnp.exp(jnp.where(allowed, scores, MASKED))
            grad_probs = matmul_last(value, jnp.where(chosen, grad, 0.0))
            delta = jnp.sum(probs * grad_probs, axis=0, keepdims=True)
            grad_scores = (probs * (grad_probs - delta)).astype(jnp.bfloat16)
            found.append(
                (
                    matmul_first(grad_scores, key),
                    matmul(grad_scores, query),
                    matmul(probs.astype(jnp.bfloat16), grad),
                )
            )
        grad_query, grad_key, grad_value = [
            jnp.where(first_head, one, two) for one, two in zip(*found)
        ]
        d_qkv[0, rows, mine] = rotate_back(
            grad_query * SCALE, cosine[rows, :], sine[rows, :]
        ).astype(jnp.bfloat16)
        for acc, part in ((acc_key, grad_key), (acc_value, grad_value)):
            if i > 0:
                acc[pl.ds(0, keys - UNIT), :] += part[: keys - UNIT]
            acc[pl.ds(keys - UNIT, UNIT), :] = part[keys - UNIT :]
        if i + 1 == blocks:
            d_qkv[1, :, mine] = rotate_back(acc_key[...] * SCALE, cosine[...], sine[...]).astype(
                jnp.bfloat16
            )
            d_qkv[2, :, mine] = acc_value[...].astype(jnp.bfloat16)

    steps = [(0, 1), (2,), (3,)] if blocks == 4 else [(i,) for i in range(blocks)]

    def attend_step(p, g):
        for i in steps[g]:
            attend_unit(p, i)

    run_units(sz.pairs, attend_step, len(steps))
    advance_to(sz.plan[4][0])

    gather(1)
    for j in range(share // PAIR):
        lanes = pl.ds(j * PAIR, PAIR)
        piece = load(resid_h.at[:, lanes], acc_key, 2)
        piece.start()
        piece.wait()

        @pl.loop(0, slots // UNIT)
        def _(i, lanes=lanes):
            rows = span(i * UNIT, UNIT)
            total = acc_key[rows, :] + send[me, rows, lanes].astype(jnp.float32)
            for away in range(1, peers):
                total += recv[away - 1, rows, lanes].astype(jnp.float32)
            send[me, rows, lanes] = total.astype(jnp.bfloat16)

    tokens_out = load(send.at[me], out_tokens_h, 0)
    tokens_out.start()

    row_part[...] = jnp.zeros_like(row_part)

    def attn_loads_of(u):
        slot = lax.rem(u, 2)
        rows = span(feature(u), UNIT)
        return [
            pltpu.make_async_copy(ref.at[rows, :], w_buf.at[slot, 0, :, at], w_sems.at[i, slot])
            for i, (ref, at) in enumerate(zip((w_query_h, w_key_h, w_value_h), attn_at))
        ]

    def attn_unit(u, _):
        prefetched(mlp_units, attn_loads_of, u)
        slot = lax.rem(u, 2)
        part = jnp.zeros((slots, UNIT), jnp.float32)
        for i in range(3):
            part += matmul_last(d_qkv[i, :, pl.ds(0, sz.attn)], w_buf[slot, 0, :, attn_at[i]])
        store_part(2, u, part)
        row_part[...] += jnp.sum(
            part * buf_b[:, span(feature(u), UNIT)].astype(jnp.float32), axis=1, keepdims=True
        )

    def row_scatter(away):
        return remote(5, away, row_send, row_recv.at[away - 1])

    for one in attn_loads_of(0):
        one.start()

    tokens_out.wait()
    run_units(mlp_units // 2, twice(attn_unit))
    row_send[...] = row_part[...].T[0:8, :]
    for away in range(1, peers):
        row_scatter(away).start()
    advance_to(sz.total)

    @pl.loop(sz.total, sz.total + 3)
    def _(k):
        line.tick(k)

    for away in range(1, peers):
        row_scatter(away).wait()
    row_sums = row_send[...]
    for away in range(1, peers):
        row_sums += row_recv[away - 1]
    row_part[...] = jnp.concatenate([row_sums] * (row_part.shape[1] // 8), axis=0).T
    gather(2)
    gain = gain_attn[0:1, own]

    @pl.loop(0, slots // UNIT)
    def _(i):
        rows = span(i * UNIT, UNIT)
        d_own = gathered(2, rows)
        straight = buf_b[rows, own].astype(jnp.float32)
        gains[dp, 1:2, :] += jnp.sum(d_own * straight, axis=0, keepdims=True) / gain
        lean = straight / gain * (row_part[rows, 0:1] / width)
        send[me, rows, :] = (
            buf_a[rows, own].astype(jnp.float32) + row_stats[rows, 1:2] * (gain * d_own - lean)
        ).astype(jnp.bfloat16)

    grad_out = load(send.at[me], grad_tokens_h, 10)
    grad_out.start()

    def gain_copy(away):
        return pltpu.make_async_remote_copy(
            src_ref=gains.at[dp], dst_ref=gains.at[dp],
            send_sem=gain_sems.at[0, away], recv_sem=gain_sems.at[1, away],
            device_id=(other_dp(away), me), device_id_type=MESH,
        )

    for away in range(1, n_dp):
        gain_copy(away).start()

    @pl.loop(sz.total + 3, sz.total + 6)
    def _(k):
        line.tick(k)

    for away in range(1, n_dp):
        gain_copy(away).wait()
    total = gains[0]
    for i in range(1, n_dp):
        total += gains[i]
    gains_out[...] = total
    gain_out = load(gains_out, gains_h, 11)
    gain_out.start()

    @pl.loop(sz.total + 6, sz.total + line.lag_d)
    def _(k):
        line.tick(k)

    grad_out.wait()
    gain_out.wait()


def backward(sz, big, small):
    whole_rows = pltpu.VMEM((sz.slots, sz.width), jnp.bfloat16)
    hidden_rows = pltpu.VMEM((sz.slots, sz.hidden), jnp.bfloat16)
    assert sz.hidden == 4 * sz.attn and sz.share % UNIT == 0 and sz.hidden <= sz.width
    n_dp = lax.axis_size("dp")
    attn_rows = max(sz.attn, 2 * UNIT)
    flops = 6 * sz.slots * (3 * sz.width * sz.hidden + 4 * sz.width * sz.attn)
    return pl.pallas_call(
        functools.partial(backward_kernel, sz),
        out_shape=[jax.ShapeDtypeStruct(s, jnp.bfloat16) for s in sz.shapes]
        + [
            jax.ShapeDtypeStruct((sz.slots, sz.share), jnp.bfloat16),
            jax.ShapeDtypeStruct((sz.slots, sz.share), jnp.bfloat16),
            jax.ShapeDtypeStruct((8, sz.share), jnp.float32),
        ],
        in_specs=[pl.BlockSpec(memory_space=pl.ANY)] * len(big)
        + [pl.BlockSpec(memory_space=pltpu.VMEM)] * len(small),
        out_specs=[pl.BlockSpec(memory_space=pl.ANY)] * 10,
        scratch_shapes=[
            whole_rows, whole_rows, whole_rows, hidden_rows, hidden_rows,
            pltpu.VMEM((sz.peers, sz.slots, sz.share), jnp.bfloat16),
            pltpu.VMEM((sz.peers, sz.slots, sz.share), jnp.bfloat16),
            pltpu.VMEM((sz.peers - 1, sz.slots, sz.share), jnp.bfloat16),
            pltpu.VMEM((sz.slots, sz.attn), jnp.bfloat16),
            pltpu.VMEM((3, sz.slots, attn_rows), jnp.bfloat16),
            pltpu.VMEM((2, 2, UNIT, sz.width), jnp.bfloat16),
            pltpu.VMEM((2, sz.hidden, UNIT), jnp.bfloat16),
            pltpu.VMEM((sz.slots, PAIR), jnp.float32),
            pltpu.VMEM((sz.slots, PAIR), jnp.float32),
            pltpu.VMEM((sz.slots, PAIR), jnp.float32),
            pltpu.VMEM((8, sz.slots), jnp.float32),
            pltpu.VMEM((sz.peers - 1, 8, sz.slots), jnp.float32),
            pltpu.VMEM((n_dp, 8, sz.share), jnp.float32),
            pltpu.VMEM((8, sz.share), jnp.float32),
            pltpu.SemaphoreType.DMA((12,)),
            pltpu.SemaphoreType.DMA((3, 2)),
            pltpu.SemaphoreType.DMA((12, sz.peers)),
            pltpu.SemaphoreType.DMA((2, n_dp)),
        ]
        + LineSum.scratch_shapes(sz.tile),
        compiler_params=pltpu.CompilerParams(
            collective_id=0, has_side_effects=True, vmem_limit_bytes=63 * MIB
        ),
        cost_estimate=pl.CostEstimate(
            flops=flops, bytes_accessed=200 * MIB, transcendentals=sz.slots * sz.slots * 8
        ),
    )(*big, *small)


def body(
    tokens,
    norm_gain_attn,
    norm_gain_mlp,
    w_query,
    w_key,
    w_value,
    w_out,
    w_gate,
    w_up,
    w_down,
    cotangent,
    lengths,
):
    slot_count = tokens.shape[0]
    share_width = tokens.shape[1]
    model_width = share_width * lax.axis_size("tensor")
    attn_width = w_query.shape[1]
    sz = Sizes(slot_count, model_width, share_width, w_gate.shape[1], attn_width)
    sequence, position = positions(lengths[0], slot_count)
    sequence = sequence.astype(jnp.float32)
    cos_lanes, sin_lanes = rotate_tables(position)
    seq_col = jnp.broadcast_to(sequence[:, None], (slot_count, PAIR))
    seq_row = jnp.broadcast_to(sequence[None, :], (8, slot_count))
    gain_attn = jnp.broadcast_to(norm_gain_attn[None, :], (8, model_width))
    gain_mlp = jnp.broadcast_to(norm_gain_mlp[None, :], (8, model_width))
    normed, qkv, mixed, log_total, resid_here, normed_mlp, hidden, silu, slope, row_stats = forward(
        sz,
        (tokens, w_query, w_key, w_value, w_out, w_gate, w_up),
        (cos_lanes, sin_lanes, seq_col, seq_row, gain_attn, gain_mlp),
    )
    down, gate, up, out, value, query, key, grad_tokens, out_tokens, gains = backward(
        sz,
        (
            hidden, silu, slope, cotangent, normed_mlp, mixed, normed, qkv,
            w_down, w_gate, w_up, w_out, w_query, w_key, w_value, resid_here,
        ),
        (cos_lanes, sin_lanes, seq_row, log_total, row_stats, gain_attn, gain_mlp),
    )

    def wide(values):
        return values.astype(jnp.float32)

    return (
        out_tokens,
        grad_tokens,
        gains[1],
        gains[0],
        wide(query),
        wide(key),
        wide(value),
        wide(out),
        wide(gate),
        wide(up),
        wide(down),
    )


def solution(mesh):
    placed = (
        P("dp", "tensor"),
        P(),
        P(),
        P(None, "tensor"),
        P(None, "tensor"),
        P(None, "tensor"),
        P("tensor", None),
        P(None, "tensor"),
        P(None, "tensor"),
        P("tensor", None),
        P("dp", "tensor"),
        P("dp", None),
    )
    return jax.shard_map(
        body,
        mesh=mesh,
        in_specs=placed,
        out_specs=(
            P("dp", "tensor"),
            P("dp", "tensor"),
            P("tensor"),
            P("tensor"),
            P(None, "tensor"),
            P(None, "tensor"),
            P(None, "tensor"),
            P("tensor", None),
            P(None, "tensor"),
            P(None, "tensor"),
            P("tensor", None),
        ),
        check_vma=False,
    )
```

```python
import functools
import math

import jax
import jax.numpy as jnp
from jax import lax
from jax.experimental import pallas as pl
from jax.experimental.pallas import tpu as pltpu
from jax.sharding import PartitionSpec as P

HDIM = 64
PAIR = 2 * HDIM


EPSILON = 1e-05
ROPE_BASE = 130000.0
SCALE = HDIM ** (-0.5)
MASKED = -1e30
MESH = pl.DeviceIdType.MESH
HOP_LAG = 2
UNIT = 256
MIB = 1024 * 1024


def matmul_first(left, right):
    return lax.dot_general(
        left, right, (((0,), (0,)), ((), ())), preferred_element_type=jnp.float32
    )


def matmul_last(left, right):
    return lax.dot_general(
        left, right, (((1,), (1,)), ((), ())), preferred_element_type=jnp.float32
    )


def matmul(left, right):
    return jnp.dot(left, right, preferred_element_type=jnp.float32)


def span(first, size):
    return pl.ds(pl.multiple_of(first, size), size)


def swap_halves(values):
    lane = lax.broadcasted_iota(jnp.int32, values.shape, 1)
    ahead = pltpu.roll(values, PAIR - HDIM // 2, 1)
    behind = pltpu.roll(values, HDIM // 2, 1)
    return jnp.where(lax.rem(lane, HDIM) < HDIM // 2, ahead, behind)


def rotate_back(values, cosine, sine):
    return values * cosine - swap_halves(values) * sine


class LineSum:
    SLOTS = (2, 2, 2, 6, 2, 4, 8, 3, 2, 4)

    def __init__(self, total, outs, tile, scratch):
        self.paired = lax.axis_size("dp") == 16
        assert lax.axis_size("dp") in (8, 16)
        self.lag_p = 1
        self.lag_a = 1 + HOP_LAG * self.paired
        self.lag_b = self.lag_a + HOP_LAG
        self.lag_c = self.lag_b + HOP_LAG
        self.lag_f = self.lag_c + HOP_LAG
        self.lag_o = self.lag_f + 1
        self.lag_d = self.lag_o + 1
        self.total = total
        self.outs = outs
        self.tile_rows, self.tile_cols = tile
        self.half = self.tile_rows // 2
        (
            self.stage, self.r_e, self.s_one, self.r_a, self.s_two, self.r_b, self.tot, self.r_f,
            self.s_zero, self.r_p, self.sems, self.out_sems,
        ) = scratch
        dp = lax.axis_index("dp")
        self.tensor = lax.axis_index("tensor")
        self.core = lax.rem(dp, 2)
        z = lax.rem(dp // 2, 4)
        self.is_end = (z == 0) | (z == 3)
        self.is_mid = jnp.logical_not(self.is_end)
        self.sibling = dp + 1 - 2 * self.core
        self.near = dp + jnp.where((z == 0) | (z == 2), 2, -2)
        self.across = dp + 6 - 4 * z
        self.twin = lax.rem(dp + 8, lax.axis_size("dp"))

    @classmethod
    def scratch_shapes(cls, tile):
        rows, cols = tile
        buffers = [
            pltpu.VMEM(
                (slots, 2, rows // 2, cols) if i == 0 else (slots, rows // 2, cols), jnp.bfloat16
            )
            for i, slots in enumerate(cls.SLOTS)
        ]
        if lax.axis_size("dp") != 16:
            buffers[8] = buffers[9] = pltpu.VMEM((1, 8, 128), jnp.bfloat16)
        return buffers + [pltpu.SemaphoreType.DMA((12, 8)), pltpu.SemaphoreType.DMA((2, 8))]

    def copy(self, hop, chunk, src, dst, target):
        slot = lax.rem(chunk, 8)
        return pltpu.make_async_remote_copy(
            src_ref=src, dst_ref=dst, send_sem=self.sems.at[2 * hop, slot],
            recv_sem=self.sems.at[2 * hop + 1, slot],
            device_id=(target, self.tensor), device_id_type=MESH,
        )

    @staticmethod
    def slot(ref, chunk):
        return ref.at[lax.rem(chunk, ref.shape[0])]

    def hop_e(self, chunk):
        src = self.stage.at[lax.rem(chunk, self.stage.shape[0]), 1 - self.core]
        return self.copy(0, chunk, src, self.slot(self.r_e, chunk), self.sibling)

    def hop_a(self, chunk):
        return self.copy(
            1, chunk, self.slot(self.s_one, chunk), self.slot(self.r_a, chunk), self.near
        )

    def hop_b(self, chunk):
        return self.copy(
            2, chunk, self.slot(self.s_two, chunk), self.slot(self.r_b, chunk), self.across
        )

    def hop_c(self, chunk):
        return self.copy(
            3, chunk, self.slot(self.tot, chunk), self.slot(self.tot, chunk), self.near
        )

    def hop_f(self, chunk):
        return self.copy(
            4, chunk, self.slot(self.tot, chunk), self.slot(self.r_f, chunk), self.sibling
        )

    def hop_p(self, chunk):
        return self.copy(
            5, chunk, self.slot(self.s_zero, chunk), self.slot(self.r_p, chunk), self.twin
        )

    def out_copies(self, chunk, ref, tile_row, tile_col):
        cols = span(tile_col * self.tile_cols, self.tile_cols)
        first = tile_row * self.tile_rows
        mine = span(first + self.core * self.half, self.half)
        other = span(first + (1 - self.core) * self.half, self.half)
        slot = lax.rem(chunk, 8)
        return (
            pltpu.make_async_copy(
                self.slot(self.tot, chunk), ref.at[mine, cols], self.out_sems.at[0, slot]
            ),
            pltpu.make_async_copy(
                self.slot(self.r_f, chunk), ref.at[other, cols], self.out_sems.at[1, slot]
            ),
        )

    def on_out(self, chunk, act):
        for ref, first, count, place in self.outs:
            local = chunk - first

            @pl.when((local >= 0) & (local < count))
            def _(ref=ref, local=local, place=place):
                for one in self.out_copies(chunk, ref, *place(local)):
                    act(one)

    def at(self, chunk, work):
        @pl.when((chunk >= 0) & (chunk < self.total))
        def _():
            work(chunk)

    def put(self, chunk, value):
        self.stage[lax.rem(chunk, self.stage.shape[0])] = value.astype(jnp.bfloat16).reshape(
            2, self.half, self.tile_cols
        )

    def add(self, into, left, right, chunk):
        total = self.slot(left, chunk)[...].astype(jnp.float32)
        total += self.slot(right, chunk)[...].astype(jnp.float32)
        self.slot(into, chunk)[...] = total.astype(jnp.bfloat16)

    def join_cores(self, into, chunk):
        self.hop_e(chunk).wait()
        total = self.stage[lax.rem(chunk, self.stage.shape[0]), self.core].astype(jnp.float32)
        total += self.slot(self.r_e, chunk)[...].astype(jnp.float32)
        self.slot(into, chunk)[...] = total.astype(jnp.bfloat16)

    def tick(self, k):
        def drop(chunk):
            self.on_out(chunk, lambda one: one.wait())

        def out(chunk):
            self.hop_f(chunk).wait()
            self.on_out(chunk, lambda one: one.start())

        def final(chunk):
            @pl.when(self.is_end)
            def _():
                self.hop_c(chunk).wait_recv()

            @pl.when(self.is_mid)
            def _():
                self.hop_c(chunk).wait_send()

            self.hop_f(chunk).start()

        def back(chunk):
            @pl.when(self.is_mid)
            def _():
                self.hop_b(chunk).wait()
                self.add(self.tot, self.s_two, self.r_b, chunk)
                self.hop_c(chunk).start()

        def across(chunk):
            @pl.when(self.is_mid)
            def _():
                self.hop_a(chunk).wait_recv()
                self.add(self.s_two, self.s_one, self.r_a, chunk)
                self.hop_b(chunk).start()

            @pl.when(self.is_end)
            def _():
                self.hop_a(chunk).wait_send()

        def inward(chunk):
            if self.paired:
                self.hop_p(chunk).wait()
                self.add(self.s_one, self.s_zero, self.r_p, chunk)
            else:
                self.join_cores(self.s_one, chunk)

            @pl.when(self.is_end)
            def _():
                self.hop_a(chunk).start()

        def pair(chunk):
            self.join_cores(self.s_zero, chunk)
            self.hop_p(chunk).start()

        self.at(k - self.lag_d, drop)
        self.at(k - self.lag_o, out)
        self.at(k - self.lag_f, final)
        self.at(k - self.lag_c, back)
        self.at(k - self.lag_b, across)
        self.at(k - self.lag_a, inward)
        if self.paired:
            self.at(k - self.lag_p, pair)
        self.at(k, lambda chunk: self.hop_e(chunk).start())


class Sizes:
    def __init__(self, slots, width, share, hidden, attn):
        self.slots, self.width, self.share = slots, width, share
        self.hidden, self.attn = hidden, attn
        self.peers = width // share
        self.pairs = attn // PAIR
        self.tile = (min(512, attn), min(512, attn))
        shapes = [
            (hidden, width), (width, hidden), (width, hidden),
            (attn, width), (width, attn), (width, attn), (width, attn),
        ]
        self.shapes = shapes
        self.plan = []
        first = 0
        for rows, cols in shapes:
            across = cols // self.tile[1]
            count = (rows // self.tile[0]) * across
            self.plan.append((first, count, across))
            first += count
        self.total = first
        self.block_units = share // UNIT
        self.act_unit = min(512, hidden)


def partner(me, away, peers):
    place, found = 1, 0
    while place < peers:
        found += lax.rem(me // place + away // place, 2) * place
        place *= 2
    return found


class Direct:
    KINDS = 3

    def __init__(self, sz, sems, tokens, rows_in, part, recv):
        self.peers, self.sems = sz.peers, sems
        self.dp, self.me = lax.axis_index("dp"), lax.axis_index("tensor")
        self.others = [partner(self.me, away, sz.peers) for away in range(sz.peers)]
        self.order = list(range(sz.peers - 1, 0, -1))
        self.tokens, self.rows_in, self.part, self.recv = tokens, rows_in, part, recv

    @staticmethod
    def scratch_shapes(sz):
        block = (sz.slots, sz.share)
        return [
            pltpu.VMEM((sz.peers - 1,) + block, jnp.bfloat16),
            pltpu.VMEM((sz.peers - 1,) + block, jnp.bfloat16),
        ]

    def remote(self, kind, c, away, src, dst):
        return pltpu.make_async_remote_copy(
            src_ref=src, dst_ref=dst, send_sem=self.sems.at[2 * kind, c, away],
            recv_sem=self.sems.at[2 * kind + 1, c, away],
            device_id=(self.dp, self.others[away]), device_id_type=MESH,
        )

    def rows(self, c):
        return pl.ds(c * UNIT, UNIT)

    def gather(self, kind, c, away):
        own = self.rows_in.at[self.me, self.rows(c), :]
        src = self.tokens.at[self.rows(c), :] if kind == 0 else own
        return self.remote(kind, c, away, src, own)

    def start(self, kind, c):
        for away in self.order:
            self.gather(kind, c, away).start()

    def forward(self, kind, c):
        pass

    def finish(self, kind, c):
        for away in self.order:
            self.gather(kind, c, away).wait()

    def scatter(self, c, away):
        rows = self.rows(c)
        return self.remote(
            2, c, away, self.part.at[away - 1, rows, :], self.recv.at[away - 1, rows, :]
        )

    def sum_start(self, c):
        for away in self.order:
            self.scatter(c, away).start()

    def sum_forward(self, c):
        pass

    def sum_finish(self, c):
        for away in self.order:
            self.scatter(c, away).wait()
        return sum(
            self.recv[away - 1, self.rows(c), :].astype(jnp.float32) for away in self.order
        )


class Relay(Direct):
    KINDS = 7

    @staticmethod
    def scratch_shapes(sz):
        block = (sz.slots, sz.share)
        return [
            pltpu.VMEM((3,) + block, jnp.bfloat16),
            pltpu.VMEM((3,) + block, jnp.bfloat16),
        ]

    def half(self, c, away):
        return pl.ds(c * UNIT + (away - 1) * (UNIT // 2), UNIT // 2)

    def relayed(self, kind, c, away):
        rows = self.half(c, away)
        block = self.rows_in.at[self.others[3 - away], rows, :]
        return self.remote(3 + kind, c, away, block, block)

    def start(self, kind, c):
        for away in (1, 2):
            self.gather(kind, c, away).start()

    def forward(self, kind, c):
        for away in (1, 2):
            self.gather(kind, c, away).wait_recv()
        for away in (1, 2):
            self.relayed(kind, c, away).start()

    def finish(self, kind, c):
        for away in (1, 2):
            self.gather(kind, c, away).wait_send()
            self.relayed(kind, c, away).wait()

    def first(self, c, away):
        rows = self.half(c, away)
        return [
            self.remote(2, c, away, self.part.at[away - 1, rows, :], self.recv.at[0, rows, :]),
            self.remote(5, c, away, self.part.at[2, rows, :], self.recv.at[1, rows, :]),
        ]

    def second(self, c, away):
        rows = self.half(c, 3 - away)
        return self.remote(6, c, away, self.part.at[away - 1, rows, :], self.recv.at[2, rows, :])

    def sum_start(self, c):
        for away in (1, 2):
            for one in self.first(c, away):
                one.start()

    def sum_forward(self, c):
        for away in (1, 2):
            for one in self.first(c, away):
                one.wait()
        for away in (1, 2):
            rows = self.half(c, 3 - away)
            total = self.part[away - 1, rows, :].astype(jnp.float32)
            total += self.recv[1, rows, :].astype(jnp.float32)
            self.part[away - 1, rows, :] = total.astype(jnp.bfloat16)
            self.second(c, away).start()

    def sum_finish(self, c):
        for away in (1, 2):
            self.second(c, away).wait()
        rows = self.rows(c)
        return self.recv[0, rows, :].astype(jnp.float32) + self.recv[2, rows, :].astype(jnp.float32)


def exchange_of(sz):
    return Relay if sz.peers == 4 else Direct


def forward_kernel(sz, *refs):
    (
        tokens_h, w_query_h, w_key_h, w_value_h, w_out_h, w_gate_h, w_up_h,
        lengths, gain_attn, gain_mlp,
        normed_h, qkv_h, mixed_h, log_h, resid_h, normed_mlp_h, hidden_h, silu_h, slope_h, stats_h,
        cosine_h, sine_h, seq_row_h,
        rows_in, w_qkv, w_out, w_mlp, normed, qkv, mixed, part, recv, resid, acts,
        log_total, row_stats, bias, cosine, sine, seq_row, load_sems, tensor_sems, out_sems, act_sems,
    ) = refs
    slots, width, share, peers, attn = sz.slots, sz.width, sz.share, sz.peers, sz.attn
    dp, me = lax.axis_index("dp"), lax.axis_index("tensor")
    chunks = slots // UNIT
    exchange = exchange_of(sz)(sz, tensor_sems, tokens_h, rows_in, part, recv)

    def rows_of(c):
        return pl.ds(c * UNIT, UNIT)

    def load(src, dst, index):
        return pltpu.make_async_copy(src, dst, load_sems.at[index])

    def out_copy(src, dst, index, c):
        return pltpu.make_async_copy(src, dst, out_sems.at[index, c])

    barrier = pltpu.get_barrier_semaphore()
    own_load = load(tokens_h, rows_in.at[me], 0)
    own_load.start()
    for other in exchange.others[1:]:
        pl.semaphore_signal(barrier, inc=1, device_id=(dp, other), device_id_type=MESH)
    weight_loads = [
        load(ref, w_qkv.at[i], 1 + i) for i, ref in enumerate((w_query_h, w_key_h, w_value_h))
    ] + [load(w_out_h, w_out, 4), load(w_gate_h, w_mlp.at[0], 5), load(w_up_h, w_mlp.at[1], 6)]
    for one in weight_loads:
        one.start()
    pl.semaphore_wait(barrier, peers - 1)
    for c in range(min(2, chunks)):
        exchange.start(0, c)

    outs = {}

    def write(src, dst, index, c):
        outs[index, c] = out_copy(src, dst, index, c)
        outs[index, c].start()

    def project(c):
        rows = rows_of(c)
        exchange.finish(0, c)
        if c == 0:
            own_load.wait()
            for one in weight_loads[:3]:
                one.wait()
        squares = jnp.zeros((UNIT, 1), jnp.float32)
        for b in range(peers):
            squares += jnp.sum(
                jnp.square(rows_in[b, rows, :].astype(jnp.float32)), axis=1, keepdims=True
            )
        rms = lax.rsqrt(squares / width + EPSILON)
        row_stats[rows, 1:2] = rms
        for b in range(peers):
            at = pl.ds(b * share, share)
            normed[rows, at] = (
                rows_in[b, rows, :].astype(jnp.float32) * rms * gain_attn[0:1, at]
            ).astype(jnp.bfloat16)
        write(normed.at[rows, :], normed_h.at[rows, :], 0, c)
        for i in range(3):
            found = matmul(normed[rows, :], w_qkv[i])
            if i < 2:
                for p in range(sz.pairs):
                    lanes = found[:, p * PAIR : (p + 1) * PAIR]
                    qkv[i, rows, pl.ds(p * PAIR, PAIR)] = (
                        lanes * cosine[rows, :] + swap_halves(lanes) * sine[rows, :]
                    ).astype(jnp.bfloat16)
            else:
                qkv[i, rows, :] = found.astype(jnp.bfloat16)
            write(qkv.at[i, rows, :], qkv_h.at[i, rows, :], 1 + i, c)

    def attend(c):
        rows = rows_of(c)
        keys = (c + 1) * UNIT
        key_slot = lax.broadcasted_iota(jnp.int32, (keys, UNIT), 0)
        query_slot = lax.broadcasted_iota(jnp.int32, (keys, UNIT), 1) + c * UNIT
        allowed = (row_stats[pl.ds(0, keys), 2:3] == seq_row[0:1, rows]) & (key_slot <= query_slot)
        bias[pl.ds(0, keys), :] = jnp.where(allowed, 0.0, MASKED)

        @pl.loop(0, sz.pairs)
        def _(p):
            mine = span(p * PAIR, PAIR)
            query = qkv[0, rows, mine]
            key = qkv[1, pl.ds(0, keys), mine]
            value = qkv[2, pl.ds(0, keys), mine]
            first_head = lax.broadcasted_iota(jnp.int32, (1, PAIR), 1) < HDIM
            found = []
            for h in range(2):
                chosen = first_head if h == 0 else jnp.logical_not(first_head)
                scores = matmul_last(key, jnp.where(chosen, query, 0.0)) * SCALE
                scores += bias[pl.ds(0, keys), :]
                peak = jnp.max(scores, axis=0, keepdims=True)
                expon = jnp.exp(scores - peak)
                total = jnp.sum(expon, axis=0, keepdims=True)
                log_total[pl.ds(2 * p + h, 1), rows] = peak + jnp.log(total)
                weights = (expon * (1.0 / total)).astype(jnp.bfloat16)
                found.append(matmul_first(weights, value))
            mixed[rows, mine] = jnp.where(first_head, *found).astype(jnp.bfloat16)

        write(mixed.at[rows, :], mixed_h.at[rows, :], 4, c)

    def project_out(c):
        rows = rows_of(c)
        if c == 0:
            weight_loads[3].wait()

        for away in exchange.order:
            at = span(exchange.others[away] * share, share)
            part[away - 1, rows, :] = matmul(mixed[rows, :], w_out[:, at]).astype(jnp.bfloat16)
        exchange.sum_start(c)
        resid[rows, :] = rows_in[me, rows, :].astype(jnp.float32) + matmul(
            mixed[rows, :], w_out[:, span(me * share, share)]
        )

    def residual(c):
        rows = rows_of(c)
        total = resid[rows, :] + exchange.sum_finish(c)
        resid[rows, :] = total
        write(resid.at[rows, :], resid_h.at[rows, :], 5, c)
        rows_in[me, rows, :] = total.astype(jnp.bfloat16)
        exchange.start(1, c)

    def act_copies(slot, c, u):
        at = pl.ds(u * sz.act_unit, sz.act_unit)
        return [
            pltpu.make_async_copy(
                acts.at[slot, i], ref.at[rows_of(c), at], act_sems.at[slot, i]
            )
            for i, ref in enumerate((hidden_h, silu_h, slope_h))
        ]

    act_units = sz.hidden // sz.act_unit
    pending = {}

    def feed(c):
        rows = rows_of(c)
        exchange.finish(1, c)
        if c == 0:
            for one in weight_loads[4:]:
                one.wait()
        squares = jnp.zeros((UNIT, 1), jnp.float32)
        for b in range(peers):
            squares += jnp.sum(
                jnp.square(rows_in[b, rows, :].astype(jnp.float32)), axis=1, keepdims=True
            )
        rms = lax.rsqrt(squares / width + EPSILON)
        row_stats[rows, 0:1] = rms
        outs.pop((0, c)).wait()
        for b in range(peers):
            at = pl.ds(b * share, share)
            normed[rows, at] = (
                rows_in[b, rows, :].astype(jnp.float32) * rms * gain_mlp[0:1, at]
            ).astype(jnp.bfloat16)
        write(normed.at[rows, :], normed_mlp_h.at[rows, :], 6, c)
        for u in range(act_units):
            slot = (c * act_units + u) % 2
            for one in pending.pop(slot, []):
                one.wait()
            at = pl.ds(u * sz.act_unit, sz.act_unit)
            gate = matmul(normed[rows, :], w_mlp[0, :, at])
            upward = matmul(normed[rows, :], w_mlp[1, :, at])
            sigmoid = 1.0 / (1.0 + jnp.exp(-gate))
            silu = gate * sigmoid
            acts[slot, 0] = (silu * upward).astype(jnp.bfloat16)
            acts[slot, 1] = silu.astype(jnp.bfloat16)
            acts[slot, 2] = (upward * sigmoid * (1.0 + gate * (1.0 - sigmoid))).astype(jnp.bfloat16)
            pending[slot] = act_copies(slot, c, u)
            for one in pending[slot]:
                one.start()

    log_total[...] = jnp.zeros_like(log_total)

    def places(slot):
        number = start = jnp.zeros_like(slot)
        end = 0
        for j in range(lengths.shape[1]):
            end += lengths[0, j]
            passed = slot >= end
            number += passed.astype(jnp.int32)
            start += jnp.where(passed, lengths[0, j], 0)
        live = slot < end
        return jnp.where(live, number, slots + slot), jnp.where(live, slot - start, 0)

    seq_row[...] = places(lax.broadcasted_iota(jnp.int32, seq_row.shape, 1))[0].astype(jnp.float32)

    @pl.loop(0, slots // PAIR)
    def _(i):
        rows = span(i * PAIR, PAIR)
        slot = lax.broadcasted_iota(jnp.int32, (PAIR, PAIR), 0) + i * PAIR
        lane = lax.broadcasted_iota(jnp.int32, (PAIR, PAIR), 1)
        sequence, position = places(slot)
        row_stats[rows, :] = sequence.astype(jnp.float32)
        freq_index = lax.rem(lane, HDIM // 2).astype(jnp.float32)
        inverse = jnp.exp(freq_index * (-2.0 * math.log(ROPE_BASE) / HDIM))
        angles = position.astype(jnp.float32) * inverse
        cosine[rows, :] = jnp.cos(angles)
        sines = jnp.sin(angles)
        sine[rows, :] = jnp.where(lax.rem(lane, HDIM) < HDIM // 2, -sines, sines)

    for i, (src, dst) in enumerate(((cosine, cosine_h), (sine, sine_h))):
        write(src, dst, 7, 2 + i)
    write(seq_row, seq_row_h, 8, 0)
    def pass_on(c):
        exchange.forward(0, c)
        if c + 2 < chunks:
            exchange.start(0, c + 2)

    passed = min(2, chunks)
    for c in range(passed):
        pass_on(c)
    for c in range(chunks + 4):
        if c < chunks:
            project(c)
            attend(c)
            project_out(c)
        if passed < chunks:
            pass_on(passed)
            passed += 1
        if 0 <= c - 1 < chunks:
            exchange.sum_forward(c - 1)
        if 0 <= c - 2 < chunks:
            residual(c - 2)
        if 0 <= c - 3 < chunks:
            exchange.forward(1, c - 3)
        if 0 <= c - 4 < chunks:
            feed(c - 4)
    write(log_total, log_h, 7, 0)
    write(row_stats, stats_h, 7, 1)
    for slot in list(pending):
        for one in pending.pop(slot):
            one.wait()
    for one in outs.values():
        one.wait()


def forward(sz, big, small):
    slots, width, share, attn, hidden = sz.slots, sz.width, sz.share, sz.attn, sz.hidden
    chunks = slots // UNIT
    bf16, f32 = jnp.bfloat16, jnp.float32
    shapes = [
        ((slots, width), bf16), ((3, slots, attn), bf16), ((slots, attn), bf16), ((8, slots), f32),
        ((slots, share), f32), ((slots, width), bf16), ((slots, hidden), bf16),
        ((slots, hidden), bf16), ((slots, hidden), bf16), ((slots, PAIR), f32),
        ((slots, PAIR), f32), ((slots, PAIR), f32), ((8, slots), f32),
    ]
    flops = 2 * slots * (4 * width * attn + 2 * width * hidden)
    return pl.pallas_call(
        functools.partial(forward_kernel, sz),
        out_shape=[jax.ShapeDtypeStruct(*s) for s in shapes],
        in_specs=[pl.BlockSpec(memory_space=pl.ANY)] * len(big)
        + [pl.BlockSpec(memory_space=pltpu.SMEM)]
        + [pl.BlockSpec(memory_space=pltpu.VMEM)] * (len(small) - 1),
        out_specs=[pl.BlockSpec(memory_space=pl.ANY)] * len(shapes),
        scratch_shapes=[
            pltpu.VMEM((sz.peers, slots, share), bf16),
            pltpu.VMEM((3, width, attn), bf16),
            pltpu.VMEM((attn, width), bf16),
            pltpu.VMEM((2, width, hidden), bf16),
            pltpu.VMEM((slots, width), bf16),
            pltpu.VMEM((3, slots, attn), bf16),
            pltpu.VMEM((slots, attn), bf16),
            *exchange_of(sz).scratch_shapes(sz),
            pltpu.VMEM((slots, share), f32),
            pltpu.VMEM((2, 3, UNIT, sz.act_unit), bf16),
            pltpu.VMEM((8, slots), f32),
            pltpu.VMEM((slots, PAIR), f32),
            pltpu.VMEM((slots, UNIT), f32),
            pltpu.VMEM((slots, PAIR), f32),
            pltpu.VMEM((slots, PAIR), f32),
            pltpu.VMEM((8, slots), f32),
            pltpu.SemaphoreType.DMA((7,)),
            pltpu.SemaphoreType.DMA((2 * exchange_of(sz).KINDS, chunks, sz.peers)),
            pltpu.SemaphoreType.DMA((9, chunks)),
            pltpu.SemaphoreType.DMA((2, 3)),
        ],
        compiler_params=pltpu.CompilerParams(
            collective_id=1, has_side_effects=True, vmem_limit_bytes=63 * MIB
        ),
        cost_estimate=pl.CostEstimate(
            flops=flops, bytes_accessed=60 * MIB, transcendentals=slots * slots * 8
        ),
    )(*big, *small)


def backward_kernel(sz, *refs):
    (
        hidden_h, silu_h, slope_h, cot_h, normed_mlp_h, mixed_h, normed_h, qkv_h,
        w_down_h, w_gate_h, w_up_h, w_out_h, w_query_h, w_key_h, w_value_h,
        resid_h, cosine, sine, seq_row, log_total, row_stats, gain_attn, gain_mlp,
        *refs,
    ) = refs
    outs, (grad_tokens_h, out_tokens_h, gains_h), refs = refs[:7], refs[7:10], refs[10:]
    (
        buf_a, buf_b, buf_c, d_gate, d_up, send, full, recv, d_mixed, d_qkv, w_buf, w_cols,
        acc_key, acc_value, row_part, row_send, row_recv, gains, gains_out,
        load_sems, w_sems, tensor_sems, gain_sems, *line_scratch,
    ) = refs
    slots, width, share, peers = sz.slots, sz.width, sz.share, sz.peers
    n_dp = lax.axis_size("dp")
    dp, me = lax.axis_index("dp"), lax.axis_index("tensor")
    tile_rows, tile_cols = sz.tile
    assert tile_cols == share

    def place_of(m):
        across, down = sz.plan[m][2], sz.shapes[m][0] // tile_rows
        if m == 0:
            return lambda i: (lax.rem(i, down), partner(me, i // down, peers))
        return lambda i: (i // across, lax.rem(i, across))

    places = [place_of(m) for m in range(len(sz.plan))]
    line = LineSum(
        sz.total, [(ref, plan[0], plan[1], at) for ref, plan, at in zip(outs, sz.plan, places)],
        sz.tile, line_scratch,
    )

    def load(src, dst, index):
        return pltpu.make_async_copy(src, dst, load_sems.at[index])

    def peer(away):
        return partner(me, away, peers)

    def other_dp(away):
        return lax.rem(dp + away, n_dp)

    barrier = pltpu.get_barrier_semaphore()
    own = span(me * share, share)
    first_loads = [
        load(hidden_h, buf_a.at[:, pl.ds(0, sz.hidden)], 0), load(cot_h, buf_b.at[:, own], 1),
        load(normed_mlp_h, buf_c, 2),
    ]
    for one in first_loads:
        one.start()

    def remote(kind, away, src, dst):
        return pltpu.make_async_remote_copy(
            src_ref=src, dst_ref=dst, send_sem=tensor_sems.at[2 * kind, away],
            recv_sem=tensor_sems.at[2 * kind + 1, away],
            device_id=(dp, peer(away)), device_id_type=MESH,
        )

    def send_cot(away):
        return remote(4, away, cot_h, buf_b.at[:, own])
    for away in range(1, n_dp):
        pl.semaphore_signal(
            barrier, inc=1, device_id=(other_dp(away), me), device_id_type=MESH
        )
    for away in range(1, peers):
        pl.semaphore_signal(barrier, inc=1, device_id=(dp, peer(away)), device_id_type=MESH)
    pl.semaphore_wait(barrier, n_dp - 1 + peers - 1)
    for away in range(1, peers):
        send_cot(away).start()

    attn_at = [pl.ds(i * sz.attn, sz.attn) for i in range(4)]
    grads = [
        (lambda r: buf_a[:, r], lambda c: buf_b[:, c]),
        (lambda r: buf_c[:, r], lambda c: d_gate[:, c]),
        (lambda r: buf_c[:, r], lambda c: d_up[:, c]),
        (lambda r: d_gate[:, pl.ds(pl.multiple_of(3 * sz.attn + r.start, tile_rows), tile_rows)],
         lambda c: buf_a[:, c]),
        (lambda r: buf_b[:, r], lambda c: d_qkv[2, :, c]),
        (lambda r: buf_b[:, r], lambda c: d_qkv[0, :, c]),
        (lambda r: buf_b[:, r], lambda c: d_qkv[1, :, c]),
    ]

    def cot_at(away):
        last = sz.plan[1][0] - sz.hidden // UNIT // 2 - 1
        return min(away * (sz.shapes[0][0] // tile_rows), last)

    def tile_tick(m, k):
        row, col = places[m](k - sz.plan[m][0])
        rows, cols = span(row * tile_rows, tile_rows), span(col * tile_cols, tile_cols)
        if m == 0:
            for away in range(1, peers):
                @pl.when(k == cot_at(away))
                def _(away=away):
                    send_cot(away).wait()
        left, right = grads[m]
        line.put(k, matmul_first(left(rows), right(cols)))
        line.tick(k)

    cursor = [0]

    def matrix_of(k):
        return [m for m, (first, count, _) in enumerate(sz.plan) if first <= k < first + count][0]

    def advance_to(stop):
        while cursor[0] < stop:
            m = matrix_of(cursor[0])
            until = min(stop, sz.plan[m][0] + sz.plan[m][1])

            @pl.loop(cursor[0], until)
            def _(k, m=m):
                tile_tick(m, k)

            cursor[0] = until

    def run_units(count, unit, group=1):
        done = 0
        while done < count:
            m = matrix_of(cursor[0])
            room = (sz.plan[m][0] + sz.plan[m][1] - cursor[0]) // group
            if not room:
                for g in range(group):
                    unit(done, g)
                    tile_tick(matrix_of(cursor[0]), cursor[0])
                    cursor[0] += 1
                done += 1
                continue
            step = min(room, count - done)

            @pl.loop(0, step)
            def _(i, m=m, done=done, start=cursor[0]):
                for g in range(group):
                    unit(done + i, g)
                    tile_tick(m, start + i * group + g)

            cursor[0] += step * group
            done += step

    order = list(range(peers - 1, 0, -1)) + [0]

    def block_of(u):
        return partner(me, peers - 1 - u // sz.block_units, peers)

    def feature(u):
        return block_of(u) * share + lax.rem(u, sz.block_units) * UNIT

    def scatter(round_, away):
        dst = full.at[me] if round_ == 2 else recv.at[away - 1]
        return remote(round_, away, send.at[peer(away)], dst)

    def store_part(round_, u, value):
        send[block_of(u), :, span(lax.rem(u, sz.block_units) * UNIT, UNIT)] = value.astype(
            jnp.bfloat16
        )
        for i, away in enumerate(order[:-1] if round_ != 1 else ()):
            @pl.when(u == (i + 1) * sz.block_units - 1)
            def _(away=away):
                scatter(round_, away).start()

    mlp_units = width // UNIT
    hid = pl.ds(0, sz.hidden)

    def prefetched(count, loads, u):
        for one in loads(u):
            one.wait()

        @pl.when(u + 1 < count)
        def _():
            for one in loads(u + 1):
                one.start()

    def hidden_loads(u):
        cols = span(u * UNIT, UNIT)
        slot = lax.rem(u, 2)
        return (
            pltpu.make_async_copy(w_down_h.at[cols, :], w_buf.at[slot, 0], w_sems.at[0, slot]),
            pltpu.make_async_copy(
                silu_h.at[:, cols], d_qkv.at[slot, :, pl.ds(0, UNIT)], w_sems.at[1, slot]
            ),
            pltpu.make_async_copy(
                slope_h.at[:, cols], d_qkv.at[slot, :, pl.ds(UNIT, UNIT)], w_sems.at[2, slot]
            ),
        )

    def hidden_unit(u, _):
        prefetched(sz.hidden // UNIT, hidden_loads, u)
        slot = lax.rem(u, 2)
        cols = span(u * UNIT, UNIT)
        d_hidden = matmul_last(buf_b[...], w_buf[slot, 0])
        d_up[:, cols] = (d_hidden * d_qkv[slot, :, pl.ds(0, UNIT)]).astype(jnp.bfloat16)
        d_gate[:, cols] = (d_hidden * d_qkv[slot, :, pl.ds(UNIT, UNIT)]).astype(jnp.bfloat16)

    def twice(unit):
        def both(u, g):
            unit(2 * u, g)
            unit(2 * u + 1, g)

        return both

    for one in hidden_loads(0):
        one.start()
    for one in first_loads:
        one.wait()
    advance_to(sz.plan[1][0] - sz.hidden // UNIT // 2)
    run_units(sz.hidden // UNIT // 2, twice(hidden_unit))

    def gather(round_):
        for away in range(1, peers):
            scatter(round_, away).wait()

    def gathered(round_, rows):
        total = send[me, rows, :].astype(jnp.float32)
        for away in range(1, peers):
            block = full[peer(away), rows, :] if round_ == 2 else recv[away - 1, rows, :]
            total += block.astype(jnp.float32)
        return total

    def mlp_loads(u):
        slot = lax.rem(u, 2)
        rows = span(feature(u), UNIT)
        return (
            pltpu.make_async_copy(
                w_gate_h.at[rows, :], w_buf.at[slot, 0, :, hid], w_sems.at[0, slot]
            ),
            pltpu.make_async_copy(
                w_up_h.at[rows, :], w_buf.at[slot, 1, :, hid], w_sems.at[1, slot]
            ),
        )

    def mlp_unit(u, _):
        prefetched(mlp_units, mlp_loads, u)
        slot = lax.rem(u, 2)
        part = matmul_last(d_gate[...], w_buf[slot, 0, :, hid])
        part += matmul_last(d_up[...], w_buf[slot, 1, :, hid])
        store_part(0, u, part)

    for one in mlp_loads(0):
        one.start()
    run_units(mlp_units, mlp_unit)
    advance_to(cursor[0] + 4)

    def spread(away):
        return remote(3, away, full.at[me], full.at[me])

    w_out_rows = sz.attn // UNIT
    w_out_loads = [
        load(w_out_h.at[pl.ds(i * UNIT, UNIT), :], w_buf.at[0, i], 3 + i) for i in range(w_out_rows)
    ]
    for one in w_out_loads:
        one.start()
    gather(0)

    @pl.loop(0, slots // UNIT)
    def _(i):
        full[me, span(i * UNIT, UNIT), :] = gathered(0, span(i * UNIT, UNIT)).astype(jnp.bfloat16)

    for away in range(1, peers):
        spread(away).start()
    advance_to(sz.plan[2][0])

    hidden_load = load(hidden_h, d_gate, 0)
    hidden_load.start()

    def out_loads(u):
        slot = lax.rem(u, 2)
        return [
            pltpu.make_async_copy(
                w_down_h.at[:, span(feature(u), UNIT)], w_cols.at[slot], w_sems.at[0, slot]
            )
        ]

    def out_unit(u, _):
        prefetched(mlp_units, out_loads, u)
        store_part(1, u, matmul(d_gate[...], w_cols[lax.rem(u, 2)]))

    for one in out_loads(0):
        one.start()
    hidden_load.wait()
    run_units(mlp_units // 2, twice(out_unit))

    for away in range(1, peers):
        spread(away).wait()
    for one in w_out_loads:
        one.wait()

    gains[dp] = jnp.zeros_like(gains[dp])

    def norm_unit(u, _):
        rows = span(u * UNIT, UNIT)
        row_sum = jnp.zeros((UNIT, 1), jnp.float32)
        for b in range(peers):
            at = pl.ds(b * share, share)
            row_sum += jnp.sum(
                full[b, rows, :].astype(jnp.float32) * buf_c[rows, at].astype(jnp.float32),
                axis=1, keepdims=True,
            )
        rms = row_stats[rows, 0:1]
        for b in range(peers):
            at = pl.ds(b * share, share)
            gain = gain_mlp[0:1, at]
            lean = buf_c[rows, at].astype(jnp.float32) / gain * (row_sum / width)
            d_resid = buf_b[rows, at].astype(jnp.float32) + rms * (
                gain * full[b, rows, :].astype(jnp.float32) - lean
            )
            buf_a[rows, at] = d_resid.astype(jnp.bfloat16)
        gains[dp, 0:1, :] += jnp.sum(
            full[me, rows, :].astype(jnp.float32) * buf_c[rows, own].astype(jnp.float32),
            axis=0, keepdims=True,
        ) / gain_mlp[0:1, own]
        for i in range(w_out_rows):
            d_mixed[rows, pl.ds(i * UNIT, UNIT)] = matmul_last(
                buf_a[rows, :], w_buf[0, i]
            ).astype(jnp.bfloat16)

    run_units(slots // UNIT, norm_unit)
    for away in range(1, peers):
        scatter(1, away).start()

    attn_loads = [
        load(ref, d_gate.at[:, attn_at[i]], 5 + i)
        for i, ref in enumerate((qkv_h.at[0], qkv_h.at[1], qkv_h.at[2], mixed_h))
    ] + [load(normed_h, buf_b, 9)]
    for one in attn_loads:
        one.start()
    for one in attn_loads:
        one.wait()
    blocks = slots // UNIT

    def attend_unit(p, i):
        rows = pl.ds(i * UNIT, UNIT)
        keys = (i + 1) * UNIT
        lanes = [pl.ds(pl.multiple_of(j * sz.attn + p * PAIR, PAIR), PAIR) for j in range(3)]
        mine = span(p * PAIR, PAIR)
        query = d_gate[rows, lanes[0]]
        key = d_gate[pl.ds(0, keys), lanes[1]]
        value = d_gate[pl.ds(0, keys), lanes[2]]
        grad = d_mixed[rows, mine]
        first_head = lax.broadcasted_iota(jnp.int32, (1, PAIR), 1) < HDIM
        key_slot = lax.broadcasted_iota(jnp.int32, (keys, UNIT), 0)
        query_slot = lax.broadcasted_iota(jnp.int32, (keys, UNIT), 1) + i * UNIT
        allowed = (row_stats[pl.ds(0, keys), 2:3] == seq_row[0:1, rows]) & (key_slot <= query_slot)
        found = []
        for h in range(2):
            chosen = first_head if h == 0 else jnp.logical_not(first_head)
            scores = matmul_last(key, jnp.where(chosen, query, 0.0)) * SCALE
            scores -= log_total[pl.ds(2 * p + h, 1), rows]
            probs = jnp.exp(jnp.where(allowed, scores, MASKED))
            grad_probs = matmul_last(value, jnp.where(chosen, grad, 0.0))
            delta = jnp.sum(probs * grad_probs, axis=0, keepdims=True)
            grad_scores = (probs * (grad_probs - delta)).astype(jnp.bfloat16)
            found.append(
                (
                    matmul_first(grad_scores, key),
                    matmul(grad_scores, query),
                    matmul(probs.astype(jnp.bfloat16), grad),
                )
            )
        grad_query, grad_key, grad_value = [
            jnp.where(first_head, one, two) for one, two in zip(*found)
        ]
        d_qkv[0, rows, mine] = rotate_back(
            grad_query * SCALE, cosine[rows, :], sine[rows, :]
        ).astype(jnp.bfloat16)
        for acc, part in ((acc_key, grad_key), (acc_value, grad_value)):
            if i > 0:
                acc[pl.ds(0, keys - UNIT), :] += part[: keys - UNIT]
            acc[pl.ds(keys - UNIT, UNIT), :] = part[keys - UNIT :]
        if i + 1 == blocks:
            d_qkv[1, :, mine] = rotate_back(acc_key[...] * SCALE, cosine[...], sine[...]).astype(
                jnp.bfloat16
            )
            d_qkv[2, :, mine] = acc_value[...].astype(jnp.bfloat16)

    steps = [(0, 1), (2,), (3,)] if blocks == 4 else [(i,) for i in range(blocks)]

    def attend_step(p, g):
        for i in steps[g]:
            attend_unit(p, i)

    run_units(sz.pairs, attend_step, len(steps))
    advance_to(sz.plan[4][0])

    gather(1)
    for j in range(share // PAIR):
        lanes = pl.ds(j * PAIR, PAIR)
        piece = load(resid_h.at[:, lanes], acc_key, 2)
        piece.start()
        piece.wait()

        @pl.loop(0, slots // UNIT)
        def _(i, lanes=lanes):
            rows = span(i * UNIT, UNIT)
            total = acc_key[rows, :] + send[me, rows, lanes].astype(jnp.float32)
            for away in range(1, peers):
                total += recv[away - 1, rows, lanes].astype(jnp.float32)
            send[me, rows, lanes] = total.astype(jnp.bfloat16)

    tokens_out = load(send.at[me], out_tokens_h, 0)
    tokens_out.start()

    row_part[...] = jnp.zeros_like(row_part)

    def attn_loads_of(u):
        slot = lax.rem(u, 2)
        rows = span(feature(u), UNIT)
        return [
            pltpu.make_async_copy(ref.at[rows, :], w_buf.at[slot, 0, :, at], w_sems.at[i, slot])
            for i, (ref, at) in enumerate(zip((w_query_h, w_key_h, w_value_h), attn_at))
        ]

    def attn_unit(u, _):
        prefetched(mlp_units, attn_loads_of, u)
        slot = lax.rem(u, 2)
        part = jnp.zeros((slots, UNIT), jnp.float32)
        for i in range(3):
            part += matmul_last(d_qkv[i, :, pl.ds(0, sz.attn)], w_buf[slot, 0, :, attn_at[i]])
        store_part(2, u, part)
        row_part[...] += jnp.sum(
            part * buf_b[:, span(feature(u), UNIT)].astype(jnp.float32), axis=1, keepdims=True
        )

    def row_scatter(away):
        return remote(5, away, row_send, row_recv.at[away - 1])

    for one in attn_loads_of(0):
        one.start()

    tokens_out.wait()
    run_units(mlp_units // 2, twice(attn_unit))
    row_send[...] = row_part[...].T[0:8, :]
    for away in range(1, peers):
        row_scatter(away).start()
    advance_to(sz.total)

    @pl.loop(sz.total, sz.total + 3)
    def _(k):
        line.tick(k)

    for away in range(1, peers):
        row_scatter(away).wait()
    row_sums = row_send[...]
    for away in range(1, peers):
        row_sums += row_recv[away - 1]
    row_part[...] = jnp.concatenate([row_sums] * (row_part.shape[1] // 8), axis=0).T
    gather(2)
    gain = gain_attn[0:1, own]

    @pl.loop(0, slots // UNIT)
    def _(i):
        rows = span(i * UNIT, UNIT)
        d_own = gathered(2, rows)
        straight = buf_b[rows, own].astype(jnp.float32)
        gains[dp, 1:2, :] += jnp.sum(d_own * straight, axis=0, keepdims=True) / gain
        lean = straight / gain * (row_part[rows, 0:1] / width)
        send[me, rows, :] = (
            buf_a[rows, own].astype(jnp.float32) + row_stats[rows, 1:2] * (gain * d_own - lean)
        ).astype(jnp.bfloat16)

    grad_out = load(send.at[me], grad_tokens_h, 10)
    grad_out.start()

    def gain_copy(away):
        return pltpu.make_async_remote_copy(
            src_ref=gains.at[dp], dst_ref=gains.at[dp],
            send_sem=gain_sems.at[0, away], recv_sem=gain_sems.at[1, away],
            device_id=(other_dp(away), me), device_id_type=MESH,
        )

    for away in range(1, n_dp):
        gain_copy(away).start()

    @pl.loop(sz.total + 3, sz.total + 6)
    def _(k):
        line.tick(k)

    for away in range(1, n_dp):
        gain_copy(away).wait()
    total = gains[0]
    for i in range(1, n_dp):
        total += gains[i]
    gains_out[...] = total
    gain_out = load(gains_out, gains_h, 11)
    gain_out.start()

    @pl.loop(sz.total + 6, sz.total + line.lag_d)
    def _(k):
        line.tick(k)

    grad_out.wait()
    gain_out.wait()


def backward(sz, big, small):
    whole_rows = pltpu.VMEM((sz.slots, sz.width), jnp.bfloat16)
    hidden_rows = pltpu.VMEM((sz.slots, sz.hidden), jnp.bfloat16)
    assert sz.hidden == 4 * sz.attn and sz.share % UNIT == 0 and sz.hidden <= sz.width
    n_dp = lax.axis_size("dp")
    attn_rows = max(sz.attn, 2 * UNIT)
    flops = 6 * sz.slots * (3 * sz.width * sz.hidden + 4 * sz.width * sz.attn)
    return pl.pallas_call(
        functools.partial(backward_kernel, sz),
        out_shape=[jax.ShapeDtypeStruct(s, jnp.bfloat16) for s in sz.shapes]
        + [
            jax.ShapeDtypeStruct((sz.slots, sz.share), jnp.bfloat16),
            jax.ShapeDtypeStruct((sz.slots, sz.share), jnp.bfloat16),
            jax.ShapeDtypeStruct((8, sz.share), jnp.float32),
        ],
        in_specs=[pl.BlockSpec(memory_space=pl.ANY)] * len(big)
        + [pl.BlockSpec(memory_space=pltpu.VMEM)] * len(small),
        out_specs=[pl.BlockSpec(memory_space=pl.ANY)] * 10,
        scratch_shapes=[
            whole_rows, whole_rows, whole_rows, hidden_rows, hidden_rows,
            pltpu.VMEM((sz.peers, sz.slots, sz.share), jnp.bfloat16),
            pltpu.VMEM((sz.peers, sz.slots, sz.share), jnp.bfloat16),
            pltpu.VMEM((sz.peers - 1, sz.slots, sz.share), jnp.bfloat16),
            pltpu.VMEM((sz.slots, sz.attn), jnp.bfloat16),
            pltpu.VMEM((3, sz.slots, attn_rows), jnp.bfloat16),
            pltpu.VMEM((2, 2, UNIT, sz.width), jnp.bfloat16),
            pltpu.VMEM((2, sz.hidden, UNIT), jnp.bfloat16),
            pltpu.VMEM((sz.slots, PAIR), jnp.float32),
            pltpu.VMEM((sz.slots, PAIR), jnp.float32),
            pltpu.VMEM((sz.slots, PAIR), jnp.float32),
            pltpu.VMEM((8, sz.slots), jnp.float32),
            pltpu.VMEM((sz.peers - 1, 8, sz.slots), jnp.float32),
            pltpu.VMEM((n_dp, 8, sz.share), jnp.float32),
            pltpu.VMEM((8, sz.share), jnp.float32),
            pltpu.SemaphoreType.DMA((12,)),
            pltpu.SemaphoreType.DMA((3, 2)),
            pltpu.SemaphoreType.DMA((12, sz.peers)),
            pltpu.SemaphoreType.DMA((2, n_dp)),
        ]
        + LineSum.scratch_shapes(sz.tile),
        compiler_params=pltpu.CompilerParams(
            collective_id=0, has_side_effects=True, vmem_limit_bytes=63 * MIB
        ),
        cost_estimate=pl.CostEstimate(
            flops=flops, bytes_accessed=200 * MIB, transcendentals=sz.slots * sz.slots * 8
        ),
    )(*big, *small)


def widen_kernel(steps, depth, *refs):
    count = 1 + max(i for i, _, _ in steps)
    sources, moved, gains, refs = refs[:count], refs[count : count + 2], refs[count + 2], refs[count + 3 :]
    results, moved_to, gains_to = refs[:count], refs[count : count + 2], refs[count + 2 : count + 4]
    narrow, wide, in_sems, out_sems, move_sems = refs[count + 4 :]
    moves = [
        pltpu.make_async_copy(src, dst, move_sems.at[i])
        for i, (src, dst) in enumerate(zip(moved, moved_to))
    ]
    for one in moves:
        one.start()
    gains_to[0][...] = gains[1, :]
    gains_to[1][...] = gains[0, :]

    def read(n):
        i, first, rows = steps[n]
        cols = sources[i].shape[1]
        slot = n % depth
        return pltpu.make_async_copy(
            sources[i].at[pl.ds(first, rows), :],
            narrow[cols].at[slot, pl.ds(0, rows), :], in_sems.at[slot],
        )

    def write(n):
        i, first, rows = steps[n]
        cols = sources[i].shape[1]
        slot = n % depth
        return pltpu.make_async_copy(
            wide[cols].at[slot, pl.ds(0, rows), :],
            results[i].at[pl.ds(first, rows), :], out_sems.at[slot],
        )

    for n in range(min(depth, len(steps))):
        read(n).start()
    for n, (i, _, rows) in enumerate(steps):
        cols = sources[i].shape[1]
        slot = n % depth
        read(n).wait()
        if n >= depth:
            write(n - depth).wait()
        strip = min(rows, 32 * 2048 // cols)

        @pl.loop(0, rows // strip)
        def _(r, cols=cols, slot=slot, strip=strip):
            at = span(r * strip, strip)
            wide[cols][slot, at, :] = narrow[cols][slot, at, :].astype(jnp.float32)

        write(n).start()
        if n + depth < len(steps):
            read(n + depth).start()
    for n in range(max(0, len(steps) - depth), len(steps)):
        write(n).wait()
    for one in moves:
        one.wait()


def widen(arrays, moved, gains):
    depth = 4
    block = 512 * 1024
    steps, most = [], {}
    for i, (rows, cols) in enumerate(a.shape for a in arrays):
        step = min(rows, block // cols)
        most[cols] = max(step, most.get(cols, 0))
        steps += [(i, first, step) for first in range(0, rows, step)]
    return pl.pallas_call(
        functools.partial(widen_kernel, steps, depth),
        out_shape=[jax.ShapeDtypeStruct(a.shape, jnp.float32) for a in arrays]
        + [jax.ShapeDtypeStruct(a.shape, a.dtype) for a in moved]
        + [jax.ShapeDtypeStruct(gains.shape[1:], gains.dtype)] * 2,
        in_specs=[pl.BlockSpec(memory_space=pl.ANY)] * (len(arrays) + 2)
        + [pl.BlockSpec(memory_space=pltpu.VMEM)],
        out_specs=[pl.BlockSpec(memory_space=pl.ANY)] * (len(arrays) + 2)
        + [pl.BlockSpec(memory_space=pltpu.VMEM)] * 2,
        scratch_shapes=[
            {cols: pltpu.VMEM((depth, rows, cols), jnp.bfloat16) for cols, rows in most.items()},
            {cols: pltpu.VMEM((depth, rows, cols), jnp.float32) for cols, rows in most.items()},
            pltpu.SemaphoreType.DMA((depth,)),
            pltpu.SemaphoreType.DMA((depth,)),
            pltpu.SemaphoreType.DMA((2,)),
        ],
        compiler_params=pltpu.CompilerParams(vmem_limit_bytes=63 * MIB),
        cost_estimate=pl.CostEstimate(flops=0, bytes_accessed=96 * MIB, transcendentals=0),
    )(*arrays, *moved, gains)


def body(
    tokens,
    norm_gain_attn,
    norm_gain_mlp,
    w_query,
    w_key,
    w_value,
    w_out,
    w_gate,
    w_up,
    w_down,
    cotangent,
    lengths,
):
    slot_count = tokens.shape[0]
    share_width = tokens.shape[1]
    model_width = share_width * lax.axis_size("tensor")
    attn_width = w_query.shape[1]
    sz = Sizes(slot_count, model_width, share_width, w_gate.shape[1], attn_width)
    gain_attn = norm_gain_attn.reshape(1, model_width)
    gain_mlp = norm_gain_mlp.reshape(1, model_width)
    (
        normed, qkv, mixed, log_total, resid_here, normed_mlp, hidden, silu, slope, row_stats,
        cosine, sine, seq_row,
    ) = forward(
        sz, (tokens, w_query, w_key, w_value, w_out, w_gate, w_up), (lengths, gain_attn, gain_mlp)
    )
    down, gate, up, out, value, query, key, grad_tokens, out_tokens, gains = backward(
        sz,
        (
            hidden, silu, slope, cotangent, normed_mlp, mixed, normed, qkv,
            w_down, w_gate, w_up, w_out, w_query, w_key, w_value, resid_here,
        ),
        (cosine, sine, seq_row, log_total, row_stats, gain_attn, gain_mlp),
    )

    down, gate, up, out, value, query, key, grad_tokens, out_tokens, gain_attn, gain_mlp = widen(
        [down, gate, up, out, value, query, key], [grad_tokens, out_tokens], gains
    )
    return (
        out_tokens, grad_tokens, gain_attn, gain_mlp, query, key, value, out, gate, up, down,
    )


def solution(mesh):
    placed = (
        P("dp", "tensor"),
        P(),
        P(),
        P(None, "tensor"),
        P(None, "tensor"),
        P(None, "tensor"),
        P("tensor", None),
        P(None, "tensor"),
        P(None, "tensor"),
        P("tensor", None),
        P("dp", "tensor"),
        P("dp", None),
    )
    return jax.shard_map(
        body,
        mesh=mesh,
        in_specs=placed,
        out_specs=(
            P("dp", "tensor"),
            P("dp", "tensor"),
            P("tensor"),
            P("tensor"),
            P(None, "tensor"),
            P(None, "tensor"),
            P(None, "tensor"),
            P("tensor", None),
            P(None, "tensor"),
            P(None, "tensor"),
            P("tensor", None),
        ),
        check_vma=False,
    )
```

```python
import functools
import math

import jax
import jax.numpy as jnp
from jax import lax
from jax.experimental import pallas as pl
from jax.experimental.pallas import tpu as pltpu
from jax.sharding import PartitionSpec as P

HDIM = 64
PAIR = 2 * HDIM


EPSILON = 1e-05
ROPE_BASE = 130000.0
SCALE = HDIM ** (-0.5)
MASKED = -1e30
MESH = pl.DeviceIdType.MESH
HOP_LAG = 2
TILE_ROWS = 512
UNIT = 256
MIB = 1024 * 1024


def matmul_first(left, right):
    return lax.dot_general(
        left, right, (((0,), (0,)), ((), ())), preferred_element_type=jnp.float32
    )


def matmul_last(left, right):
    return lax.dot_general(
        left, right, (((1,), (1,)), ((), ())), preferred_element_type=jnp.float32
    )


def matmul(left, right):
    return jnp.dot(left, right, preferred_element_type=jnp.float32)


def span(first, size):
    return pl.ds(pl.multiple_of(first, size), size)


def swap_halves(values):
    lane = lax.broadcasted_iota(jnp.int32, values.shape, 1)
    ahead = pltpu.roll(values, PAIR - HDIM // 2, 1)
    behind = pltpu.roll(values, HDIM // 2, 1)
    return jnp.where(lax.rem(lane, HDIM) < HDIM // 2, ahead, behind)


def rotate_back(values, cosine, sine):
    return values * cosine - swap_halves(values) * sine


class LineSum:
    SLOTS = (
        2, 2, HOP_LAG, 3 * HOP_LAG, HOP_LAG, 2 * HOP_LAG, 3 * HOP_LAG + 2, 3, HOP_LAG, 2 * HOP_LAG,
    )
    SIGNALS = 16

    def __init__(self, total, outs, tile, scratch):
        self.paired = lax.axis_size("dp") == 16
        assert lax.axis_size("dp") in (8, 16)
        self.lag_p = 1
        self.lag_a = 1 + HOP_LAG * self.paired
        self.lag_b = self.lag_a + HOP_LAG
        self.lag_c = self.lag_b + HOP_LAG
        self.lag_f = self.lag_c + HOP_LAG
        self.lag_o = self.lag_f + 1
        self.lag_d = self.lag_o + 1
        self.length = self.lag_d
        self.total = total
        self.outs = outs
        self.tile_rows, self.tile_cols = tile
        self.half = self.tile_rows // 2
        (
            self.stage, self.r_e, self.s_one, self.r_a, self.s_two, self.r_b, self.tot, self.r_f,
            self.s_zero, self.r_p, self.sems, self.out_sems,
        ) = scratch
        dp = lax.axis_index("dp")
        self.tensor = lax.axis_index("tensor")
        self.core = lax.rem(dp, 2)
        z = lax.rem(dp // 2, 4)
        self.is_end = (z == 0) | (z == 3)
        self.is_mid = jnp.logical_not(self.is_end)
        self.sibling = dp + 1 - 2 * self.core
        self.near = dp + jnp.where((z == 0) | (z == 2), 2, -2)
        self.across = dp + 6 - 4 * z
        self.twin = lax.rem(dp + 8, lax.axis_size("dp"))

    @classmethod
    def scratch_shapes(cls, tile):
        rows, cols = tile
        buffers = [
            pltpu.VMEM(
                (slots, 2, rows // 2, cols) if i == 0 else (slots, rows // 2, cols), jnp.bfloat16
            )
            for i, slots in enumerate(cls.SLOTS)
        ]
        if lax.axis_size("dp") != 16:
            buffers[8] = buffers[9] = pltpu.VMEM((1, 8, 128), jnp.bfloat16)
        return buffers + [
            pltpu.SemaphoreType.DMA((12, cls.SIGNALS)),
            pltpu.SemaphoreType.DMA((2, cls.SIGNALS)),
        ]

    def copy(self, hop, chunk, src, dst, target):
        slot = lax.rem(chunk, self.SIGNALS)
        return pltpu.make_async_remote_copy(
            src_ref=src, dst_ref=dst, send_sem=self.sems.at[2 * hop, slot],
            recv_sem=self.sems.at[2 * hop + 1, slot],
            device_id=(target, self.tensor), device_id_type=MESH,
        )

    @staticmethod
    def slot(ref, chunk):
        return ref.at[lax.rem(chunk, ref.shape[0])]

    def hop_e(self, chunk):
        src = self.stage.at[lax.rem(chunk, self.stage.shape[0]), 1 - self.core]
        return self.copy(0, chunk, src, self.slot(self.r_e, chunk), self.sibling)

    def hop_a(self, chunk):
        return self.copy(
            1, chunk, self.slot(self.s_one, chunk), self.slot(self.r_a, chunk), self.near
        )

    def hop_b(self, chunk):
        return self.copy(
            2, chunk, self.slot(self.s_two, chunk), self.slot(self.r_b, chunk), self.across
        )

    def hop_c(self, chunk):
        return self.copy(
            3, chunk, self.slot(self.tot, chunk), self.slot(self.tot, chunk), self.near
        )

    def hop_f(self, chunk):
        return self.copy(
            4, chunk, self.slot(self.tot, chunk), self.slot(self.r_f, chunk), self.sibling
        )

    def hop_p(self, chunk):
        return self.copy(
            5, chunk, self.slot(self.s_zero, chunk), self.slot(self.r_p, chunk), self.twin
        )

    def out_copies(self, chunk, ref, tile_row, tile_col):
        cols = span(tile_col * self.tile_cols, self.tile_cols)
        first = tile_row * self.tile_rows
        mine = span(first + self.core * self.half, self.half)
        other = span(first + (1 - self.core) * self.half, self.half)
        slot = lax.rem(chunk, self.SIGNALS)
        return (
            pltpu.make_async_copy(
                self.slot(self.tot, chunk), ref.at[mine, cols], self.out_sems.at[0, slot]
            ),
            pltpu.make_async_copy(
                self.slot(self.r_f, chunk), ref.at[other, cols], self.out_sems.at[1, slot]
            ),
        )

    def on_out(self, chunk, act):
        for ref, first, count, place in self.outs:
            local = chunk - first

            @pl.when((local >= 0) & (local < count))
            def _(ref=ref, local=local, place=place):
                for one in self.out_copies(chunk, ref, *place(local)):
                    act(one)

    def at(self, chunk, work):
        @pl.when((chunk >= 0) & (chunk < self.total))
        def _():
            work(chunk)

    def put(self, chunk, value):
        self.stage[lax.rem(chunk, self.stage.shape[0])] = value.astype(jnp.bfloat16).reshape(
            2, self.half, self.tile_cols
        )

    def add(self, into, left, right, chunk):
        total = self.slot(left, chunk)[...].astype(jnp.float32)
        total += self.slot(right, chunk)[...].astype(jnp.float32)
        self.slot(into, chunk)[...] = total.astype(jnp.bfloat16)

    def join_cores(self, into, chunk):
        self.hop_e(chunk).wait()
        total = self.stage[lax.rem(chunk, self.stage.shape[0]), self.core].astype(jnp.float32)
        total += self.slot(self.r_e, chunk)[...].astype(jnp.float32)
        self.slot(into, chunk)[...] = total.astype(jnp.bfloat16)

    def late(self, k):
        pass

    def early(self, k):
        def drop(chunk):
            self.on_out(chunk, lambda one: one.wait())

        def out(chunk):
            self.hop_f(chunk).wait()
            self.on_out(chunk, lambda one: one.start())

        def final(chunk):
            @pl.when(self.is_end)
            def _():
                self.hop_c(chunk).wait_recv()

            @pl.when(self.is_mid)
            def _():
                self.hop_c(chunk).wait_send()

            self.hop_f(chunk).start()

        def back(chunk):
            @pl.when(self.is_mid)
            def _():
                self.hop_b(chunk).wait()
                self.add(self.tot, self.s_two, self.r_b, chunk)
                self.hop_c(chunk).start()

        def across(chunk):
            @pl.when(self.is_mid)
            def _():
                self.hop_a(chunk).wait_recv()
                self.add(self.s_two, self.s_one, self.r_a, chunk)
                self.hop_b(chunk).start()

            @pl.when(self.is_end)
            def _():
                self.hop_a(chunk).wait_send()

        def inward(chunk):
            if self.paired:
                self.hop_p(chunk).wait()
                self.add(self.s_one, self.s_zero, self.r_p, chunk)
            else:
                self.join_cores(self.s_one, chunk)

            @pl.when(self.is_end)
            def _():
                self.hop_a(chunk).start()

        def pair(chunk):
            self.join_cores(self.s_zero, chunk)
            self.hop_p(chunk).start()

        self.at(k - self.lag_d, drop)
        self.at(k - self.lag_o, out)
        self.at(k - self.lag_f, final)
        self.at(k - self.lag_c, back)
        self.at(k - self.lag_b, across)
        self.at(k - self.lag_a, inward)
        if self.paired:
            self.at(k - self.lag_p, pair)
        self.at(k, lambda chunk: self.hop_e(chunk).start())


class Sizes:
    def __init__(self, slots, width, share, hidden, attn):
        self.slots, self.width, self.share = slots, width, share
        self.hidden, self.attn = hidden, attn
        self.peers = width // share
        self.pairs = attn // PAIR
        self.tile = (min(TILE_ROWS, attn), min(512, attn))
        self.pace = min(512, attn) // self.tile[0]
        shapes = [
            (hidden, width), (width, hidden), (width, hidden),
            (attn, width), (width, attn), (width, attn), (width, attn),
        ]
        self.shapes = shapes
        self.plan = []
        first = 0
        for rows, cols in shapes:
            across = cols // self.tile[1]
            count = (rows // self.tile[0]) * across
            self.plan.append((first, count, across))
            first += count
        self.total = first
        self.block_units = share // UNIT
        self.act_unit = min(512, hidden)


def partner(me, away, peers):
    place, found = 1, 0
    while place < peers:
        found += lax.rem(me // place + away // place, 2) * place
        place *= 2
    return found


class Direct:
    HOPS = 1
    NEAR = ()

    def __init__(self, sz, sems, kinds):
        self.sems, self.kinds = sems, kinds
        self.dp, self.me = lax.axis_index("dp"), lax.axis_index("tensor")
        self.others = [partner(self.me, away, sz.peers) for away in range(sz.peers)]
        self.order = list(range(sz.peers - 1, 0, -1))

    def remote(self, hop, kind, c, away, src, dst):
        row = 2 * (kind * self.HOPS + hop)
        return pltpu.make_async_remote_copy(
            src_ref=src, dst_ref=dst, send_sem=self.sems.at[row, c, away],
            recv_sem=self.sems.at[row + 1, c, away],
            device_id=(self.dp, self.others[away]), device_id_type=MESH,
        )

    def straight(self, kind, c, away):
        first, size, own, gathered = self.kinds[kind](c)
        dst = gathered.at[self.me, span(first, size), :]
        return self.remote(0, kind, c, away, own, dst)

    def start(self, kind, c):
        for away in self.order:
            self.straight(kind, c, away).start()

    def forward(self, kind, c):
        pass

    def finish(self, kind, c):
        for away in self.order:
            self.straight(kind, c, away).wait()


class Relay(Direct):
    HOPS = 2
    NEAR = (1, 2)

    def relayed(self, kind, c, away):
        first, size, _, gathered = self.kinds[kind](c)
        rows = span(first + (away - 1) * (size // 2), size // 2)
        block = gathered.at[self.others[3 - away], rows, :]
        return self.remote(1, kind, c, away, block, block)

    def start(self, kind, c):
        for away in (1, 2):
            self.straight(kind, c, away).start()

    def forward(self, kind, c):
        for away in (1, 2):
            self.straight(kind, c, away).wait_recv()
        for away in (1, 2):
            self.relayed(kind, c, away).start()

    def finish(self, kind, c):
        for away in (1, 2):
            self.straight(kind, c, away).wait_send()
            self.relayed(kind, c, away).wait()


def exchange_of(sz):
    return Relay if sz.peers == 4 else Direct


def forward_kernel(sz, *refs):
    (
        tokens_h, w_query_h, w_key_h, w_value_h, w_out_h, w_gate_h, w_up_h,
        lengths, gain_attn, gain_mlp,
        normed_h, qkv_h, mixed_h, log_h, resid_h, normed_mlp_h, hidden_h, silu_h, slope_h, stats_h,
        cosine_h, sine_h, seq_row_h,
        rows_in, w_qkv, w_out, w_mlp, normed, qkv, mixed, resid, own_resid, acts,
        log_total, row_stats, bias, cosine, sine, seq_row, load_sems, tensor_sems, dp_sems, out_sems, act_sems,
    ) = refs
    slots, width, share, peers, attn = sz.slots, sz.width, sz.share, sz.peers, sz.attn
    dp, me = lax.axis_index("dp"), lax.axis_index("tensor")
    chunks = slots // UNIT
    core, z_odd = lax.rem(dp, 2), lax.rem(dp // 2, 2)
    sibling, twin = dp + 1 - 2 * core, dp + 2 - 4 * z_odd
    quarter = attn // 4

    def part_rows(odd, of_core):
        return span((2 * odd + of_core) * quarter, quarter)

    exchange = exchange_of(sz)(
        sz,
        tensor_sems,
        (
            lambda c: (c * UNIT, UNIT, tokens_h.at[rows_of(c), :], rows_in),
            lambda c: (c * UNIT, UNIT, mixed.at[me, rows_of(c), :], mixed),
            lambda c: (
                (2 * z_odd + core) * quarter, quarter, w_out_h.at[part_rows(z_odd, core), :], w_out
            ),
        ),
    )

    def w_out_copy(step, away):
        odd = 1 - z_odd if step == 2 else z_odd
        block = w_out.at[exchange.others[away], part_rows(odd, core), :]
        return pltpu.make_async_remote_copy(
            src_ref=block, dst_ref=block, send_sem=dp_sems.at[step, 0, away],
            recv_sem=dp_sems.at[step, 1, away],
            device_id=(twin if step == 0 else sibling, me), device_id_type=MESH,
        )

    def rows_of(c):
        return pl.ds(c * UNIT, UNIT)

    def load(src, dst, index):
        return pltpu.make_async_copy(src, dst, load_sems.at[index])

    def out_copy(src, dst, index, c):
        return pltpu.make_async_copy(src, dst, out_sems.at[index, c])

    barrier = pltpu.get_barrier_semaphore()
    own_load = load(tokens_h, rows_in.at[me], 0)
    own_load.start()
    for other in exchange.others[1:]:
        pl.semaphore_signal(barrier, inc=1, device_id=(dp, other), device_id_type=MESH)
    weight_loads = [
        load(ref, w_qkv.at[i], 1 + i) for i, ref in enumerate((w_query_h, w_key_h, w_value_h))
    ] + [load(w_out_h, w_out.at[me], 4), load(w_gate_h, w_mlp.at[0], 5), load(w_up_h, w_mlp.at[1], 6)]
    for one in weight_loads:
        one.start()
    for other in (sibling, twin):
        pl.semaphore_signal(barrier, inc=1, device_id=(other, me), device_id_type=MESH)
    pl.semaphore_wait(barrier, peers + 1)
    exchange.start(2, 0)
    for c in range(min(2, chunks)):
        exchange.start(0, c)

    outs = {}

    def write(src, dst, index, c):
        outs[index, c] = out_copy(src, dst, index, c)
        outs[index, c].start()

    def project(c):
        rows = rows_of(c)
        exchange.finish(0, c)
        if c == 0:
            own_load.wait()
            for one in weight_loads[:3]:
                one.wait()
        squares = jnp.zeros((UNIT, 1), jnp.float32)
        for b in range(peers):
            squares += jnp.sum(
                jnp.square(rows_in[b, rows, :].astype(jnp.float32)), axis=1, keepdims=True
            )
        rms = lax.rsqrt(squares / width + EPSILON)
        row_stats[rows, 1:2] = rms
        for b in range(peers):
            at = pl.ds(b * share, share)
            normed[rows, at] = (
                rows_in[b, rows, :].astype(jnp.float32) * rms * gain_attn[0:1, at]
            ).astype(jnp.bfloat16)
        write(normed.at[rows, :], normed_h.at[rows, :], 0, c)
        for i in range(3):
            found = matmul(normed[rows, :], w_qkv[i])
            if i < 2:
                for p in range(sz.pairs):
                    lanes = found[:, p * PAIR : (p + 1) * PAIR]
                    qkv[i, rows, pl.ds(p * PAIR, PAIR)] = (
                        lanes * cosine[rows, :] + swap_halves(lanes) * sine[rows, :]
                    ).astype(jnp.bfloat16)
            else:
                qkv[i, rows, :] = found.astype(jnp.bfloat16)
            write(qkv.at[i, rows, :], qkv_h.at[i, rows, :], 1 + i, c)

    def attend(c):
        rows = rows_of(c)
        keys = (c + 1) * UNIT
        key_slot = lax.broadcasted_iota(jnp.int32, (keys, UNIT), 0)
        query_slot = lax.broadcasted_iota(jnp.int32, (keys, UNIT), 1) + c * UNIT
        allowed = (row_stats[pl.ds(0, keys), 2:3] == seq_row[0:1, rows]) & (key_slot <= query_slot)
        bias[pl.ds(0, keys), :] = jnp.where(allowed, 0.0, MASKED)

        @pl.loop(0, sz.pairs)
        def _(p):
            mine = span(p * PAIR, PAIR)
            query = qkv[0, rows, mine]
            key = qkv[1, pl.ds(0, keys), mine]
            value = qkv[2, pl.ds(0, keys), mine]
            first_head = lax.broadcasted_iota(jnp.int32, (1, PAIR), 1) < HDIM
            found = []
            for h in range(2):
                chosen = first_head if h == 0 else jnp.logical_not(first_head)
                scores = matmul_last(key, jnp.where(chosen, query, 0.0)) * SCALE
                scores += bias[pl.ds(0, keys), :]
                peak = jnp.max(scores, axis=0, keepdims=True)
                expon = jnp.exp(scores - peak)
                total = jnp.sum(expon, axis=0, keepdims=True)
                log_total[pl.ds(2 * p + h, 1), rows] = peak + jnp.log(total)
                weights = (expon * (1.0 / total)).astype(jnp.bfloat16)
                found.append(matmul_first(weights, value))
            mixed[me, rows, mine] = jnp.where(first_head, *found).astype(jnp.bfloat16)

        write(mixed.at[me, rows, :], mixed_h.at[rows, :], 4, c)
        if c < 2:
            exchange.start(1, c)

    def act_copies(slot, c, u):
        at = pl.ds(u * sz.act_unit, sz.act_unit)
        return [
            pltpu.make_async_copy(
                acts.at[slot, i], ref.at[rows_of(c), at], act_sems.at[slot, i]
            )
            for i, ref in enumerate((hidden_h, silu_h, slope_h))
        ]

    act_units = sz.hidden // sz.act_unit
    pending = {}

    def feed(c):
        rows = rows_of(c)
        exchange.finish(1, c)
        if c == 0:
            for one in weight_loads[3:]:
                one.wait()
        squares = jnp.zeros((UNIT, 1), jnp.float32)
        for n in range(peers):
            at = pl.ds(n * share, share)
            total = rows_in[n, rows, :].astype(jnp.float32)
            for b in range(peers):
                total += matmul(mixed[b, rows, :], w_out[b, :, at])
            resid[:, at] = total
            squares += jnp.sum(jnp.square(total), axis=1, keepdims=True)
        rms = lax.rsqrt(squares / width + EPSILON)
        row_stats[rows, 0:1] = rms
        outs.pop((0, c)).wait()
        if c > 0:
            outs.pop((5, c - 1)).wait()
        own_resid[...] = resid[:, span(me * share, share)]
        write(own_resid, resid_h.at[rows, :], 5, c)
        for b in range(peers):
            at = pl.ds(b * share, share)
            normed[rows, at] = (resid[:, at] * rms * gain_mlp[0:1, at]).astype(jnp.bfloat16)
        write(normed.at[rows, :], normed_mlp_h.at[rows, :], 6, c)
        for u in range(act_units):
            slot = (c * act_units + u) % 2
            for one in pending.pop(slot, []):
                one.wait()
            at = pl.ds(u * sz.act_unit, sz.act_unit)
            gate = matmul(normed[rows, :], w_mlp[0, :, at])
            upward = matmul(normed[rows, :], w_mlp[1, :, at])
            sigmoid = 1.0 / (1.0 + jnp.exp(-gate))
            silu = gate * sigmoid
            acts[slot, 0] = (silu * upward).astype(jnp.bfloat16)
            acts[slot, 1] = silu.astype(jnp.bfloat16)
            acts[slot, 2] = (upward * sigmoid * (1.0 + gate * (1.0 - sigmoid))).astype(jnp.bfloat16)
            pending[slot] = act_copies(slot, c, u)
            for one in pending[slot]:
                one.start()

    log_total[...] = jnp.zeros_like(log_total)

    def places(slot):
        number = start = jnp.zeros_like(slot)
        end = 0
        for j in range(lengths.shape[1]):
            end += lengths[0, j]
            passed = slot >= end
            number += passed.astype(jnp.int32)
            start += jnp.where(passed, lengths[0, j], 0)
        live = slot < end
        return jnp.where(live, number, slots + slot), jnp.where(live, slot - start, 0)

    seq_row[...] = places(lax.broadcasted_iota(jnp.int32, seq_row.shape, 1))[0].astype(jnp.float32)

    @pl.loop(0, slots // PAIR)
    def _(i):
        rows = span(i * PAIR, PAIR)
        slot = lax.broadcasted_iota(jnp.int32, (PAIR, PAIR), 0) + i * PAIR
        lane = lax.broadcasted_iota(jnp.int32, (PAIR, PAIR), 1)
        sequence, position = places(slot)
        row_stats[rows, :] = sequence.astype(jnp.float32)
        freq_index = lax.rem(lane, HDIM // 2).astype(jnp.float32)
        inverse = jnp.exp(freq_index * (-2.0 * math.log(ROPE_BASE) / HDIM))
        angles = position.astype(jnp.float32) * inverse
        cosine[rows, :] = jnp.cos(angles)
        sines = jnp.sin(angles)
        sine[rows, :] = jnp.where(lax.rem(lane, HDIM) < HDIM // 2, -sines, sines)

    for i, (src, dst) in enumerate(((cosine, cosine_h), (sine, sine_h))):
        write(src, dst, 7, 2 + i)
    write(seq_row, seq_row_h, 8, 0)
    def pass_on(kind, c):
        exchange.forward(kind, c)
        if c + 2 < chunks:
            exchange.start(kind, c + 2)

    w_peers = range(1, peers)
    def share_w_out(peers_done):
        for step in (0, 1):
            for away in peers_done:
                w_out_copy(step, away).start()

    exchange.forward(2, 0)
    share_w_out(exchange.NEAR)
    for c in range(min(2, chunks)):
        pass_on(0, c)
    exchange.finish(2, 0)
    share_w_out([away for away in w_peers if away not in exchange.NEAR])
    for c in range(chunks):
        project(c)
        attend(c)
        if c + 2 < chunks:
            pass_on(0, c + 2)
        if c == chunks - 2:
            pass_on(1, 0)
    for away in w_peers:
        w_out_copy(0, away).wait()
        w_out_copy(2, away).start()
    for away in w_peers:
        w_out_copy(1, away).wait()
        w_out_copy(2, away).wait()
    for c in range(chunks):
        if c + 1 < chunks:
            pass_on(1, c + 1)
        feed(c)
    write(log_total, log_h, 7, 0)
    write(row_stats, stats_h, 7, 1)
    for slot in list(pending):
        for one in pending.pop(slot):
            one.wait()
    for one in outs.values():
        one.wait()


def forward(sz, big, small):
    slots, width, share, attn, hidden = sz.slots, sz.width, sz.share, sz.attn, sz.hidden
    chunks = slots // UNIT
    bf16, f32 = jnp.bfloat16, jnp.float32
    shapes = [
        ((slots, width), bf16), ((3, slots, attn), bf16), ((slots, attn), bf16), ((8, slots), f32),
        ((slots, share), f32), ((slots, width), bf16), ((slots, hidden), bf16),
        ((slots, hidden), bf16), ((slots, hidden), bf16), ((slots, PAIR), f32),
        ((slots, PAIR), f32), ((slots, PAIR), f32), ((8, slots), f32),
    ]
    flops = 2 * slots * (4 * width * attn + 2 * width * hidden)
    return pl.pallas_call(
        functools.partial(forward_kernel, sz),
        out_shape=[jax.ShapeDtypeStruct(*s) for s in shapes],
        in_specs=[pl.BlockSpec(memory_space=pl.ANY)] * len(big)
        + [pl.BlockSpec(memory_space=pltpu.SMEM)]
        + [pl.BlockSpec(memory_space=pltpu.VMEM)] * (len(small) - 1),
        out_specs=[pl.BlockSpec(memory_space=pl.ANY)] * len(shapes),
        scratch_shapes=[
            pltpu.VMEM((sz.peers, slots, share), bf16),
            pltpu.VMEM((3, width, attn), bf16),
            pltpu.VMEM((sz.peers, attn, width), bf16),
            pltpu.VMEM((2, width, hidden), bf16),
            pltpu.VMEM((slots, width), bf16),
            pltpu.VMEM((3, slots, attn), bf16),
            pltpu.VMEM((sz.peers, slots, attn), bf16),
            pltpu.VMEM((UNIT, width), f32),
            pltpu.VMEM((UNIT, share), f32),
            pltpu.VMEM((2, 3, UNIT, sz.act_unit), bf16),
            pltpu.VMEM((8, slots), f32),
            pltpu.VMEM((slots, PAIR), f32),
            pltpu.VMEM((slots, UNIT), f32),
            pltpu.VMEM((slots, PAIR), f32),
            pltpu.VMEM((slots, PAIR), f32),
            pltpu.VMEM((8, slots), f32),
            pltpu.SemaphoreType.DMA((7,)),
            pltpu.SemaphoreType.DMA((6 * exchange_of(sz).HOPS, chunks, sz.peers)),
            pltpu.SemaphoreType.DMA((3, 2, sz.peers)),
            pltpu.SemaphoreType.DMA((9, chunks)),
            pltpu.SemaphoreType.DMA((2, 3)),
        ],
        compiler_params=pltpu.CompilerParams(
            collective_id=1, has_side_effects=True, vmem_limit_bytes=63 * MIB
        ),
        cost_estimate=pl.CostEstimate(
            flops=flops, bytes_accessed=60 * MIB, transcendentals=slots * slots * 8
        ),
    )(*big, *small)


def backward_kernel(sz, *refs):
    (
        hidden_h, silu_h, slope_h, cot_h, normed_mlp_h, mixed_h, normed_h, qkv_h,
        w_down_h, w_gate_h, w_up_h, w_out_h, w_query_h, w_key_h, w_value_h,
        resid_h, cosine, sine, seq_row, log_total, row_stats, gain_attn, gain_mlp,
        *refs,
    ) = refs
    outs, (grad_tokens_h, out_tokens_h, gains_h), refs = refs[:7], refs[7:10], refs[10:]
    (
        buf_a, buf_b, buf_c, d_gate, d_up, send, full, recv, d_mixed, d_qkv, w_buf, w_cols,
        acc_key, acc_value, row_part, row_send, row_recv, gains, gains_out,
        load_sems, w_sems, tensor_sems, gain_sems, *line_scratch,
    ) = refs
    slots, width, share, peers = sz.slots, sz.width, sz.share, sz.peers
    n_dp = lax.axis_size("dp")
    dp, me = lax.axis_index("dp"), lax.axis_index("tensor")
    tile_rows, tile_cols = sz.tile
    assert tile_cols == share

    def place_of(m):
        across, down = sz.plan[m][2], sz.shapes[m][0] // tile_rows
        if m == 0:
            return lambda i: (lax.rem(i, down), partner(me, i // down, peers))
        return lambda i: (i // across, lax.rem(i, across))

    places = [place_of(m) for m in range(len(sz.plan))]
    line = LineSum(
        sz.total, [(ref, plan[0], plan[1], at) for ref, plan, at in zip(outs, sz.plan, places)],
        sz.tile, line_scratch,
    )

    def load(src, dst, index):
        return pltpu.make_async_copy(src, dst, load_sems.at[index])

    def peer(away):
        return partner(me, away, peers)

    def other_dp(away):
        return lax.rem(dp + away, n_dp)

    barrier = pltpu.get_barrier_semaphore()
    own = span(me * share, share)
    first_loads = [
        load(hidden_h, buf_a.at[:, pl.ds(0, sz.hidden)], 0), load(cot_h, buf_b.at[:, own], 1),
        load(normed_mlp_h, buf_c, 2),
    ]
    for one in first_loads:
        one.start()

    def remote(kind, away, src, dst):
        return pltpu.make_async_remote_copy(
            src_ref=src, dst_ref=dst, send_sem=tensor_sems.at[2 * kind, away],
            recv_sem=tensor_sems.at[2 * kind + 1, away],
            device_id=(dp, peer(away)), device_id_type=MESH,
        )

    def send_cot(away):
        return remote(4, away, cot_h, buf_b.at[:, own])
    for away in range(1, n_dp):
        pl.semaphore_signal(
            barrier, inc=1, device_id=(other_dp(away), me), device_id_type=MESH
        )
    for away in range(1, peers):
        pl.semaphore_signal(barrier, inc=1, device_id=(dp, peer(away)), device_id_type=MESH)
    pl.semaphore_wait(barrier, n_dp - 1 + peers - 1)
    for away in range(1, peers):
        send_cot(away).start()

    attn_at = [pl.ds(i * sz.attn, sz.attn) for i in range(4)]
    grads = [
        (lambda r: buf_a[:, r], lambda c: buf_b[:, c]),
        (lambda r: buf_c[:, r], lambda c: d_gate[:, c]),
        (lambda r: buf_c[:, r], lambda c: d_up[:, c]),
        (lambda r: d_gate[:, pl.ds(pl.multiple_of(3 * sz.attn + r.start, tile_rows), tile_rows)],
         lambda c: buf_a[:, c]),
        (lambda r: buf_b[:, r], lambda c: d_qkv[2, :, c]),
        (lambda r: buf_b[:, r], lambda c: d_qkv[0, :, c]),
        (lambda r: buf_b[:, r], lambda c: d_qkv[1, :, c]),
    ]

    def cot_at(away):
        last = sz.plan[1][0] - sz.pace * (sz.hidden // UNIT // 2) - 1
        return min(away * (sz.shapes[0][0] // tile_rows), last)

    def tile_tick(m, k, work=None):
        row, col = places[m](k - sz.plan[m][0])
        rows, cols = span(row * tile_rows, tile_rows), span(col * tile_cols, tile_cols)
        if m == 0:
            for away in range(1, peers):
                @pl.when(k == cot_at(away))
                def _(away=away):
                    send_cot(away).wait()
        left, right = grads[m]
        line.put(k, matmul_first(left(rows), right(cols)))
        line.early(k)
        if work is not None:
            work()
        line.late(k)

    cursor = [0]

    def matrix_of(k):
        return [m for m, (first, count, _) in enumerate(sz.plan) if first <= k < first + count][0]

    def advance_to(stop):
        while cursor[0] < stop:
            m = matrix_of(cursor[0])
            until = min(stop, sz.plan[m][0] + sz.plan[m][1])

            @pl.loop(cursor[0], until)
            def _(k, m=m):
                tile_tick(m, k)

            cursor[0] = until

    def run_units(count, unit, group=1):
        ticks = group * sz.pace
        done = 0
        while done < count:
            m = matrix_of(cursor[0])
            room = (sz.plan[m][0] + sz.plan[m][1] - cursor[0]) // ticks
            if not room:
                for g in range(group):
                    for t in range(sz.pace):
                        work = functools.partial(unit, done, g) if t == 0 else None
                        tile_tick(matrix_of(cursor[0]), cursor[0], work)
                        cursor[0] += 1
                done += 1
                continue
            step = min(room, count - done)

            @pl.loop(0, step)
            def _(i, m=m, done=done, start=cursor[0]):
                for g in range(group):
                    for t in range(sz.pace):
                        work = functools.partial(unit, done + i, g) if t == 0 else None
                        tile_tick(m, start + i * ticks + g * sz.pace + t, work)

            cursor[0] += step * ticks
            done += step

    order = list(range(peers - 1, 0, -1)) + [0]

    def block_of(u):
        return partner(me, peers - 1 - u // sz.block_units, peers)

    def feature(u):
        return block_of(u) * share + lax.rem(u, sz.block_units) * UNIT

    def scatter(round_, away):
        dst = full.at[me] if round_ == 2 else recv.at[away - 1]
        return remote(round_, away, send.at[peer(away)], dst)

    def store_part(round_, u, value):
        send[block_of(u), :, span(lax.rem(u, sz.block_units) * UNIT, UNIT)] = value.astype(
            jnp.bfloat16
        )
        for i, away in enumerate(order[:-1] if round_ != 1 else ()):
            @pl.when(u == (i + 1) * sz.block_units - 1)
            def _(away=away):
                scatter(round_, away).start()

    mlp_units = width // UNIT
    hid = pl.ds(0, sz.hidden)

    def prefetched(count, loads, u):
        for one in loads(u):
            one.wait()

        @pl.when(u + 1 < count)
        def _():
            for one in loads(u + 1):
                one.start()

    def hidden_loads(u):
        cols = span(u * UNIT, UNIT)
        slot = lax.rem(u, 2)
        return (
            pltpu.make_async_copy(w_down_h.at[cols, :], w_buf.at[slot, 0], w_sems.at[0, slot]),
            pltpu.make_async_copy(
                silu_h.at[:, cols], d_qkv.at[slot, :, pl.ds(0, UNIT)], w_sems.at[1, slot]
            ),
            pltpu.make_async_copy(
                slope_h.at[:, cols], d_qkv.at[slot, :, pl.ds(UNIT, UNIT)], w_sems.at[2, slot]
            ),
        )

    def hidden_unit(u, _):
        prefetched(sz.hidden // UNIT, hidden_loads, u)
        slot = lax.rem(u, 2)
        cols = span(u * UNIT, UNIT)
        d_hidden = matmul_last(buf_b[...], w_buf[slot, 0])
        d_up[:, cols] = (d_hidden * d_qkv[slot, :, pl.ds(0, UNIT)]).astype(jnp.bfloat16)
        d_gate[:, cols] = (d_hidden * d_qkv[slot, :, pl.ds(UNIT, UNIT)]).astype(jnp.bfloat16)

    def twice(unit):
        def both(u, g):
            unit(2 * u, g)
            unit(2 * u + 1, g)

        return both

    for one in hidden_loads(0):
        one.start()
    for one in first_loads[:2]:
        one.wait()
    advance_to(sz.plan[1][0] - sz.pace * (sz.hidden // UNIT // 2))
    run_units(sz.hidden // UNIT // 2, twice(hidden_unit))
    first_loads[2].wait()

    def gather(round_):
        for away in range(1, peers):
            scatter(round_, away).wait()

    def gathered(round_, rows):
        total = send[me, rows, :].astype(jnp.float32)
        for away in range(1, peers):
            block = full[peer(away), rows, :] if round_ == 2 else recv[away - 1, rows, :]
            total += block.astype(jnp.float32)
        return total

    def mlp_loads(u):
        slot = lax.rem(u, 2)
        rows = span(feature(u), UNIT)
        return (
            pltpu.make_async_copy(
                w_gate_h.at[rows, :], w_buf.at[slot, 0, :, hid], w_sems.at[0, slot]
            ),
            pltpu.make_async_copy(
                w_up_h.at[rows, :], w_buf.at[slot, 1, :, hid], w_sems.at[1, slot]
            ),
        )

    def mlp_unit(u, _):
        prefetched(mlp_units, mlp_loads, u)
        slot = lax.rem(u, 2)
        part = matmul_last(d_gate[...], w_buf[slot, 0, :, hid])
        part += matmul_last(d_up[...], w_buf[slot, 1, :, hid])
        store_part(0, u, part)

    for one in mlp_loads(0):
        one.start()
    run_units(mlp_units, mlp_unit)
    advance_to(cursor[0] + 4 * sz.pace)

    def spread(away):
        return remote(3, away, full.at[me], full.at[me])

    w_out_rows = sz.attn // UNIT
    w_out_loads = [
        load(w_out_h.at[pl.ds(i * UNIT, UNIT), :], w_buf.at[0, i], 3 + i) for i in range(w_out_rows)
    ]
    for one in w_out_loads:
        one.start()
    gather(0)

    @pl.loop(0, slots // UNIT)
    def _(i):
        full[me, span(i * UNIT, UNIT), :] = gathered(0, span(i * UNIT, UNIT)).astype(jnp.bfloat16)

    for away in range(1, peers):
        spread(away).start()
    advance_to(sz.plan[2][0])

    hidden_load = load(hidden_h, d_gate, 0)
    hidden_load.start()

    def out_loads(u):
        slot = lax.rem(u, 2)
        return [
            pltpu.make_async_copy(
                w_down_h.at[:, span(feature(u), UNIT)], w_cols.at[slot], w_sems.at[0, slot]
            )
        ]

    def out_unit(u, _):
        prefetched(mlp_units, out_loads, u)
        store_part(1, u, matmul(d_gate[...], w_cols[lax.rem(u, 2)]))

    for one in out_loads(0):
        one.start()
    hidden_load.wait()
    run_units(mlp_units // 2, twice(out_unit))

    for away in range(1, peers):
        spread(away).wait()
    for one in w_out_loads:
        one.wait()

    gains[dp] = jnp.zeros_like(gains[dp])

    def norm_unit(u, _):
        rows = span(u * UNIT, UNIT)
        row_sum = jnp.zeros((UNIT, 1), jnp.float32)
        for b in range(peers):
            at = pl.ds(b * share, share)
            row_sum += jnp.sum(
                full[b, rows, :].astype(jnp.float32) * buf_c[rows, at].astype(jnp.float32),
                axis=1, keepdims=True,
            )
        rms = row_stats[rows, 0:1]
        for b in range(peers):
            at = pl.ds(b * share, share)
            gain = gain_mlp[0:1, at]
            lean = buf_c[rows, at].astype(jnp.float32) / gain * (row_sum / width)
            d_resid = buf_b[rows, at].astype(jnp.float32) + rms * (
                gain * full[b, rows, :].astype(jnp.float32) - lean
            )
            buf_a[rows, at] = d_resid.astype(jnp.bfloat16)
        gains[dp, 0:1, :] += jnp.sum(
            full[me, rows, :].astype(jnp.float32) * buf_c[rows, own].astype(jnp.float32),
            axis=0, keepdims=True,
        ) / gain_mlp[0:1, own]
        for i in range(w_out_rows):
            d_mixed[rows, pl.ds(i * UNIT, UNIT)] = matmul_last(
                buf_a[rows, :], w_buf[0, i]
            ).astype(jnp.bfloat16)

    run_units(slots // UNIT, norm_unit)
    for away in range(1, peers):
        scatter(1, away).start()

    attn_loads = [
        load(ref, d_gate.at[:, attn_at[i]], 5 + i)
        for i, ref in enumerate((qkv_h.at[0], qkv_h.at[1], qkv_h.at[2], mixed_h))
    ] + [load(normed_h, buf_b, 9)]
    for one in attn_loads:
        one.start()
    for one in attn_loads:
        one.wait()
    blocks = slots // UNIT

    def attend_unit(p, i):
        rows = pl.ds(i * UNIT, UNIT)
        keys = (i + 1) * UNIT
        lanes = [pl.ds(pl.multiple_of(j * sz.attn + p * PAIR, PAIR), PAIR) for j in range(3)]
        mine = span(p * PAIR, PAIR)
        query = d_gate[rows, lanes[0]]
        key = d_gate[pl.ds(0, keys), lanes[1]]
        value = d_gate[pl.ds(0, keys), lanes[2]]
        grad = d_mixed[rows, mine]
        first_head = lax.broadcasted_iota(jnp.int32, (1, PAIR), 1) < HDIM
        key_slot = lax.broadcasted_iota(jnp.int32, (keys, UNIT), 0)
        query_slot = lax.broadcasted_iota(jnp.int32, (keys, UNIT), 1) + i * UNIT
        allowed = (row_stats[pl.ds(0, keys), 2:3] == seq_row[0:1, rows]) & (key_slot <= query_slot)
        found = []
        for h in range(2):
            chosen = first_head if h == 0 else jnp.logical_not(first_head)
            scores = matmul_last(key, jnp.where(chosen, query, 0.0)) * SCALE
            scores -= log_total[pl.ds(2 * p + h, 1), rows]
            probs = jnp.exp(jnp.where(allowed, scores, MASKED))
            grad_probs = matmul_last(value, jnp.where(chosen, grad, 0.0))
            delta = jnp.sum(probs * grad_probs, axis=0, keepdims=True)
            grad_scores = (probs * (grad_probs - delta)).astype(jnp.bfloat16)
            found.append(
                (
                    matmul_first(grad_scores, key),
                    matmul(grad_scores, query),
                    matmul(probs.astype(jnp.bfloat16), grad),
                )
            )
        grad_query, grad_key, grad_value = [
            jnp.where(first_head, one, two) for one, two in zip(*found)
        ]
        d_qkv[0, rows, mine] = rotate_back(
            grad_query * SCALE, cosine[rows, :], sine[rows, :]
        ).astype(jnp.bfloat16)
        for acc, part in ((acc_key, grad_key), (acc_value, grad_value)):
            if i > 0:
                acc[pl.ds(0, keys - UNIT), :] += part[: keys - UNIT]
            acc[pl.ds(keys - UNIT, UNIT), :] = part[keys - UNIT :]
        if i + 1 == blocks:
            d_qkv[1, :, mine] = rotate_back(acc_key[...] * SCALE, cosine[...], sine[...]).astype(
                jnp.bfloat16
            )
            d_qkv[2, :, mine] = acc_value[...].astype(jnp.bfloat16)

    steps = [(0, 1), (2,), (3,)] if blocks == 4 else [(i,) for i in range(blocks)]

    def attend_step(p, g):
        for i in steps[g]:
            attend_unit(p, i)

    run_units(sz.pairs, attend_step, len(steps))
    advance_to(sz.plan[4][0])

    gather(1)
    for j in range(share // PAIR):
        lanes = pl.ds(j * PAIR, PAIR)
        piece = load(resid_h.at[:, lanes], acc_key, 2)
        piece.start()
        piece.wait()

        @pl.loop(0, slots // UNIT)
        def _(i, lanes=lanes):
            rows = span(i * UNIT, UNIT)
            total = acc_key[rows, :] + send[me, rows, lanes].astype(jnp.float32)
            for away in range(1, peers):
                total += recv[away - 1, rows, lanes].astype(jnp.float32)
            send[me, rows, lanes] = total.astype(jnp.bfloat16)

    tokens_out = load(send.at[me], out_tokens_h, 0)
    tokens_out.start()

    row_part[...] = jnp.zeros_like(row_part)

    def attn_loads_of(u):
        slot = lax.rem(u, 2)
        rows = span(feature(u), UNIT)
        return [
            pltpu.make_async_copy(ref.at[rows, :], w_buf.at[slot, 0, :, at], w_sems.at[i, slot])
            for i, (ref, at) in enumerate(zip((w_query_h, w_key_h, w_value_h), attn_at))
        ]

    def attn_unit(u, _):
        prefetched(mlp_units, attn_loads_of, u)
        slot = lax.rem(u, 2)
        part = jnp.zeros((slots, UNIT), jnp.float32)
        for i in range(3):
            part += matmul_last(d_qkv[i, :, pl.ds(0, sz.attn)], w_buf[slot, 0, :, attn_at[i]])
        store_part(2, u, part)
        row_part[...] += jnp.sum(
            part * buf_b[:, span(feature(u), UNIT)].astype(jnp.float32), axis=1, keepdims=True
        )

    def row_scatter(away):
        return remote(5, away, row_send, row_recv.at[away - 1])

    for one in attn_loads_of(0):
        one.start()

    tokens_out.wait()
    run_units(mlp_units // 2, twice(attn_unit))
    row_send[...] = row_part[...].T[0:8, :]
    for away in range(1, peers):
        row_scatter(away).start()
    advance_to(sz.total - 2 * sz.pace)
    gather(2)
    for away in range(1, peers):
        row_scatter(away).wait()
    row_sums = row_send[...]
    for away in range(1, peers):
        row_sums += row_recv[away - 1]
    row_part[...] = jnp.concatenate([row_sums] * (row_part.shape[1] // 8), axis=0).T

    def last_unit(u, _):
        rows = span(u * UNIT, UNIT)
        d_own = gathered(2, rows)
        straight = buf_b[rows, own].astype(jnp.float32)
        gain = gain_attn[0:1, own]
        gains[dp, 1:2, :] += jnp.sum(d_own * straight, axis=0, keepdims=True) / gain
        lean = straight / gain * (row_part[rows, 0:1] / width)
        send[me, rows, :] = (
            buf_a[rows, own].astype(jnp.float32) + row_stats[rows, 1:2] * (gain * d_own - lean)
        ).astype(jnp.bfloat16)

    run_units(slots // UNIT // 2, twice(last_unit))
    grad_out = load(send.at[me], grad_tokens_h, 10)
    grad_out.start()

    def gain_copy(away):
        return pltpu.make_async_remote_copy(
            src_ref=gains.at[dp], dst_ref=gains.at[dp],
            send_sem=gain_sems.at[0, away], recv_sem=gain_sems.at[1, away],
            device_id=(other_dp(away), me), device_id_type=MESH,
        )

    for away in range(1, n_dp):
        gain_copy(away).start()

    @pl.loop(sz.total, sz.total + line.length)
    def _(k):
        line.early(k)
        line.late(k)

    for away in range(1, n_dp):
        gain_copy(away).wait()
    total = gains[0]
    for i in range(1, n_dp):
        total += gains[i]
    gains_out[...] = total
    gain_out = load(gains_out, gains_h, 11)
    gain_out.start()

    grad_out.wait()
    gain_out.wait()


def backward(sz, big, small):
    whole_rows = pltpu.VMEM((sz.slots, sz.width), jnp.bfloat16)
    hidden_rows = pltpu.VMEM((sz.slots, sz.hidden), jnp.bfloat16)
    assert sz.hidden == 4 * sz.attn and sz.share % UNIT == 0 and sz.hidden <= sz.width
    n_dp = lax.axis_size("dp")
    attn_rows = max(sz.attn, 2 * UNIT)
    flops = 6 * sz.slots * (3 * sz.width * sz.hidden + 4 * sz.width * sz.attn)
    return pl.pallas_call(
        functools.partial(backward_kernel, sz),
        out_shape=[jax.ShapeDtypeStruct(s, jnp.bfloat16) for s in sz.shapes]
        + [
            jax.ShapeDtypeStruct((sz.slots, sz.share), jnp.bfloat16),
            jax.ShapeDtypeStruct((sz.slots, sz.share), jnp.bfloat16),
            jax.ShapeDtypeStruct((8, sz.share), jnp.float32),
        ],
        in_specs=[pl.BlockSpec(memory_space=pl.ANY)] * len(big)
        + [pl.BlockSpec(memory_space=pltpu.VMEM)] * len(small),
        out_specs=[pl.BlockSpec(memory_space=pl.ANY)] * 10,
        scratch_shapes=[
            whole_rows, whole_rows, whole_rows, hidden_rows, hidden_rows,
            pltpu.VMEM((sz.peers, sz.slots, sz.share), jnp.bfloat16),
            pltpu.VMEM((sz.peers, sz.slots, sz.share), jnp.bfloat16),
            pltpu.VMEM((sz.peers - 1, sz.slots, sz.share), jnp.bfloat16),
            pltpu.VMEM((sz.slots, sz.attn), jnp.bfloat16),
            pltpu.VMEM((3, sz.slots, attn_rows), jnp.bfloat16),
            pltpu.VMEM((2, 2, UNIT, sz.width), jnp.bfloat16),
            pltpu.VMEM((2, sz.hidden, UNIT), jnp.bfloat16),
            pltpu.VMEM((sz.slots, PAIR), jnp.float32),
            pltpu.VMEM((sz.slots, PAIR), jnp.float32),
            pltpu.VMEM((sz.slots, PAIR), jnp.float32),
            pltpu.VMEM((8, sz.slots), jnp.float32),
            pltpu.VMEM((sz.peers - 1, 8, sz.slots), jnp.float32),
            pltpu.VMEM((n_dp, 8, sz.share), jnp.float32),
            pltpu.VMEM((8, sz.share), jnp.float32),
            pltpu.SemaphoreType.DMA((12,)),
            pltpu.SemaphoreType.DMA((3, 2)),
            pltpu.SemaphoreType.DMA((12, sz.peers)),
            pltpu.SemaphoreType.DMA((2, n_dp)),
        ]
        + LineSum.scratch_shapes(sz.tile),
        compiler_params=pltpu.CompilerParams(
            collective_id=0, has_side_effects=True, vmem_limit_bytes=63 * MIB
        ),
        cost_estimate=pl.CostEstimate(
            flops=flops, bytes_accessed=200 * MIB, transcendentals=sz.slots * sz.slots * 8
        ),
    )(*big, *small)


def widen_kernel(steps, depth, *refs):
    count = 1 + max(i for i, _, _ in steps)
    sources, moved, gains, refs = refs[:count], refs[count : count + 2], refs[count + 2], refs[count + 3 :]
    results, moved_to, gains_to = refs[:count], refs[count : count + 2], refs[count + 2 : count + 4]
    narrow, wide, held, in_sems, out_sems, move_sems = refs[count + 4 :]
    moves_in = [
        pltpu.make_async_copy(src, held.at[i], move_sems.at[0, i]) for i, src in enumerate(moved)
    ]
    moves_out = [
        pltpu.make_async_copy(held.at[i], dst, move_sems.at[1, i])
        for i, dst in enumerate(moved_to)
    ]
    for one in moves_in:
        one.start()
    gains_to[0][...] = gains[1, :]
    gains_to[1][...] = gains[0, :]

    def read(n):
        i, first, rows = steps[n]
        cols = sources[i].shape[1]
        slot = n % depth
        return pltpu.make_async_copy(
            sources[i].at[pl.ds(first, rows), :],
            narrow[cols].at[slot, pl.ds(0, rows), :], in_sems.at[slot],
        )

    def write(n):
        i, first, rows = steps[n]
        cols = sources[i].shape[1]
        slot = n % depth
        return pltpu.make_async_copy(
            wide[cols].at[slot, pl.ds(0, rows), :],
            results[i].at[pl.ds(first, rows), :], out_sems.at[slot],
        )

    for n in range(min(depth, len(steps))):
        read(n).start()
    for n, (i, _, rows) in enumerate(steps):
        cols = sources[i].shape[1]
        slot = n % depth
        read(n).wait()
        if n == len(steps) // 2:
            for one, then in zip(moves_in, moves_out):
                one.wait()
                then.start()
        if n >= depth:
            write(n - depth).wait()
        strip = min(rows, 32 * 2048 // cols)

        @pl.loop(0, rows // strip)
        def _(r, cols=cols, slot=slot, strip=strip):
            at = span(r * strip, strip)
            wide[cols][slot, at, :] = narrow[cols][slot, at, :].astype(jnp.float32)

        write(n).start()
        if n + depth < len(steps):
            read(n + depth).start()
    for n in range(max(0, len(steps) - depth), len(steps)):
        write(n).wait()
    for one in moves_out:
        one.wait()


def widen(arrays, moved, gains):
    depth = 4
    block = 512 * 1024
    steps, most = [], {}
    for i, (rows, cols) in enumerate(a.shape for a in arrays):
        step = min(rows, block // cols)
        most[cols] = max(step, most.get(cols, 0))
        steps += [(i, first, step) for first in range(0, rows, step)]
    return pl.pallas_call(
        functools.partial(widen_kernel, steps, depth),
        out_shape=[jax.ShapeDtypeStruct(a.shape, jnp.float32) for a in arrays]
        + [jax.ShapeDtypeStruct(a.shape, a.dtype) for a in moved]
        + [jax.ShapeDtypeStruct(gains.shape[1:], gains.dtype)] * 2,
        in_specs=[pl.BlockSpec(memory_space=pl.ANY)] * (len(arrays) + 2)
        + [pl.BlockSpec(memory_space=pltpu.VMEM)],
        out_specs=[pl.BlockSpec(memory_space=pl.ANY)] * (len(arrays) + 2)
        + [pl.BlockSpec(memory_space=pltpu.VMEM)] * 2,
        scratch_shapes=[
            {cols: pltpu.VMEM((depth, rows, cols), jnp.bfloat16) for cols, rows in most.items()},
            {cols: pltpu.VMEM((depth, rows, cols), jnp.float32) for cols, rows in most.items()},
            pltpu.VMEM((2,) + moved[0].shape, moved[0].dtype),
            pltpu.SemaphoreType.DMA((depth,)),
            pltpu.SemaphoreType.DMA((depth,)),
            pltpu.SemaphoreType.DMA((2, 2)),
        ],
        compiler_params=pltpu.CompilerParams(vmem_limit_bytes=63 * MIB),
        cost_estimate=pl.CostEstimate(flops=0, bytes_accessed=96 * MIB, transcendentals=0),
    )(*arrays, *moved, gains)


def body(
    tokens,
    norm_gain_attn,
    norm_gain_mlp,
    w_query,
    w_key,
    w_value,
    w_out,
    w_gate,
    w_up,
    w_down,
    cotangent,
    lengths,
):
    slot_count = tokens.shape[0]
    share_width = tokens.shape[1]
    model_width = share_width * lax.axis_size("tensor")
    attn_width = w_query.shape[1]
    sz = Sizes(slot_count, model_width, share_width, w_gate.shape[1], attn_width)
    gain_attn = norm_gain_attn.reshape(1, model_width)
    gain_mlp = norm_gain_mlp.reshape(1, model_width)
    (
        normed, qkv, mixed, log_total, resid_here, normed_mlp, hidden, silu, slope, row_stats,
        cosine, sine, seq_row,
    ) = forward(
        sz, (tokens, w_query, w_key, w_value, w_out, w_gate, w_up), (lengths, gain_attn, gain_mlp)
    )
    down, gate, up, out, value, query, key, grad_tokens, out_tokens, gains = backward(
        sz,
        (
            hidden, silu, slope, cotangent, normed_mlp, mixed, normed, qkv,
            w_down, w_gate, w_up, w_out, w_query, w_key, w_value, resid_here,
        ),
        (cosine, sine, seq_row, log_total, row_stats, gain_attn, gain_mlp),
    )

    down, gate, up, out, value, query, key, grad_tokens, out_tokens, gain_attn, gain_mlp = widen(
        [down, gate, up, out, value, query, key], [grad_tokens, out_tokens], gains
    )
    return (
        out_tokens, grad_tokens, gain_attn, gain_mlp, query, key, value, out, gate, up, down,
    )


def solution(mesh):
    placed = (
        P("dp", "tensor"),
        P(),
        P(),
        P(None, "tensor"),
        P(None, "tensor"),
        P(None, "tensor"),
        P("tensor", None),
        P(None, "tensor"),
        P(None, "tensor"),
        P("tensor", None),
        P("dp", "tensor"),
        P("dp", None),
    )
    return jax.shard_map(
        body,
        mesh=mesh,
        in_specs=placed,
        out_specs=(
            P("dp", "tensor"),
            P("dp", "tensor"),
            P("tensor"),
            P("tensor"),
            P(None, "tensor"),
            P(None, "tensor"),
            P(None, "tensor"),
            P("tensor", None),
            P(None, "tensor"),
            P(None, "tensor"),
            P("tensor", None),
        ),
        check_vma=False,
    )
```

```python
import functools
import math

import jax
import jax.numpy as jnp
from jax import lax
from jax.experimental import pallas as pl
from jax.experimental.pallas import tpu as pltpu
from jax.sharding import PartitionSpec as P

HDIM = 64
PAIR = 2 * HDIM


EPSILON = 1e-05
ROPE_BASE = 130000.0
SCALE = HDIM ** (-0.5)
MASKED = -1e30
MESH = pl.DeviceIdType.MESH
HOP_LAG = 2
TILE_ROWS = 512
UNIT = 256
MIB = 1024 * 1024


def matmul_first(left, right):
    return lax.dot_general(
        left, right, (((0,), (0,)), ((), ())), preferred_element_type=jnp.float32
    )


def matmul_last(left, right):
    return lax.dot_general(
        left, right, (((1,), (1,)), ((), ())), preferred_element_type=jnp.float32
    )


def matmul(left, right):
    return jnp.dot(left, right, preferred_element_type=jnp.float32)


def span(first, size):
    return pl.ds(pl.multiple_of(first, size), size)


def swap_halves(values):
    lane = lax.broadcasted_iota(jnp.int32, values.shape, 1)
    ahead = pltpu.roll(values, PAIR - HDIM // 2, 1)
    behind = pltpu.roll(values, HDIM // 2, 1)
    return jnp.where(lax.rem(lane, HDIM) < HDIM // 2, ahead, behind)


def rotate_back(values, cosine, sine):
    return values * cosine - swap_halves(values) * sine


class LineSum:
    SLOTS = (
        2, 2, HOP_LAG, 3 * HOP_LAG, HOP_LAG, 2 * HOP_LAG, 3 * HOP_LAG + 2, 3, HOP_LAG, 2 * HOP_LAG,
    )
    SIGNALS = 16

    def __init__(self, total, outs, tile, scratch):
        self.paired = lax.axis_size("dp") == 16
        assert lax.axis_size("dp") in (8, 16)
        self.lag_p = 1
        self.lag_a = 1 + HOP_LAG * self.paired
        self.lag_b = self.lag_a + HOP_LAG
        self.lag_c = self.lag_b + HOP_LAG
        self.lag_f = self.lag_c + HOP_LAG
        self.lag_o = self.lag_f + 1
        self.lag_d = self.lag_o + 1
        self.length = self.lag_d
        self.total = total
        self.outs = outs
        self.tile_rows, self.tile_cols = tile
        self.half = self.tile_rows // 2
        (
            self.stage, self.r_e, self.s_one, self.r_a, self.s_two, self.r_b, self.tot, self.r_f,
            self.s_zero, self.r_p, self.sems, self.out_sems,
        ) = scratch
        dp = lax.axis_index("dp")
        self.tensor = lax.axis_index("tensor")
        self.core = lax.rem(dp, 2)
        z = lax.rem(dp // 2, 4)
        self.is_end = (z == 0) | (z == 3)
        self.is_mid = jnp.logical_not(self.is_end)
        self.sibling = dp + 1 - 2 * self.core
        self.near = dp + jnp.where((z == 0) | (z == 2), 2, -2)
        self.across = dp + 6 - 4 * z
        self.twin = lax.rem(dp + 8, lax.axis_size("dp"))

    @classmethod
    def scratch_shapes(cls, tile):
        rows, cols = tile
        buffers = [
            pltpu.VMEM(
                (slots, 2, rows // 2, cols) if i == 0 else (slots, rows // 2, cols), jnp.bfloat16
            )
            for i, slots in enumerate(cls.SLOTS)
        ]
        if lax.axis_size("dp") != 16:
            buffers[8] = buffers[9] = pltpu.VMEM((1, 8, 128), jnp.bfloat16)
        return buffers + [
            pltpu.SemaphoreType.DMA((12, cls.SIGNALS)),
            pltpu.SemaphoreType.DMA((2, cls.SIGNALS)),
        ]

    def copy(self, hop, chunk, src, dst, target):
        slot = lax.rem(chunk, self.SIGNALS)
        return pltpu.make_async_remote_copy(
            src_ref=src, dst_ref=dst, send_sem=self.sems.at[2 * hop, slot],
            recv_sem=self.sems.at[2 * hop + 1, slot],
            device_id=(target, self.tensor), device_id_type=MESH,
        )

    @staticmethod
    def slot(ref, chunk):
        return ref.at[lax.rem(chunk, ref.shape[0])]

    def hop_e(self, chunk):
        src = self.stage.at[lax.rem(chunk, self.stage.shape[0]), 1 - self.core]
        return self.copy(0, chunk, src, self.slot(self.r_e, chunk), self.sibling)

    def hop_a(self, chunk):
        return self.copy(
            1, chunk, self.slot(self.s_one, chunk), self.slot(self.r_a, chunk), self.near
        )

    def hop_b(self, chunk):
        return self.copy(
            2, chunk, self.slot(self.s_two, chunk), self.slot(self.r_b, chunk), self.across
        )

    def hop_c(self, chunk):
        return self.copy(
            3, chunk, self.slot(self.tot, chunk), self.slot(self.tot, chunk), self.near
        )

    def hop_f(self, chunk):
        return self.copy(
            4, chunk, self.slot(self.tot, chunk), self.slot(self.r_f, chunk), self.sibling
        )

    def hop_p(self, chunk):
        return self.copy(
            5, chunk, self.slot(self.s_zero, chunk), self.slot(self.r_p, chunk), self.twin
        )

    def out_copies(self, chunk, ref, tile_row, tile_col):
        cols = span(tile_col * self.tile_cols, self.tile_cols)
        first = tile_row * self.tile_rows
        mine = span(first + self.core * self.half, self.half)
        other = span(first + (1 - self.core) * self.half, self.half)
        slot = lax.rem(chunk, self.SIGNALS)
        return (
            pltpu.make_async_copy(
                self.slot(self.tot, chunk), ref.at[mine, cols], self.out_sems.at[0, slot]
            ),
            pltpu.make_async_copy(
                self.slot(self.r_f, chunk), ref.at[other, cols], self.out_sems.at[1, slot]
            ),
        )

    def on_out(self, chunk, act):
        for ref, first, count, place in self.outs:
            local = chunk - first

            @pl.when((local >= 0) & (local < count))
            def _(ref=ref, local=local, place=place):
                for one in self.out_copies(chunk, ref, *place(local)):
                    act(one)

    def at(self, chunk, work):
        @pl.when((chunk >= 0) & (chunk < self.total))
        def _():
            work(chunk)

    def put(self, chunk, value):
        self.stage[lax.rem(chunk, self.stage.shape[0])] = value.astype(jnp.bfloat16).reshape(
            2, self.half, self.tile_cols
        )

    def add(self, into, left, right, chunk):
        total = self.slot(left, chunk)[...].astype(jnp.float32)
        total += self.slot(right, chunk)[...].astype(jnp.float32)
        self.slot(into, chunk)[...] = total.astype(jnp.bfloat16)

    def join_cores(self, into, chunk):
        self.hop_e(chunk).wait()
        total = self.stage[lax.rem(chunk, self.stage.shape[0]), self.core].astype(jnp.float32)
        total += self.slot(self.r_e, chunk)[...].astype(jnp.float32)
        self.slot(into, chunk)[...] = total.astype(jnp.bfloat16)

    def late(self, k):
        pass

    def early(self, k):
        def drop(chunk):
            self.on_out(chunk, lambda one: one.wait())

        def out(chunk):
            self.hop_f(chunk).wait()
            self.on_out(chunk, lambda one: one.start())

        def final(chunk):
            @pl.when(self.is_end)
            def _():
                self.hop_c(chunk).wait_recv()

            @pl.when(self.is_mid)
            def _():
                self.hop_c(chunk).wait_send()

            self.hop_f(chunk).start()

        def back(chunk):
            @pl.when(self.is_mid)
            def _():
                self.hop_b(chunk).wait()
                self.add(self.tot, self.s_two, self.r_b, chunk)
                self.hop_c(chunk).start()

        def across(chunk):
            @pl.when(self.is_mid)
            def _():
                self.hop_a(chunk).wait_recv()
                self.add(self.s_two, self.s_one, self.r_a, chunk)
                self.hop_b(chunk).start()

            @pl.when(self.is_end)
            def _():
                self.hop_a(chunk).wait_send()

        def inward(chunk):
            if self.paired:
                self.hop_p(chunk).wait()
                self.add(self.s_one, self.s_zero, self.r_p, chunk)
            else:
                self.join_cores(self.s_one, chunk)

            @pl.when(self.is_end)
            def _():
                self.hop_a(chunk).start()

        def pair(chunk):
            self.join_cores(self.s_zero, chunk)
            self.hop_p(chunk).start()

        self.at(k - self.lag_d, drop)
        self.at(k - self.lag_o, out)
        self.at(k - self.lag_f, final)
        self.at(k - self.lag_c, back)
        self.at(k - self.lag_b, across)
        self.at(k - self.lag_a, inward)
        if self.paired:
            self.at(k - self.lag_p, pair)
        self.at(k, lambda chunk: self.hop_e(chunk).start())


class Sizes:
    def __init__(self, slots, width, share, hidden, attn):
        self.slots, self.width, self.share = slots, width, share
        self.hidden, self.attn = hidden, attn
        self.peers = width // share
        self.pairs = attn // PAIR
        self.tile = (min(TILE_ROWS, attn), min(512, attn))
        self.pace = min(512, attn) // self.tile[0]
        shapes = [
            (hidden, width), (width, hidden), (width, hidden),
            (attn, width), (width, attn), (width, attn), (width, attn),
        ]
        self.shapes = shapes
        self.plan = []
        first = 0
        for rows, cols in shapes:
            across = cols // self.tile[1]
            count = (rows // self.tile[0]) * across
            self.plan.append((first, count, across))
            first += count
        self.total = first
        self.block_units = share // UNIT
        self.act_unit = min(512, hidden)


def partner(me, away, peers):
    place, found = 1, 0
    while place < peers:
        found += lax.rem(me // place + away // place, 2) * place
        place *= 2
    return found


class Direct:
    HOPS = 1
    NEAR = ()

    def __init__(self, sz, sems, kinds):
        self.sems, self.kinds = sems, kinds
        self.dp, self.me = lax.axis_index("dp"), lax.axis_index("tensor")
        self.others = [partner(self.me, away, sz.peers) for away in range(sz.peers)]
        self.order = list(range(sz.peers - 1, 0, -1))

    def remote(self, hop, kind, c, away, src, dst):
        row = 2 * (kind * self.HOPS + hop)
        return pltpu.make_async_remote_copy(
            src_ref=src, dst_ref=dst, send_sem=self.sems.at[row, c, away],
            recv_sem=self.sems.at[row + 1, c, away],
            device_id=(self.dp, self.others[away]), device_id_type=MESH,
        )

    def straight(self, kind, c, away):
        first, size, own, gathered = self.kinds[kind](c)
        dst = gathered.at[self.me, span(first, size), :]
        return self.remote(0, kind, c, away, own, dst)

    def start(self, kind, c):
        for away in self.order:
            self.straight(kind, c, away).start()

    def forward(self, kind, c):
        pass

    def finish(self, kind, c):
        for away in self.order:
            self.straight(kind, c, away).wait()


class Relay(Direct):
    HOPS = 2
    NEAR = (1, 2)

    def relayed(self, kind, c, away):
        first, size, _, gathered = self.kinds[kind](c)
        rows = span(first + (away - 1) * (size // 2), size // 2)
        block = gathered.at[self.others[3 - away], rows, :]
        return self.remote(1, kind, c, away, block, block)

    def start(self, kind, c):
        for away in (1, 2):
            self.straight(kind, c, away).start()

    def forward(self, kind, c):
        for away in (1, 2):
            self.straight(kind, c, away).wait_recv()
        for away in (1, 2):
            self.relayed(kind, c, away).start()

    def finish(self, kind, c):
        for away in (1, 2):
            self.straight(kind, c, away).wait_send()
            self.relayed(kind, c, away).wait()


def exchange_of(sz):
    return Relay if sz.peers == 4 else Direct


def forward_kernel(sz, *refs):
    (
        tokens_h, w_query_h, w_key_h, w_value_h, w_out_h, w_gate_h, w_up_h,
        lengths, gain_attn, gain_mlp,
        normed_h, qkv_h, mixed_h, log_h, resid_h, normed_mlp_h, hidden_h, silu_h, slope_h, stats_h,
        cosine_h, sine_h, seq_row_h,
        rows_in, w_qkv, w_out, w_mlp, normed, qkv, mixed, resid, own_resid, acts,
        log_total, row_stats, bias, cosine, sine, seq_row, load_sems, tensor_sems, dp_sems, out_sems, act_sems,
    ) = refs
    slots, width, share, peers, attn = sz.slots, sz.width, sz.share, sz.peers, sz.attn
    dp, me = lax.axis_index("dp"), lax.axis_index("tensor")
    chunks = slots // UNIT
    core, z_odd = lax.rem(dp, 2), lax.rem(dp // 2, 2)
    sibling, twin = dp + 1 - 2 * core, dp + 2 - 4 * z_odd
    quarter = attn // 4

    def part_rows(odd, of_core):
        return span((2 * odd + of_core) * quarter, quarter)

    exchange = exchange_of(sz)(
        sz,
        tensor_sems,
        (
            lambda c: (c * UNIT, UNIT, tokens_h.at[rows_of(c), :], rows_in),
            lambda c: (c * UNIT, UNIT, mixed.at[me, rows_of(c), :], mixed),
            lambda c: (
                (2 * z_odd + core) * quarter, quarter, w_out_h.at[part_rows(z_odd, core), :], w_out
            ),
        ),
    )

    def w_out_copy(step, away):
        odd = 1 - z_odd if step == 2 else z_odd
        block = w_out.at[exchange.others[away], part_rows(odd, core), :]
        return pltpu.make_async_remote_copy(
            src_ref=block, dst_ref=block, send_sem=dp_sems.at[step, 0, away],
            recv_sem=dp_sems.at[step, 1, away],
            device_id=(twin if step == 0 else sibling, me), device_id_type=MESH,
        )

    def rows_of(c):
        return pl.ds(c * UNIT, UNIT)

    def load(src, dst, index):
        return pltpu.make_async_copy(src, dst, load_sems.at[index])

    def out_copy(src, dst, index, c):
        return pltpu.make_async_copy(src, dst, out_sems.at[index, c])

    barrier = pltpu.get_barrier_semaphore()
    own_load = load(tokens_h, rows_in.at[me], 0)
    own_load.start()
    for other in exchange.others[1:]:
        pl.semaphore_signal(barrier, inc=1, device_id=(dp, other), device_id_type=MESH)
    weight_loads = [
        load(ref, w_qkv.at[i], 1 + i) for i, ref in enumerate((w_query_h, w_key_h, w_value_h))
    ] + [load(w_out_h, w_out.at[me], 4), load(w_gate_h, w_mlp.at[0], 5), load(w_up_h, w_mlp.at[1], 6)]
    for one in weight_loads:
        one.start()
    for other in (sibling, twin):
        pl.semaphore_signal(barrier, inc=1, device_id=(other, me), device_id_type=MESH)
    pl.semaphore_wait(barrier, peers + 1)
    exchange.start(2, 0)
    for c in range(min(2, chunks)):
        exchange.start(0, c)

    outs = {}

    def write(src, dst, index, c):
        outs[index, c] = out_copy(src, dst, index, c)
        outs[index, c].start()

    def project(c):
        rows = rows_of(c)
        exchange.finish(0, c)
        if c == 0:
            own_load.wait()
            for one in weight_loads[:3]:
                one.wait()
        squares = jnp.zeros((UNIT, 1), jnp.float32)
        for b in range(peers):
            squares += jnp.sum(
                jnp.square(rows_in[b, rows, :].astype(jnp.float32)), axis=1, keepdims=True
            )
        rms = lax.rsqrt(squares / width + EPSILON)
        row_stats[rows, 1:2] = rms
        for b in range(peers):
            at = pl.ds(b * share, share)
            normed[rows, at] = (
                rows_in[b, rows, :].astype(jnp.float32) * rms * gain_attn[0:1, at]
            ).astype(jnp.bfloat16)
        write(normed.at[rows, :], normed_h.at[rows, :], 0, c)
        for i in range(3):
            found = matmul(normed[rows, :], w_qkv[i])
            if i < 2:
                for p in range(sz.pairs):
                    lanes = found[:, p * PAIR : (p + 1) * PAIR]
                    qkv[i, rows, pl.ds(p * PAIR, PAIR)] = (
                        lanes * cosine[rows, :] + swap_halves(lanes) * sine[rows, :]
                    ).astype(jnp.bfloat16)
            else:
                qkv[i, rows, :] = found.astype(jnp.bfloat16)
            write(qkv.at[i, rows, :], qkv_h.at[i, rows, :], 1 + i, c)

    def attend(c):
        rows = rows_of(c)
        keys = (c + 1) * UNIT
        key_slot = lax.broadcasted_iota(jnp.int32, (keys, UNIT), 0)
        query_slot = lax.broadcasted_iota(jnp.int32, (keys, UNIT), 1) + c * UNIT
        allowed = (row_stats[pl.ds(0, keys), 2:3] == seq_row[0:1, rows]) & (key_slot <= query_slot)
        bias[pl.ds(0, keys), :] = jnp.where(allowed, 0.0, MASKED)

        @pl.loop(0, sz.pairs)
        def _(p):
            mine = span(p * PAIR, PAIR)
            query = qkv[0, rows, mine] * jnp.bfloat16(SCALE)
            key = qkv[1, pl.ds(0, keys), mine]
            value = qkv[2, pl.ds(0, keys), mine]
            first_head = lax.broadcasted_iota(jnp.int32, (1, PAIR), 1) < HDIM
            found = []
            for h in range(2):
                chosen = first_head if h == 0 else jnp.logical_not(first_head)
                scores = matmul_last(key, jnp.where(chosen, query, 0.0))
                scores += bias[pl.ds(0, keys), :]
                peak = jnp.max(scores, axis=0, keepdims=True)
                expon = jnp.exp(scores - peak)
                total = jnp.sum(expon, axis=0, keepdims=True)
                log_total[pl.ds(2 * p + h, 1), rows] = peak + jnp.log(total)
                weights = (expon * (1.0 / total)).astype(jnp.bfloat16)
                found.append(matmul_first(weights, value))
            mixed[me, rows, mine] = jnp.where(first_head, *found).astype(jnp.bfloat16)

        write(mixed.at[me, rows, :], mixed_h.at[rows, :], 4, c)
        exchange.start(1, c)

    def act_copies(slot, c, u):
        at = pl.ds(u * sz.act_unit, sz.act_unit)
        return [
            pltpu.make_async_copy(
                acts.at[slot, i], ref.at[rows_of(c), at], act_sems.at[slot, i]
            )
            for i, ref in enumerate((hidden_h, silu_h, slope_h))
        ]

    act_units = sz.hidden // sz.act_unit
    pending = {}

    def feed(c):
        rows = rows_of(c)
        exchange.finish(1, c)
        if c == 0:
            for one in weight_loads[3:]:
                one.wait()
        squares = jnp.zeros((UNIT, 1), jnp.float32)
        for n in range(peers):
            at = pl.ds(n * share, share)
            total = rows_in[n, rows, :].astype(jnp.float32)
            for b in range(peers):
                total += matmul(mixed[b, rows, :], w_out[b, :, at])
            resid[:, at] = total
            squares += jnp.sum(jnp.square(total), axis=1, keepdims=True)
        rms = lax.rsqrt(squares / width + EPSILON)
        row_stats[rows, 0:1] = rms
        outs.pop((0, c)).wait()
        if c > 0:
            outs.pop((5, c - 1)).wait()
        own_resid[...] = resid[:, span(me * share, share)]
        write(own_resid, resid_h.at[rows, :], 5, c)
        for b in range(peers):
            at = pl.ds(b * share, share)
            normed[rows, at] = (resid[:, at] * rms * gain_mlp[0:1, at]).astype(jnp.bfloat16)
        write(normed.at[rows, :], normed_mlp_h.at[rows, :], 6, c)
        for u in range(act_units):
            slot = (c * act_units + u) % 2
            for one in pending.pop(slot, []):
                one.wait()
            at = pl.ds(u * sz.act_unit, sz.act_unit)
            gate = matmul(normed[rows, :], w_mlp[0, :, at])
            upward = matmul(normed[rows, :], w_mlp[1, :, at])
            sigmoid = 0.5 + 0.5 * jnp.tanh(0.5 * gate)
            silu = gate * sigmoid
            acts[slot, 0] = (silu * upward).astype(jnp.bfloat16)
            acts[slot, 1] = silu.astype(jnp.bfloat16)
            acts[slot, 2] = (upward * sigmoid * (1.0 + gate * (1.0 - sigmoid))).astype(jnp.bfloat16)
            pending[slot] = act_copies(slot, c, u)
            for one in pending[slot]:
                one.start()

    log_total[...] = jnp.zeros_like(log_total)

    def places(slot):
        number = start = jnp.zeros_like(slot)
        end = 0
        for j in range(lengths.shape[1]):
            end += lengths[0, j]
            passed = slot >= end
            number += passed.astype(jnp.int32)
            start += jnp.where(passed, lengths[0, j], 0)
        live = slot < end
        return jnp.where(live, number, slots + slot), jnp.where(live, slot - start, 0)

    seq_row[...] = places(lax.broadcasted_iota(jnp.int32, seq_row.shape, 1))[0].astype(jnp.float32)

    @pl.loop(0, slots // PAIR)
    def _(i):
        rows = span(i * PAIR, PAIR)
        slot = lax.broadcasted_iota(jnp.int32, (PAIR, PAIR), 0) + i * PAIR
        lane = lax.broadcasted_iota(jnp.int32, (PAIR, PAIR), 1)
        sequence, position = places(slot)
        row_stats[rows, :] = sequence.astype(jnp.float32)
        freq_index = lax.rem(lane, HDIM // 2).astype(jnp.float32)
        inverse = jnp.exp(freq_index * (-2.0 * math.log(ROPE_BASE) / HDIM))
        angles = position.astype(jnp.float32) * inverse
        cosine[rows, :] = jnp.cos(angles)
        sines = jnp.sin(angles)
        sine[rows, :] = jnp.where(lax.rem(lane, HDIM) < HDIM // 2, -sines, sines)

    for i, (src, dst) in enumerate(((cosine, cosine_h), (sine, sine_h))):
        write(src, dst, 7, 2 + i)
    write(seq_row, seq_row_h, 8, 0)
    def pass_on(kind, c):
        exchange.forward(kind, c)
        if kind == 0 and c + 2 < chunks:
            exchange.start(kind, c + 2)

    w_peers = range(1, peers)
    def share_w_out(peers_done):
        for step in (0, 1):
            for away in peers_done:
                w_out_copy(step, away).start()

    exchange.forward(2, 0)
    share_w_out(exchange.NEAR)
    for c in range(min(2, chunks)):
        pass_on(0, c)
    exchange.finish(2, 0)
    share_w_out([away for away in w_peers if away not in exchange.NEAR])
    for c in range(chunks):
        project(c)
        attend(c)
        if c + 2 < chunks:
            pass_on(0, c + 2)
        if c == chunks - 2:
            pass_on(1, 0)
    for away in w_peers:
        w_out_copy(0, away).wait()
        w_out_copy(2, away).start()
    for away in w_peers:
        w_out_copy(1, away).wait()
        w_out_copy(2, away).wait()
    for c in range(chunks):
        if c + 1 < chunks:
            pass_on(1, c + 1)
        feed(c)
    write(log_total, log_h, 7, 0)
    write(row_stats, stats_h, 7, 1)
    for slot in list(pending):
        for one in pending.pop(slot):
            one.wait()
    for one in outs.values():
        one.wait()


def forward(sz, big, small):
    slots, width, share, attn, hidden = sz.slots, sz.width, sz.share, sz.attn, sz.hidden
    chunks = slots // UNIT
    bf16, f32 = jnp.bfloat16, jnp.float32
    shapes = [
        ((slots, width), bf16), ((3, slots, attn), bf16), ((slots, attn), bf16), ((8, slots), f32),
        ((slots, share), f32), ((slots, width), bf16), ((slots, hidden), bf16),
        ((slots, hidden), bf16), ((slots, hidden), bf16), ((slots, PAIR), f32),
        ((slots, PAIR), f32), ((slots, PAIR), f32), ((8, slots), f32),
    ]
    flops = 2 * slots * (4 * width * attn + 2 * width * hidden)
    return pl.pallas_call(
        functools.partial(forward_kernel, sz),
        out_shape=[jax.ShapeDtypeStruct(*s) for s in shapes],
        in_specs=[pl.BlockSpec(memory_space=pl.ANY)] * len(big)
        + [pl.BlockSpec(memory_space=pltpu.SMEM)]
        + [pl.BlockSpec(memory_space=pltpu.VMEM)] * (len(small) - 1),
        out_specs=[pl.BlockSpec(memory_space=pl.ANY)] * len(shapes),
        scratch_shapes=[
            pltpu.VMEM((sz.peers, slots, share), bf16),
            pltpu.VMEM((3, width, attn), bf16),
            pltpu.VMEM((sz.peers, attn, width), bf16),
            pltpu.VMEM((2, width, hidden), bf16),
            pltpu.VMEM((slots, width), bf16),
            pltpu.VMEM((3, slots, attn), bf16),
            pltpu.VMEM((sz.peers, slots, attn), bf16),
            pltpu.VMEM((UNIT, width), f32),
            pltpu.VMEM((UNIT, share), f32),
            pltpu.VMEM((2, 3, UNIT, sz.act_unit), bf16),
            pltpu.VMEM((8, slots), f32),
            pltpu.VMEM((slots, PAIR), f32),
            pltpu.VMEM((slots, UNIT), f32),
            pltpu.VMEM((slots, PAIR), f32),
            pltpu.VMEM((slots, PAIR), f32),
            pltpu.VMEM((8, slots), f32),
            pltpu.SemaphoreType.DMA((7,)),
            pltpu.SemaphoreType.DMA((6 * exchange_of(sz).HOPS, chunks, sz.peers)),
            pltpu.SemaphoreType.DMA((3, 2, sz.peers)),
            pltpu.SemaphoreType.DMA((9, chunks)),
            pltpu.SemaphoreType.DMA((2, 3)),
        ],
        compiler_params=pltpu.CompilerParams(
            collective_id=1, has_side_effects=True, vmem_limit_bytes=63 * MIB
        ),
        cost_estimate=pl.CostEstimate(
            flops=flops, bytes_accessed=60 * MIB, transcendentals=slots * slots * 8
        ),
    )(*big, *small)


def backward_kernel(sz, *refs):
    (
        hidden_h, silu_h, slope_h, cot_h, normed_mlp_h, mixed_h, normed_h, qkv_h,
        w_down_h, w_gate_h, w_up_h, w_out_h, w_query_h, w_key_h, w_value_h,
        resid_h, cosine, sine, seq_row, log_total, row_stats, gain_attn, gain_mlp,
        *refs,
    ) = refs
    outs, (grad_tokens_h, out_tokens_h, gains_h), refs = refs[:7], refs[7:10], refs[10:]
    (
        buf_a, buf_b, buf_c, d_gate, d_up, send, full, recv, d_mixed, d_qkv, w_buf, w_cols,
        acc_key, acc_value, row_part, row_send, row_recv, gains, gains_out,
        load_sems, w_sems, tensor_sems, gain_sems, *line_scratch,
    ) = refs
    slots, width, share, peers = sz.slots, sz.width, sz.share, sz.peers
    n_dp = lax.axis_size("dp")
    dp, me = lax.axis_index("dp"), lax.axis_index("tensor")
    tile_rows, tile_cols = sz.tile
    assert tile_cols == share

    def place_of(m):
        across, down = sz.plan[m][2], sz.shapes[m][0] // tile_rows
        if m == 0:
            return lambda i: (lax.rem(i, down), partner(me, i // down, peers))
        return lambda i: (i // across, lax.rem(i, across))

    places = [place_of(m) for m in range(len(sz.plan))]
    line = LineSum(
        sz.total, [(ref, plan[0], plan[1], at) for ref, plan, at in zip(outs, sz.plan, places)],
        sz.tile, line_scratch,
    )

    def load(src, dst, index):
        return pltpu.make_async_copy(src, dst, load_sems.at[index])

    def peer(away):
        return partner(me, away, peers)

    def other_dp(away):
        return lax.rem(dp + away, n_dp)

    barrier = pltpu.get_barrier_semaphore()
    own = span(me * share, share)
    first_loads = [
        load(hidden_h, buf_a.at[:, pl.ds(0, sz.hidden)], 0), load(cot_h, buf_b.at[:, own], 1),
        load(normed_mlp_h, buf_c, 2),
    ]
    for one in first_loads:
        one.start()

    def remote(kind, away, src, dst):
        return pltpu.make_async_remote_copy(
            src_ref=src, dst_ref=dst, send_sem=tensor_sems.at[2 * kind, away],
            recv_sem=tensor_sems.at[2 * kind + 1, away],
            device_id=(dp, peer(away)), device_id_type=MESH,
        )

    def send_cot(away):
        return remote(4, away, cot_h, buf_b.at[:, own])
    for away in range(1, n_dp):
        pl.semaphore_signal(
            barrier, inc=1, device_id=(other_dp(away), me), device_id_type=MESH
        )
    for away in range(1, peers):
        pl.semaphore_signal(barrier, inc=1, device_id=(dp, peer(away)), device_id_type=MESH)
    pl.semaphore_wait(barrier, n_dp - 1 + peers - 1)
    for away in range(1, peers):
        send_cot(away).start()

    attn_at = [pl.ds(i * sz.attn, sz.attn) for i in range(4)]
    grads = [
        (lambda r: buf_a[:, r], lambda c: buf_b[:, c]),
        (lambda r: buf_c[:, r], lambda c: d_gate[:, c]),
        (lambda r: buf_c[:, r], lambda c: d_up[:, c]),
        (lambda r: d_gate[:, pl.ds(pl.multiple_of(3 * sz.attn + r.start, tile_rows), tile_rows)],
         lambda c: buf_a[:, c]),
        (lambda r: buf_b[:, r], lambda c: d_qkv[2, :, c]),
        (lambda r: buf_b[:, r], lambda c: d_qkv[0, :, c]),
        (lambda r: buf_b[:, r], lambda c: d_qkv[1, :, c]),
    ]

    def cot_at(away):
        last = sz.plan[1][0] - sz.pace * (sz.hidden // UNIT // 2) - 1
        return min(away * (sz.shapes[0][0] // tile_rows), last)

    def tile_tick(m, k, work=None):
        row, col = places[m](k - sz.plan[m][0])
        rows, cols = span(row * tile_rows, tile_rows), span(col * tile_cols, tile_cols)
        if m == 0:
            for away in range(1, peers):
                @pl.when(k == cot_at(away))
                def _(away=away):
                    send_cot(away).wait()
        left, right = grads[m]
        line.put(k, matmul_first(left(rows), right(cols)))
        line.early(k)
        if work is not None:
            work()
        line.late(k)

    cursor = [0]

    def matrix_of(k):
        return [m for m, (first, count, _) in enumerate(sz.plan) if first <= k < first + count][0]

    def advance_to(stop):
        while cursor[0] < stop:
            m = matrix_of(cursor[0])
            until = min(stop, sz.plan[m][0] + sz.plan[m][1])

            @pl.loop(cursor[0], until)
            def _(k, m=m):
                tile_tick(m, k)

            cursor[0] = until

    def run_units(count, unit, group=1):
        ticks = group * sz.pace
        done = 0
        while done < count:
            m = matrix_of(cursor[0])
            room = (sz.plan[m][0] + sz.plan[m][1] - cursor[0]) // ticks
            if not room:
                for g in range(group):
                    for t in range(sz.pace):
                        work = functools.partial(unit, done, g) if t == 0 else None
                        tile_tick(matrix_of(cursor[0]), cursor[0], work)
                        cursor[0] += 1
                done += 1
                continue
            step = min(room, count - done)

            @pl.loop(0, step)
            def _(i, m=m, done=done, start=cursor[0]):
                for g in range(group):
                    for t in range(sz.pace):
                        work = functools.partial(unit, done + i, g) if t == 0 else None
                        tile_tick(m, start + i * ticks + g * sz.pace + t, work)

            cursor[0] += step * ticks
            done += step

    order = list(range(peers - 1, 0, -1)) + [0]

    def block_of(u):
        return partner(me, peers - 1 - u // sz.block_units, peers)

    def feature(u):
        return block_of(u) * share + lax.rem(u, sz.block_units) * UNIT

    def scatter(round_, away):
        dst = full.at[me] if round_ == 2 else recv.at[away - 1]
        return remote(round_, away, send.at[peer(away)], dst)

    def store_part(round_, u, value):
        send[block_of(u), :, span(lax.rem(u, sz.block_units) * UNIT, UNIT)] = value.astype(
            jnp.bfloat16
        )
        for i, away in enumerate(order[:-1] if round_ != 1 else ()):
            @pl.when(u == (i + 1) * sz.block_units - 1)
            def _(away=away):
                scatter(round_, away).start()

    mlp_units = width // UNIT
    hid = pl.ds(0, sz.hidden)

    def prefetched(count, loads, u):
        for one in loads(u):
            one.wait()

        @pl.when(u + 1 < count)
        def _():
            for one in loads(u + 1):
                one.start()

    def hidden_loads(u):
        cols = span(u * UNIT, UNIT)
        slot = lax.rem(u, 2)
        return (
            pltpu.make_async_copy(w_down_h.at[cols, :], w_buf.at[slot, 0], w_sems.at[0, slot]),
            pltpu.make_async_copy(
                silu_h.at[:, cols], d_qkv.at[slot, :, pl.ds(0, UNIT)], w_sems.at[1, slot]
            ),
            pltpu.make_async_copy(
                slope_h.at[:, cols], d_qkv.at[slot, :, pl.ds(UNIT, UNIT)], w_sems.at[2, slot]
            ),
        )

    def hidden_unit(u, _):
        prefetched(sz.hidden // UNIT, hidden_loads, u)
        slot = lax.rem(u, 2)
        cols = span(u * UNIT, UNIT)
        d_hidden = matmul_last(buf_b[...], w_buf[slot, 0])
        d_up[:, cols] = (d_hidden * d_qkv[slot, :, pl.ds(0, UNIT)]).astype(jnp.bfloat16)
        d_gate[:, cols] = (d_hidden * d_qkv[slot, :, pl.ds(UNIT, UNIT)]).astype(jnp.bfloat16)

    def twice(unit):
        def both(u, g):
            unit(2 * u, g)
            unit(2 * u + 1, g)

        return both

    for one in hidden_loads(0):
        one.start()
    for one in first_loads[:2]:
        one.wait()
    advance_to(sz.plan[1][0] - sz.pace * (sz.hidden // UNIT // 2))
    run_units(sz.hidden // UNIT // 2, twice(hidden_unit))
    first_loads[2].wait()

    def gather(round_):
        for away in range(1, peers):
            scatter(round_, away).wait()

    def gathered(round_, rows):
        total = send[me, rows, :].astype(jnp.float32)
        for away in range(1, peers):
            block = full[peer(away), rows, :] if round_ == 2 else recv[away - 1, rows, :]
            total += block.astype(jnp.float32)
        return total

    def mlp_loads(u):
        slot = lax.rem(u, 2)
        rows = span(feature(u), UNIT)
        return (
            pltpu.make_async_copy(
                w_gate_h.at[rows, :], w_buf.at[slot, 0, :, hid], w_sems.at[0, slot]
            ),
            pltpu.make_async_copy(
                w_up_h.at[rows, :], w_buf.at[slot, 1, :, hid], w_sems.at[1, slot]
            ),
        )

    def mlp_unit(u, _):
        prefetched(mlp_units, mlp_loads, u)
        slot = lax.rem(u, 2)
        part = matmul_last(d_gate[...], w_buf[slot, 0, :, hid])
        part += matmul_last(d_up[...], w_buf[slot, 1, :, hid])
        store_part(0, u, part)

    for one in mlp_loads(0):
        one.start()
    run_units(mlp_units, mlp_unit)
    advance_to(cursor[0] + 4 * sz.pace)

    def spread(away):
        return remote(3, away, full.at[me], full.at[me])

    w_out_rows = sz.attn // UNIT
    w_out_loads = [
        load(w_out_h.at[pl.ds(i * UNIT, UNIT), :], w_buf.at[0, i], 3 + i) for i in range(w_out_rows)
    ]
    for one in w_out_loads:
        one.start()
    gather(0)

    @pl.loop(0, slots // UNIT)
    def _(i):
        full[me, span(i * UNIT, UNIT), :] = gathered(0, span(i * UNIT, UNIT)).astype(jnp.bfloat16)

    for away in range(1, peers):
        spread(away).start()
    advance_to(sz.plan[2][0])

    hidden_load = load(hidden_h, d_gate, 0)
    hidden_load.start()

    def out_loads(u):
        slot = lax.rem(u, 2)
        return [
            pltpu.make_async_copy(
                w_down_h.at[:, span(feature(u), UNIT)], w_cols.at[slot], w_sems.at[0, slot]
            )
        ]

    def out_unit(u, _):
        prefetched(mlp_units, out_loads, u)
        store_part(1, u, matmul(d_gate[...], w_cols[lax.rem(u, 2)]))

    for one in out_loads(0):
        one.start()
    hidden_load.wait()
    run_units(mlp_units // 2, twice(out_unit))

    for away in range(1, peers):
        spread(away).wait()
    for one in w_out_loads:
        one.wait()

    gains[dp] = jnp.zeros_like(gains[dp])

    def norm_unit(u, _):
        rows = span(u * UNIT, UNIT)
        row_sum = jnp.zeros((UNIT, 1), jnp.float32)
        for b in range(peers):
            at = pl.ds(b * share, share)
            row_sum += jnp.sum(
                full[b, rows, :].astype(jnp.float32) * buf_c[rows, at].astype(jnp.float32),
                axis=1, keepdims=True,
            )
        rms = row_stats[rows, 0:1]
        for b in range(peers):
            at = pl.ds(b * share, share)
            gain = gain_mlp[0:1, at]
            lean = buf_c[rows, at].astype(jnp.float32) / gain * (row_sum / width)
            d_resid = buf_b[rows, at].astype(jnp.float32) + rms * (
                gain * full[b, rows, :].astype(jnp.float32) - lean
            )
            buf_a[rows, at] = d_resid.astype(jnp.bfloat16)
        gains[dp, 0:1, :] += jnp.sum(
            full[me, rows, :].astype(jnp.float32) * buf_c[rows, own].astype(jnp.float32),
            axis=0, keepdims=True,
        ) / gain_mlp[0:1, own]
        for i in range(w_out_rows):
            d_mixed[rows, pl.ds(i * UNIT, UNIT)] = matmul_last(
                buf_a[rows, :], w_buf[0, i]
            ).astype(jnp.bfloat16)

    run_units(slots // UNIT, norm_unit)
    for away in range(1, peers):
        scatter(1, away).start()

    attn_loads = [
        load(ref, d_gate.at[:, attn_at[i]], 5 + i)
        for i, ref in enumerate((qkv_h.at[0], qkv_h.at[1], qkv_h.at[2], mixed_h))
    ] + [load(normed_h, buf_b, 9)]
    for one in attn_loads:
        one.start()
    for one in attn_loads:
        one.wait()
    blocks = slots // UNIT

    def attend_unit(p, i):
        rows = pl.ds(i * UNIT, UNIT)
        keys = (i + 1) * UNIT
        lanes = [pl.ds(pl.multiple_of(j * sz.attn + p * PAIR, PAIR), PAIR) for j in range(3)]
        mine = span(p * PAIR, PAIR)
        query = d_gate[rows, lanes[0]]
        key = d_gate[pl.ds(0, keys), lanes[1]]
        value = d_gate[pl.ds(0, keys), lanes[2]]
        grad = d_mixed[rows, mine]
        first_head = lax.broadcasted_iota(jnp.int32, (1, PAIR), 1) < HDIM
        key_slot = lax.broadcasted_iota(jnp.int32, (keys, UNIT), 0)
        query_slot = lax.broadcasted_iota(jnp.int32, (keys, UNIT), 1) + i * UNIT
        allowed = (row_stats[pl.ds(0, keys), 2:3] == seq_row[0:1, rows]) & (key_slot <= query_slot)
        found = []
        for h in range(2):
            chosen = first_head if h == 0 else jnp.logical_not(first_head)
            scores = matmul_last(key, jnp.where(chosen, query, 0.0)) * SCALE
            scores -= log_total[pl.ds(2 * p + h, 1), rows]
            probs = jnp.exp(jnp.where(allowed, scores, MASKED))
            grad_probs = matmul_last(value, jnp.where(chosen, grad, 0.0))
            delta = jnp.sum(probs * grad_probs, axis=0, keepdims=True)
            grad_scores = (probs * (grad_probs - delta)).astype(jnp.bfloat16)
            found.append(
                (
                    matmul_first(grad_scores, key),
                    matmul(grad_scores, query),
                    matmul(probs.astype(jnp.bfloat16), grad),
                )
            )
        grad_query, grad_key, grad_value = [
            jnp.where(first_head, one, two) for one, two in zip(*found)
        ]
        d_qkv[0, rows, mine] = rotate_back(
            grad_query * SCALE, cosine[rows, :], sine[rows, :]
        ).astype(jnp.bfloat16)
        for acc, part in ((acc_key, grad_key), (acc_value, grad_value)):
            if i > 0:
                acc[pl.ds(0, keys - UNIT), :] += part[: keys - UNIT]
            acc[pl.ds(keys - UNIT, UNIT), :] = part[keys - UNIT :]
        if i + 1 == blocks:
            d_qkv[1, :, mine] = rotate_back(acc_key[...] * SCALE, cosine[...], sine[...]).astype(
                jnp.bfloat16
            )
            d_qkv[2, :, mine] = acc_value[...].astype(jnp.bfloat16)

    steps = [(0, 1), (2,), (3,)] if blocks == 4 else [(i,) for i in range(blocks)]

    def attend_step(p, g):
        for i in steps[g]:
            attend_unit(p, i)

    run_units(sz.pairs, attend_step, len(steps))
    advance_to(sz.plan[4][0])

    gather(1)
    for j in range(share // PAIR):
        lanes = pl.ds(j * PAIR, PAIR)
        piece = load(resid_h.at[:, lanes], acc_key, 2)
        piece.start()
        piece.wait()

        @pl.loop(0, slots // UNIT)
        def _(i, lanes=lanes):
            rows = span(i * UNIT, UNIT)
            total = acc_key[rows, :] + send[me, rows, lanes].astype(jnp.float32)
            for away in range(1, peers):
                total += recv[away - 1, rows, lanes].astype(jnp.float32)
            send[me, rows, lanes] = total.astype(jnp.bfloat16)

    tokens_out = load(send.at[me], out_tokens_h, 0)
    tokens_out.start()

    row_part[...] = jnp.zeros_like(row_part)

    def attn_loads_of(u):
        slot = lax.rem(u, 2)
        rows = span(feature(u), UNIT)
        return [
            pltpu.make_async_copy(ref.at[rows, :], w_buf.at[slot, 0, :, at], w_sems.at[i, slot])
            for i, (ref, at) in enumerate(zip((w_query_h, w_key_h, w_value_h), attn_at))
        ]

    def attn_unit(u, _):
        prefetched(mlp_units, attn_loads_of, u)
        slot = lax.rem(u, 2)
        part = jnp.zeros((slots, UNIT), jnp.float32)
        for i in range(3):
            part += matmul_last(d_qkv[i, :, pl.ds(0, sz.attn)], w_buf[slot, 0, :, attn_at[i]])
        store_part(2, u, part)
        row_part[...] += jnp.sum(
            part * buf_b[:, span(feature(u), UNIT)].astype(jnp.float32), axis=1, keepdims=True
        )

    def row_scatter(away):
        return remote(5, away, row_send, row_recv.at[away - 1])

    for one in attn_loads_of(0):
        one.start()

    tokens_out.wait()
    run_units(mlp_units // 2, twice(attn_unit))
    row_send[...] = row_part[...].T[0:8, :]
    for away in range(1, peers):
        row_scatter(away).start()
    advance_to(sz.total - 2 * sz.pace)
    gather(2)
    for away in range(1, peers):
        row_scatter(away).wait()
    row_sums = row_send[...]
    for away in range(1, peers):
        row_sums += row_recv[away - 1]
    row_part[...] = jnp.concatenate([row_sums] * (row_part.shape[1] // 8), axis=0).T

    def last_unit(u, _):
        rows = span(u * UNIT, UNIT)
        d_own = gathered(2, rows)
        straight = buf_b[rows, own].astype(jnp.float32)
        gain = gain_attn[0:1, own]
        gains[dp, 1:2, :] += jnp.sum(d_own * straight, axis=0, keepdims=True) / gain
        lean = straight / gain * (row_part[rows, 0:1] / width)
        send[me, rows, :] = (
            buf_a[rows, own].astype(jnp.float32) + row_stats[rows, 1:2] * (gain * d_own - lean)
        ).astype(jnp.bfloat16)

    run_units(slots // UNIT // 2, twice(last_unit))
    grad_out = load(send.at[me], grad_tokens_h, 10)
    grad_out.start()

    def gain_copy(away):
        return pltpu.make_async_remote_copy(
            src_ref=gains.at[dp], dst_ref=gains.at[dp],
            send_sem=gain_sems.at[0, away], recv_sem=gain_sems.at[1, away],
            device_id=(other_dp(away), me), device_id_type=MESH,
        )

    for away in range(1, n_dp):
        gain_copy(away).start()

    @pl.loop(sz.total, sz.total + line.length)
    def _(k):
        line.early(k)
        line.late(k)

    for away in range(1, n_dp):
        gain_copy(away).wait()
    total = gains[0]
    for i in range(1, n_dp):
        total += gains[i]
    gains_out[...] = total
    gain_out = load(gains_out, gains_h, 11)
    gain_out.start()

    grad_out.wait()
    gain_out.wait()


def backward(sz, big, small):
    whole_rows = pltpu.VMEM((sz.slots, sz.width), jnp.bfloat16)
    hidden_rows = pltpu.VMEM((sz.slots, sz.hidden), jnp.bfloat16)
    assert sz.hidden == 4 * sz.attn and sz.share % UNIT == 0 and sz.hidden <= sz.width
    n_dp = lax.axis_size("dp")
    attn_rows = max(sz.attn, 2 * UNIT)
    flops = 6 * sz.slots * (3 * sz.width * sz.hidden + 4 * sz.width * sz.attn)
    return pl.pallas_call(
        functools.partial(backward_kernel, sz),
        out_shape=[jax.ShapeDtypeStruct(s, jnp.bfloat16) for s in sz.shapes]
        + [
            jax.ShapeDtypeStruct((sz.slots, sz.share), jnp.bfloat16),
            jax.ShapeDtypeStruct((sz.slots, sz.share), jnp.bfloat16),
            jax.ShapeDtypeStruct((8, sz.share), jnp.float32),
        ],
        in_specs=[pl.BlockSpec(memory_space=pl.ANY)] * len(big)
        + [pl.BlockSpec(memory_space=pltpu.VMEM)] * len(small),
        out_specs=[pl.BlockSpec(memory_space=pl.ANY)] * 10,
        scratch_shapes=[
            whole_rows, whole_rows, whole_rows, hidden_rows, hidden_rows,
            pltpu.VMEM((sz.peers, sz.slots, sz.share), jnp.bfloat16),
            pltpu.VMEM((sz.peers, sz.slots, sz.share), jnp.bfloat16),
            pltpu.VMEM((sz.peers - 1, sz.slots, sz.share), jnp.bfloat16),
            pltpu.VMEM((sz.slots, sz.attn), jnp.bfloat16),
            pltpu.VMEM((3, sz.slots, attn_rows), jnp.bfloat16),
            pltpu.VMEM((2, 2, UNIT, sz.width), jnp.bfloat16),
            pltpu.VMEM((2, sz.hidden, UNIT), jnp.bfloat16),
            pltpu.VMEM((sz.slots, PAIR), jnp.float32),
            pltpu.VMEM((sz.slots, PAIR), jnp.float32),
            pltpu.VMEM((sz.slots, PAIR), jnp.float32),
            pltpu.VMEM((8, sz.slots), jnp.float32),
            pltpu.VMEM((sz.peers - 1, 8, sz.slots), jnp.float32),
            pltpu.VMEM((n_dp, 8, sz.share), jnp.float32),
            pltpu.VMEM((8, sz.share), jnp.float32),
            pltpu.SemaphoreType.DMA((12,)),
            pltpu.SemaphoreType.DMA((3, 2)),
            pltpu.SemaphoreType.DMA((12, sz.peers)),
            pltpu.SemaphoreType.DMA((2, n_dp)),
        ]
        + LineSum.scratch_shapes(sz.tile),
        compiler_params=pltpu.CompilerParams(
            collective_id=0, has_side_effects=True, vmem_limit_bytes=63 * MIB
        ),
        cost_estimate=pl.CostEstimate(
            flops=flops, bytes_accessed=200 * MIB, transcendentals=sz.slots * sz.slots * 8
        ),
    )(*big, *small)


def widen_kernel(steps, depth, *refs):
    count = 1 + max(i for i, _, _ in steps)
    sources, moved, gains, refs = refs[:count], refs[count : count + 2], refs[count + 2], refs[count + 3 :]
    results, moved_to, gains_to = refs[:count], refs[count : count + 2], refs[count + 2 : count + 4]
    narrow, wide, held, in_sems, out_sems, move_sems = refs[count + 4 :]
    moves_in = [
        pltpu.make_async_copy(src, held.at[i], move_sems.at[0, i]) for i, src in enumerate(moved)
    ]
    moves_out = [
        pltpu.make_async_copy(held.at[i], dst, move_sems.at[1, i])
        for i, dst in enumerate(moved_to)
    ]
    for one in moves_in:
        one.start()
    gains_to[0][...] = gains[1, :]
    gains_to[1][...] = gains[0, :]

    def read(n):
        i, first, rows = steps[n]
        cols = sources[i].shape[1]
        slot = n % depth
        return pltpu.make_async_copy(
            sources[i].at[pl.ds(first, rows), :],
            narrow[cols].at[slot, pl.ds(0, rows), :], in_sems.at[slot],
        )

    def write(n):
        i, first, rows = steps[n]
        cols = sources[i].shape[1]
        slot = n % depth
        return pltpu.make_async_copy(
            wide[cols].at[slot, pl.ds(0, rows), :],
            results[i].at[pl.ds(first, rows), :], out_sems.at[slot],
        )

    for n in range(min(depth, len(steps))):
        read(n).start()
    for n, (i, _, rows) in enumerate(steps):
        cols = sources[i].shape[1]
        slot = n % depth
        read(n).wait()
        if n == len(steps) // 2:
            for one, then in zip(moves_in, moves_out):
                one.wait()
                then.start()
        if n >= depth:
            write(n - depth).wait()
        strip = min(rows, 32 * 2048 // cols)

        @pl.loop(0, rows // strip)
        def _(r, cols=cols, slot=slot, strip=strip):
            at = span(r * strip, strip)
            wide[cols][slot, at, :] = narrow[cols][slot, at, :].astype(jnp.float32)

        write(n).start()
        if n + depth < len(steps):
            read(n + depth).start()
    for n in range(max(0, len(steps) - depth), len(steps)):
        write(n).wait()
    for one in moves_out:
        one.wait()


def widen(arrays, moved, gains):
    depth = 4
    block = 1024 * 1024
    steps, most = [], {}
    for i, (rows, cols) in enumerate(a.shape for a in arrays):
        step = min(rows, block // cols)
        most[cols] = max(step, most.get(cols, 0))
        steps += [(i, first, step) for first in range(0, rows, step)]
    return pl.pallas_call(
        functools.partial(widen_kernel, steps, depth),
        out_shape=[jax.ShapeDtypeStruct(a.shape, jnp.float32) for a in arrays]
        + [jax.ShapeDtypeStruct(a.shape, a.dtype) for a in moved]
        + [jax.ShapeDtypeStruct(gains.shape[1:], gains.dtype)] * 2,
        in_specs=[pl.BlockSpec(memory_space=pl.ANY)] * (len(arrays) + 2)
        + [pl.BlockSpec(memory_space=pltpu.VMEM)],
        out_specs=[pl.BlockSpec(memory_space=pl.ANY)] * (len(arrays) + 2)
        + [pl.BlockSpec(memory_space=pltpu.VMEM)] * 2,
        scratch_shapes=[
            {cols: pltpu.VMEM((depth, rows, cols), jnp.bfloat16) for cols, rows in most.items()},
            {cols: pltpu.VMEM((depth, rows, cols), jnp.float32) for cols, rows in most.items()},
            pltpu.VMEM((2,) + moved[0].shape, moved[0].dtype),
            pltpu.SemaphoreType.DMA((depth,)),
            pltpu.SemaphoreType.DMA((depth,)),
            pltpu.SemaphoreType.DMA((2, 2)),
        ],
        compiler_params=pltpu.CompilerParams(vmem_limit_bytes=63 * MIB),
        cost_estimate=pl.CostEstimate(flops=0, bytes_accessed=96 * MIB, transcendentals=0),
    )(*arrays, *moved, gains)


def body(
    tokens,
    norm_gain_attn,
    norm_gain_mlp,
    w_query,
    w_key,
    w_value,
    w_out,
    w_gate,
    w_up,
    w_down,
    cotangent,
    lengths,
):
    slot_count = tokens.shape[0]
    share_width = tokens.shape[1]
    model_width = share_width * lax.axis_size("tensor")
    attn_width = w_query.shape[1]
    sz = Sizes(slot_count, model_width, share_width, w_gate.shape[1], attn_width)
    gain_attn = norm_gain_attn.reshape(1, model_width)
    gain_mlp = norm_gain_mlp.reshape(1, model_width)
    (
        normed, qkv, mixed, log_total, resid_here, normed_mlp, hidden, silu, slope, row_stats,
        cosine, sine, seq_row,
    ) = forward(
        sz, (tokens, w_query, w_key, w_value, w_out, w_gate, w_up), (lengths, gain_attn, gain_mlp)
    )
    down, gate, up, out, value, query, key, grad_tokens, out_tokens, gains = backward(
        sz,
        (
            hidden, silu, slope, cotangent, normed_mlp, mixed, normed, qkv,
            w_down, w_gate, w_up, w_out, w_query, w_key, w_value, resid_here,
        ),
        (cosine, sine, seq_row, log_total, row_stats, gain_attn, gain_mlp),
    )

    down, gate, up, out, value, query, key, grad_tokens, out_tokens, gain_attn, gain_mlp = widen(
        [down, gate, up, out, value, query, key], [grad_tokens, out_tokens], gains
    )
    return (
        out_tokens, grad_tokens, gain_attn, gain_mlp, query, key, value, out, gate, up, down,
    )


def solution(mesh):
    placed = (
        P("dp", "tensor"),
        P(),
        P(),
        P(None, "tensor"),
        P(None, "tensor"),
        P(None, "tensor"),
        P("tensor", None),
        P(None, "tensor"),
        P(None, "tensor"),
        P("tensor", None),
        P("dp", "tensor"),
        P("dp", None),
    )
    return jax.shard_map(
        body,
        mesh=mesh,
        in_specs=placed,
        out_specs=(
            P("dp", "tensor"),
            P("dp", "tensor"),
            P("tensor"),
            P("tensor"),
            P(None, "tensor"),
            P(None, "tensor"),
            P(None, "tensor"),
            P("tensor", None),
            P(None, "tensor"),
            P(None, "tensor"),
            P("tensor", None),
        ),
        check_vma=False,
    )
```
